32 devices in a mesh: img: 2 (over x), row: 4 (over y, core), col: 4 (over z).
Axes of the slice: x: 2, y: 2, z: 4, core: 2. Of those that a mesh axis runs over, the one named last changes fastest.
Arguments:
- images: float32 [16, 56, 56, 512], P('img', 'row', 'col'), may hold values from -6 to 6
- grad_out: float32 [16, 56, 56, 512], P('img', 'row', 'col'), may hold values from -6 to 6
- w_qkv: float32 [2, 512, 1536], P(None, 'img', ('row', 'col')), may hold values from -0.25 to 0.25
- w_proj: float32 [2, 512, 512], P(None, 'img', ('row', 'col')), may hold values from -1 to 1
- w_fc1: float32 [2, 512, 2048], P(None, 'img', ('row', 'col')), may hold values from -0.25 to 0.25
- w_fc2: float32 [2, 2048, 512], P(None, 'img', ('row', 'col')), may hold values from -0.125 to 0.125
- first_qkv: float32 [2, 512, 1536], P(None, 'img', ('row', 'col')), may hold values from -128 to 128
- first_proj: float32 [2, 512, 512], P(None, 'img', ('row', 'col')), may hold values from -128 to 128
- first_fc1: float32 [2, 512, 2048], P(None, 'img', ('row', 'col')), may hold values from -128 to 128
- first_fc2: float32 [2, 2048, 512], P(None, 'img', ('row', 'col')), may hold values from -128 to 128
- second_qkv: float32 [2, 512, 1536], P(None, 'img', ('row', 'col')), may hold values from 50 to 200
- second_proj: float32 [2, 512, 512], P(None, 'img', ('row', 'col')), may hold values from 50 to 200
- second_fc1: float32 [2, 512, 2048], P(None, 'img', ('row', 'col')), may hold values from 50 to 200
- second_fc2: float32 [2, 2048, 512], P(None, 'img', ('row', 'col')), may hold values from 50 to 200
- small_params: float32 [2, 9360], replicated, may hold values from -4 to 4
- small_first: float32 [2, 9360], replicated, may hold values from -128 to 128
- small_second: float32 [2, 9360], replicated, may hold values from 50 to 200
- rel_index: int32 [49, 49], replicated, may hold values from 0 to 168, as said below
Outputs:
- images_out: float32 [16, 56, 56, 512], P('img', 'row', 'col')
- grad_input: float32 [16, 56, 56, 512], P('img', 'row', 'col')
- new_w_qkv: float32 [2, 512, 1536], P(None, 'img', ('row', 'col'))
- new_w_proj: float32 [2, 512, 512], P(None, 'img', ('row', 'col'))
- new_w_fc1: float32 [2, 512, 2048], P(None, 'img', ('row', 'col'))
- new_w_fc2: float32 [2, 2048, 512], P(None, 'img', ('row', 'col'))
- new_first_qkv: float32 [2, 512, 1536], P(None, 'img', ('row', 'col'))
- new_first_proj: float32 [2, 512, 512], P(None, 'img', ('row', 'col'))
- new_first_fc1: float32 [2, 512, 2048], P(None, 'img', ('row', 'col'))
- new_first_fc2: float32 [2, 2048, 512], P(None, 'img', ('row', 'col'))
- new_second_qkv: float32 [2, 512, 1536], P(None, 'img', ('row', 'col'))
- new_second_proj: float32 [2, 512, 512], P(None, 'img', ('row', 'col'))
- new_second_fc1: float32 [2, 512, 2048], P(None, 'img', ('row', 'col'))
- new_second_fc2: float32 [2, 2048, 512], P(None, 'img', ('row', 'col'))
- new_small: float32 [2, 9360], replicated
- new_small_first: float32 [2, 9360], replicated
- new_small_second: float32 [2, 9360], replicated
The draws below stay inside these ranges and needn't reach their ends.
Inputs may be any that keep to these rules, and one draw needn't show every extreme that they name: rel_index[i, j] is a one-to-one relabeling, drawn from the seed, of the offset number (i // 7 - j // 7 + 6) * 13 + (i % 7 - j % 7 + 6).
All inputs are finite; a program needn't handle non-finite values.
Results may differ from the reference program's by a relative error of at most 0.025.
Values may be sent and summed in bfloat16 or wider, within the bound.
No kernel may reach another device: no remote copies, remote signals or barrier semaphores. Data moves between devices by JAX's collectives and lax.ppermute only.
A program may use at most 384 MiB of HBM per device.

```python
import math
import jax
import jax.numpy as jnp
from jax import lax

D = 512
HEADS = 16
HEAD_DIM = 32
MLP = 2048
WIN = 7
SHIFT = 3
LAYERS = 2
STEP = 10
IMAGES = 16
GRID = 56
RELPOS = 169
SMALL = 9360


def draw_rel_index(key, part):
    key = jax.random.fold_in(key, 7)
    token = jnp.arange(WIN * WIN, dtype=jnp.int32)
    down = token // WIN
    across = token % WIN
    offset = (down[:, None] - down[None, :] + WIN - 1) * (2 * WIN - 1) + (across[:, None] - across[None, :] + WIN - 1)
    relabel = jax.random.permutation(key, jnp.arange(RELPOS, dtype=jnp.int32))
    return relabel[offset].astype(jnp.int32)


def draw_small_params(key, part):
    key = jax.random.fold_in(key, 5)
    normal_draw = jnp.clip(jax.random.normal(key, (LAYERS, SMALL), jnp.float32), -4.0, 4.0)
    position = jnp.arange(SMALL)
    is_gain = (position < D) | (position >= 2 * D) & (position < 3 * D)
    is_table = position >= 9 * D + MLP
    factor = jnp.where(is_table, 1.0, jnp.where(is_gain, 0.2, 0.3))
    return jnp.where(is_gain, 1.0, 0.0) + factor * normal_draw


def level_of(key, dims, cuts, smallest, top_value):
    def one(axis_at, shards_of):
        steps = jax.random.uniform(jax.random.fold_in(jax.random.fold_in(key, 6), axis_at), (shards_of,), jnp.float32, smallest / len(cuts), top_value / len(cuts))
        return jnp.repeat(jnp.exp(steps), dims[axis_at] // shards_of).reshape((-1,) + (1,) * (len(dims) - axis_at - 1))

    factor_of = one(*cuts[0])
    for cut in cuts[1:]:
        factor_of = factor_of * one(*cut)
    return factor_of


def noise(stream_key, dims, scale, limit, cuts=(), kind=jnp.bfloat16):
    result = scale * jax.random.normal(stream_key, dims, jnp.float32)
    if cuts:
        result = result * level_of(stream_key, dims, cuts, -0.22, 0.18)
    return jnp.clip(result, -limit, limit).astype(kind)


def setup_inputs(seed: int = 0) -> dict:
    seeds = jax.random.split(jax.random.key(seed), 19)
    return {
        "images": noise(seeds[0], (IMAGES, GRID, GRID, D), 1.0, 6.0, ((0, 2), (1, 4), (2, 4)), jnp.float32),
        "grad_out": noise(seeds[1], (IMAGES, GRID, GRID, D), 1.0, 6.0, ((0, 2), (1, 4), (2, 4)), jnp.float32),
        "w_qkv": noise(seeds[2], (LAYERS, D, 3 * D), D ** -0.5, 0.25, ((1, 2), (2, 16)), jnp.float32),
        "w_proj": noise(seeds[3], (LAYERS, D, D), (D // 16) ** -0.5, 1.0, ((1, 2), (2, 16)), jnp.float32),
        "w_fc1": noise(seeds[4], (LAYERS, D, MLP), D ** -0.5, 0.25, ((1, 2), (2, 16)), jnp.float32),
        "w_fc2": noise(seeds[5], (LAYERS, MLP, D), MLP ** -0.5, 0.125, ((1, 2), (2, 16)), jnp.float32),
        "first_qkv": noise(seeds[6], (LAYERS, D, 3 * D), (0.1 * GRID * IMAGES ** 0.5), 128.0, ((1, 2), (2, 16)), jnp.float32),
        "first_proj": noise(seeds[7], (LAYERS, D, D), (0.1 * GRID * IMAGES ** 0.5), 128.0, ((1, 2), (2, 16)), jnp.float32),
        "first_fc1": noise(seeds[8], (LAYERS, D, MLP), (0.1 * GRID * IMAGES ** 0.5), 128.0, ((1, 2), (2, 16)), jnp.float32),
        "first_fc2": noise(seeds[9], (LAYERS, MLP, D), (0.1 * GRID * IMAGES ** 0.5), 128.0, ((1, 2), (2, 16)), jnp.float32),
        "second_qkv": jnp.clip(jnp.exp(math.log(200.0) - 1.3862944 * jax.random.uniform(seeds[10], (LAYERS, D, 3 * D), jnp.float32) ** level_of(seeds[10], (LAYERS, D, 3 * D), ((1, 2), (2, 16)), -0.2, 0.2)), 50.0, 200.0),
        "second_proj": jnp.clip(jnp.exp(math.log(200.0) - 1.3862944 * jax.random.uniform(seeds[11], (LAYERS, D, D), jnp.float32) ** level_of(seeds[11], (LAYERS, D, D), ((1, 2), (2, 16)), -0.2, 0.2)), 50.0, 200.0),
        "second_fc1": jnp.clip(jnp.exp(math.log(200.0) - 1.3862944 * jax.random.uniform(seeds[12], (LAYERS, D, MLP), jnp.float32) ** level_of(seeds[12], (LAYERS, D, MLP), ((1, 2), (2, 16)), -0.2, 0.2)), 50.0, 200.0),
        "second_fc2": jnp.clip(jnp.exp(math.log(200.0) - 1.3862944 * jax.random.uniform(seeds[13], (LAYERS, MLP, D), jnp.float32) ** level_of(seeds[13], (LAYERS, MLP, D), ((1, 2), (2, 16)), -0.2, 0.2)), 50.0, 200.0),
        "small_params": draw_small_params(jax.random.fold_in(seeds[18], 71), 0),
        "small_first": noise(seeds[15], (LAYERS, SMALL), (0.1 * GRID * IMAGES ** 0.5), 128.0, (), jnp.float32),
        "small_second": jnp.clip(jnp.exp(jax.random.uniform(seeds[16], (LAYERS, SMALL), jnp.float32, math.log(50.0), math.log(200.0))), 50.0, 200.0),
        "rel_index": draw_rel_index(jax.random.fold_in(seeds[18], 71), 0),
    }


EPS_NORM = 1e-05
BETA_ONE = 0.9
BETA_TWO = 0.999
EPS_ADAM = 1e-08
RATE_MATRIX = 0.05
RATE_SMALL = 0.3
DECAY_MATRIX = 0.05
MASKED = -1e+30
HIGHEST = lax.Precision.HIGHEST

@jax.custom_vjp
def low(v):
    return lax.optimization_barrier(v.astype(jnp.bfloat16)).astype(jnp.float32)

@jax.custom_vjp
def low_back(v):
    return v

def low_keep(v):
    return (low(v), None)

def low_pass(kept, grad):
    return (grad,)

def back_keep(v):
    return (v, None)

def back_low(kept, grad):
    return (low(grad),)
low.defvjp(low_keep, low_pass)
low_back.defvjp(back_keep, back_low)

def matmul(left, right):
    return jnp.dot(left, right, precision=HIGHEST, preferred_element_type=jnp.float32)

def layer_norm(inputs, gain_vec, shift_bias):
    center = inputs - lax.optimization_barrier(jnp.mean(inputs, axis=-1, keepdims=True))
    spread = lax.optimization_barrier(jnp.mean(center * center, axis=-1, keepdims=True))
    return center * lax.rsqrt(spread + EPS_NORM) * gain_vec + shift_bias

def split_small(vector):
    pieces = [vector[number * D:(number + 1) * D] for number in range(6)]
    pieces.append(vector[6 * D:9 * D])
    pieces.append(vector[9 * D:9 * D + MLP])
    pieces.append(vector[9 * D + MLP:].reshape(RELPOS, HEADS))
    return pieces

def to_windows(grid_field):
    batches, grid_side = (grid_field.shape[0], grid_field.shape[1])
    blocks = grid_side // WIN
    channels = grid_field.shape[-1]
    folded = grid_field.reshape(batches, blocks, WIN, blocks, WIN, channels)
    folded = folded.transpose(0, 1, 3, 2, 4, 5)
    return folded.reshape(batches * blocks * blocks, WIN * WIN, channels)

def from_windows(windows, batches, grid_side):
    blocks = grid_side // WIN
    channels = windows.shape[-1]
    folded = windows.reshape(batches, blocks, blocks, WIN, WIN, channels)
    folded = folded.transpose(0, 1, 3, 2, 4, 5)
    return folded.reshape(batches, grid_side, grid_side, channels)

def region_labels(grid_side):
    position = jnp.arange(grid_side, dtype=jnp.int32)
    band_index = (position >= grid_side - WIN).astype(jnp.int32) + (position >= grid_side - SHIFT).astype(jnp.int32)
    return 3 * band_index[:, None] + band_index[None, :]

def ref_layer(tokens, weights, small, rel_index, same_region):
    w_qkv, w_proj, w_fc1, w_fc2 = weights
    gain_one, bias_one, gain_two, bias_two, bias_proj, bias_fc2, bias_qkv, bias_fc1, pos_table = split_small(small)
    windows = tokens.shape[0] // (WIN * WIN)
    normed = low(layer_norm(tokens, gain_one, bias_one))
    qkv_rows = low(low_back(matmul(normed, low(w_qkv)) + bias_qkv))
    grouped = qkv_rows.reshape(windows, WIN * WIN, 3, HEADS, HEAD_DIM)
    queries, key_part, val_part = (grouped[:, :, 0], grouped[:, :, 1], grouped[:, :, 2])
    pos_bias = jnp.transpose(pos_table[rel_index], (2, 0, 1))
    scores = jnp.einsum('wqhd,wkhd->whqk', queries, key_part, precision=HIGHEST) * HEAD_DIM ** (-0.5) + pos_bias
    if same_region is not None:
        scores = jnp.where(same_region[:, None], scores, MASKED)
    scores = low_back(scores)
    largest = lax.optimization_barrier(jnp.max(scores, axis=-1, keepdims=True))
    powers = jnp.exp(scores - largest)
    attn_probs = powers / lax.optimization_barrier(jnp.sum(powers, axis=-1, keepdims=True))
    attended = jnp.einsum('whqk,wkhd->wqhd', low(attn_probs), val_part, precision=HIGHEST)
    attended = low(low_back(attended.reshape(tokens.shape[0], D)))
    middle = tokens + low_back(matmul(attended, low(w_proj)) + bias_proj)
    normed_two = low(layer_norm(middle, gain_two, bias_two))
    hidden_pre = low_back(matmul(normed_two, low(w_fc1)) + bias_fc1)
    activated = low(jax.nn.gelu(hidden_pre, approximate=False))
    return middle + low_back(matmul(activated, low(w_fc2)) + bias_fc2)

def forward(params, picture, rel_index):
    weights, small = (params[:4], params[4])
    grid_side = picture.shape[0]
    tokens = to_windows(picture[None]).reshape(-1, D)
    tokens = ref_layer(tokens, tuple((matrix[0] for matrix in weights)), small[0], rel_index, None)
    shifted = jnp.roll(from_windows(tokens, 1, grid_side)[0], (-SHIFT, -SHIFT), axis=(0, 1))
    labels = to_windows(region_labels(grid_side)[None, :, :, None])[:, :, 0]
    same_region = labels[:, :, None] == labels[:, None, :]
    tokens = to_windows(shifted[None]).reshape(-1, D)
    tokens = ref_layer(tokens, tuple((matrix[1] for matrix in weights)), small[1], rel_index, same_region)
    return jnp.roll(from_windows(tokens, 1, grid_side)[0], (SHIFT, SHIFT), axis=(0, 1))

def adam_step(weight, moment_one, second, gradient, rate_value, decay_rate):
    moment_one = BETA_ONE * moment_one + (1.0 - BETA_ONE) * gradient
    second = BETA_TWO * second + (1.0 - BETA_TWO) * gradient * gradient
    update = moment_one / (1.0 - BETA_ONE ** STEP) / (jnp.sqrt(second / (1.0 - BETA_TWO ** STEP)) + EPS_ADAM)
    return (weight - rate_value * (update + decay_rate * weight), moment_one, second)

def reference(images, grad_out, w_qkv, w_proj, w_fc1, w_fc2, first_qkv, first_proj, first_fc1, first_fc2, second_qkv, second_proj, second_fc1, second_fc2, small_params, small_first, small_second, rel_index):
    params = (w_qkv, w_proj, w_fc1, w_fc2, small_params)

    def one_image(totals, image_pair):
        picture, cotangent = image_pair
        outputs, backward = jax.vjp(lambda inner_params, inner_pic: forward(inner_params, inner_pic, rel_index), params, picture)
        grad_params, grad_image = backward(cotangent)
        return (jax.tree.map(jnp.add, totals, grad_params), (outputs, grad_image))
    zero_grads = jax.tree.map(jnp.zeros_like, params)
    totals, (outputs, grad_images) = lax.scan(one_image, zero_grads, (images, grad_out))
    firsts = (first_qkv, first_proj, first_fc1, first_fc2)
    seconds = (second_qkv, second_proj, second_fc1, second_fc2)
    updated = [adam_step(params[number], firsts[number], seconds[number], totals[number], RATE_MATRIX, DECAY_MATRIX) for number in range(4)]
    small_new = adam_step(small_params, small_first, small_second, totals[4], RATE_SMALL, 0.0)
    return (outputs, grad_images, updated[0][0], updated[1][0], updated[2][0], updated[3][0], updated[0][1], updated[1][1], updated[2][1], updated[3][1], updated[0][2], updated[1][2], updated[2][2], updated[3][2], small_new[0], small_new[1], small_new[2])
```

```python
from functools import partial

import jax
import jax.numpy as jnp
from jax import lax
from jax.experimental import pallas as pl
from jax.experimental.pallas import tpu as pltpu
from jax.sharding import PartitionSpec as P

D = 512
HEADS = 16
HEAD_DIM = 32
MLP = 2048
WIN = 7
SHIFT = 3
STEP = 10
RELPOS = 169

EPS_NORM = 1e-05
BETA_ONE = 0.9
BETA_TWO = 0.999
EPS_ADAM = 1e-08
RATE_MATRIX = 0.05
RATE_SMALL = 0.3
DECAY_MATRIX = 0.05
MASKED = -1e30

AXES = ("img", "row", "col")
F32 = jnp.float32
BF16 = jnp.bfloat16
LOG2E = 1.4426950408889634
SCALE = HEAD_DIM ** (-0.5)

SLOT = 8
WROWS = WIN * SLOT
AROWS = 64
PER_STEP = 2
CHUNK = 512
CHUNKS = MLP // CHUNK
HALF = D // 2
VMEM_LIMIT = 60 * 1024 * 1024


def mm(left, right):
    return lax.dot_general(left, right, (((1,), (0,)), ((), ())), preferred_element_type=F32)


def mm_t(left, right):
    return lax.dot_general(left, right, (((1,), (1,)), ((), ())), preferred_element_type=F32)


def t_mm(left, right):
    return lax.dot_general(left, right, (((0,), (0,)), ((), ())), preferred_element_type=F32)


def col_sum(value):
    return jnp.sum(value, axis=0, keepdims=True)


def normalize(rows):
    center = rows - jnp.mean(rows, axis=-1, keepdims=True)
    spread = jnp.mean(center * center, axis=-1, keepdims=True)
    rstd = lax.rsqrt(spread + EPS_NORM)
    return center * rstd, rstd


def norm_back(grad, xhat, rstd, gain):
    scaled = grad * gain
    mean_one = jnp.mean(scaled, axis=-1, keepdims=True)
    mean_two = jnp.mean(scaled * xhat, axis=-1, keepdims=True)
    return rstd * (scaled - mean_one - xhat * mean_two)


def gelu_both(pre):
    size = jnp.abs(pre)
    t = 1.0 / (1.0 + size * (0.3275911 * 0.7071067811865476))
    bell = jnp.exp2(pre * pre * (-0.5 * LOG2E))
    poly = 0.5 * 1.061405429
    poly = poly * t + 0.5 * -1.453152027
    poly = poly * t + 0.5 * 1.421413741
    poly = poly * t + 0.5 * -0.284496736
    poly = poly * t + 0.5 * 0.254829592
    tail = poly * t * bell
    cdf = jnp.where(pre >= 0.0, 1.0 - tail, tail)
    return pre * cdf, cdf + pre * bell * 0.3989422804014327


def grid_to_rows(grid_ref, slots):
    slots[:, :, WIN:, :] = jnp.zeros(slots[:, :, WIN:, :].shape, F32)
    for n in range(PER_STEP):
        for a in range(2):
            for b in range(2):
                slots[4 * n + 2 * a + b, :, :WIN, :] = grid_ref[
                    n, WIN * a : WIN * (a + 1), WIN * b : WIN * (b + 1), :
                ]
    return slots[...].reshape(4 * PER_STEP * WROWS, D)


def rows_to_grid(rows, slots, grid_ref):
    slots[...] = rows.reshape(4 * PER_STEP, WIN, SLOT, D)
    for n in range(PER_STEP):
        for a in range(2):
            for b in range(2):
                grid_ref[n, WIN * a : WIN * (a + 1), WIN * b : WIN * (b + 1), :] = slots[
                    4 * n + 2 * a + b, :, :WIN, :
                ]


def to_sixty_four(rows):
    windows = rows.shape[0] // WROWS
    channels = rows.shape[1]
    grouped = rows.reshape(windows, WROWS, channels)
    padding = jnp.zeros((windows, AROWS - WROWS, channels), F32)
    return jnp.concatenate([grouped, padding], axis=1).astype(BF16)


def head_masks():
    lane = lax.broadcasted_iota(jnp.int32, (16, HALF), 1)
    head = jnp.bitwise_and(lax.shift_right_logical(lane, 5), 3)
    return [jnp.where(head == a, 1.0, 0.0).astype(BF16) for a in range(4)]


def stack_heads(part, masks):
    split = part.reshape(AROWS // 16, 16, HALF)
    return jnp.concatenate(
        [(split * mask[None]).reshape(AROWS, HALF) for mask in masks], axis=0
    )


def stack_halves(part):
    zero = jnp.zeros((AROWS, HALF // 2), part.dtype)
    return jnp.concatenate(
        [
            jnp.concatenate([part[:, : HALF // 2], zero], axis=1),
            jnp.concatenate([zero, part[:, HALF // 2 :]], axis=1),
        ],
        axis=0,
    )


def pick_halves(result):
    return jnp.concatenate(
        [result[:WROWS, : HALF // 2], result[AROWS : AROWS + WROWS, HALF // 2 :]], axis=1
    )


def pick_heads(result):
    lane = lax.broadcasted_iota(jnp.int32, (WROWS, HALF), 1)
    head = jnp.bitwise_and(lax.shift_right_logical(lane, 5), 3)
    picked = result[3 * AROWS : 3 * AROWS + WROWS]
    for a in (2, 1, 0):
        picked = jnp.where(head == a, result[a * AROWS : a * AROWS + WROWS], picked)
    return picked


def pad_keys(value):
    padding = jnp.zeros((4, AROWS - WROWS, 128), F32)
    return jnp.concatenate([value, padding], axis=1).astype(BF16).reshape(4 * AROWS, 128)


def unpack_attention(pack_ref, w_qkv, w_proj):
    ranks = pack_ref.shape[1]
    n_qkv, n_proj = 3 * D // ranks, D // ranks
    for i in range(2):
        for r in range(ranks):
            cols = slice(i * HALF, (i + 1) * HALF)
            w_qkv[r * n_qkv : (r + 1) * n_qkv, cols] = pack_ref[i, r, :n_qkv, :]
            w_proj[r * n_proj : (r + 1) * n_proj, cols] = pack_ref[i, r, n_qkv:, :]


def pack_attention(g_qkv, g_proj, pack_ref):
    ranks = pack_ref.shape[1]
    n_qkv, n_proj = 3 * D // ranks, D // ranks
    for i in range(2):
        for r in range(ranks):
            cols = slice(i * HALF, (i + 1) * HALF)
            pack_ref[i, r, :n_qkv, :] = g_qkv[r * n_qkv : (r + 1) * n_qkv, cols].astype(BF16)
            pack_ref[i, r, n_qkv:, :] = g_proj[r * n_proj : (r + 1) * n_proj, cols].astype(BF16)


def mlp_pieces(ranks):
    n_one, n_two = MLP // ranks, D // ranks
    per_chunk = CHUNK // HALF
    for i in range(2):
        for r in range(ranks):
            row = r * n_one
            yield (
                (i, r, slice(0, n_one)),
                0,
                (row // CHUNK, slice(row % CHUNK, row % CHUNK + n_one), slice(i * HALF, (i + 1) * HALF)),
            )
            for kb in range(4):
                block = 4 * i + kb
                col = (block % per_chunk) * HALF
                yield (
                    (i, r, slice(n_one + kb * n_two, n_one + (kb + 1) * n_two)),
                    1,
                    (block // per_chunk, slice(r * n_two, (r + 1) * n_two), slice(col, col + HALF)),
                )


def attention_forward_kernel(
    layer, variants, x_ref, pack_ref, small_ref, bias_ref,
    xw_ref, qkv_ref, p_ref, att_ref, mid_ref, slots, w_qkv, w_proj, attf,
):
    @pl.when(pl.program_id(0) == 0)
    def _():
        unpack_attention(pack_ref, w_qkv, w_proj)

    gain = small_ref[layer : layer + 1, 0:D]
    shift = small_ref[layer : layer + 1, D : 2 * D]
    rows = grid_to_rows(x_ref, slots)
    xw_ref[...] = rows
    xhat, _ = normalize(rows)
    normed = (xhat * gain + shift).astype(BF16)
    for part in range(3):
        cols = slice(part * D, (part + 1) * D)
        bias = small_ref[layer : layer + 1, 6 * D + part * D : 7 * D + part * D]
        qkv_ref[:, :, cols] = to_sixty_four(mm_t(normed, w_qkv[cols, :]) + bias)
    masks = head_masks()

    def windows(at, carry):
        for k in range(2):
            w = 2 * at + k
            v = lax.rem(w, 4) if variants == 4 else 0
            for g in range(2):
                q = qkv_ref[w, :, g * HALF : (g + 1) * HALF]
                key = qkv_ref[w, :, D + g * HALF : D + (g + 1) * HALF]
                val = qkv_ref[w, :, 2 * D + g * HALF : 2 * D + (g + 1) * HALF]
                scores = mm_t(stack_heads(key, masks), stack_halves(q))
                scores = scores.reshape(4, AROWS, 128)[:, :WROWS] * (SCALE * LOG2E) + bias_ref[v, g]
                largest = jnp.max(scores, axis=1, keepdims=True)
                powers = jnp.exp2(scores - largest)
                total = jnp.sum(powers, axis=1, keepdims=True)
                probs = pad_keys(powers * (1.0 / total))
                p_ref[w, g] = probs
                attended = pick_halves(t_mm(probs, stack_heads(val, masks)))
                attf[pl.ds(pl.multiple_of(w * WROWS, 8), WROWS), g * HALF : (g + 1) * HALF] = attended
        return carry

    lax.fori_loop(0, 2 * PER_STEP, windows, 0)
    att = attf[...].astype(BF16)
    att_ref[...] = att
    bias = small_ref[layer : layer + 1, 4 * D : 5 * D]
    mid_ref[...] = rows + (mm_t(att, w_proj[...]) + bias)


def attention_backward_kernel(
    layer, gm_ref, xw_ref, qkv_ref, p_ref, att_ref, pack_ref, small_ref,
    dx_ref, dpack_ref, dtab_ref, dgain_ref, dshift_ref, dbproj_ref, dbqkv_ref,
    slots, w_qkv, w_proj, gat, dqkv, acc_qkv, acc_proj,
):
    step = pl.program_id(0)

    @pl.when(step == 0)
    def _():
        unpack_attention(pack_ref, w_qkv, w_proj)
        for ref in (dtab_ref, dgain_ref, dshift_ref, dbproj_ref, dbqkv_ref, acc_qkv, acc_proj):
            ref[...] = jnp.zeros(ref.shape, ref.dtype)

    gain = small_ref[layer : layer + 1, 0:D]
    shift = small_ref[layer : layer + 1, D : 2 * D]
    grad_mid = gm_ref[...]
    mid_low = grad_mid.astype(BF16)
    dbproj_ref[...] += col_sum(mid_low.astype(F32))
    acc_proj[...] += t_mm(mid_low, att_ref[...])
    gat[...] = to_sixty_four(mm(mid_low, w_proj[...]))
    masks = head_masks()

    def windows(at, carry):
        for g in range(2):
            total = None
            for k in range(2):
                w = 2 * at + k
                q = qkv_ref[w, :, g * HALF : (g + 1) * HALF]
                key = qkv_ref[w, :, D + g * HALF : D + (g + 1) * HALF]
                val = qkv_ref[w, :, 2 * D + g * HALF : 2 * D + (g + 1) * HALF]
                grad = stack_halves(gat[w, :, g * HALF : (g + 1) * HALF])
                probs = p_ref[w, g]
                dprobs = mm_t(stack_heads(val, masks), grad).reshape(4, AROWS, 128)[:, :WROWS]
                p = probs.astype(F32).reshape(4, AROWS, 128)[:, :WROWS]
                delta = jnp.sum(p * dprobs, axis=1, keepdims=True)
                dscores = p * (dprobs - delta)
                total = dscores if total is None else total + dscores
                low = pad_keys(dscores)
                at_row = pl.ds(pl.multiple_of(w * WROWS, 8), WROWS)
                dqkv[at_row, g * HALF : (g + 1) * HALF] = (
                    pick_halves(t_mm(low, stack_heads(key, masks))) * SCALE
                )
                dqkv[at_row, D + g * HALF : D + (g + 1) * HALF] = (
                    pick_heads(mm(low, stack_halves(q))) * SCALE
                )
                dqkv[at_row, 2 * D + g * HALF : 2 * D + (g + 1) * HALF] = pick_heads(mm(probs, grad))
            dtab_ref[g] += total
        return carry

    lax.fori_loop(0, 2 * PER_STEP, windows, 0)
    xhat, rstd = normalize(xw_ref[...])
    normed = (xhat * gain + shift).astype(BF16)
    grad_normed = None
    for part in range(3):
        cols = slice(part * D, (part + 1) * D)
        low = dqkv[:, cols].astype(BF16)
        dbqkv_ref[:, cols] += col_sum(low.astype(F32))
        acc_qkv[cols, :] += t_mm(low, normed)
        term = mm(low, w_qkv[cols, :])
        grad_normed = term if grad_normed is None else grad_normed + term
    dgain_ref[...] += col_sum(grad_normed * xhat)
    dshift_ref[...] += col_sum(grad_normed)
    rows_to_grid(grad_mid + norm_back(grad_normed, xhat, rstd, gain), slots, dx_ref)

    @pl.when(step == pl.num_programs(0) - 1)
    def _():
        pack_attention(acc_qkv, acc_proj, dpack_ref)


def mlp_forward_kernel(layer, mid_ref, pack_ref, small_ref, y_ref, act_ref, slope_ref, slots, weights):
    @pl.when(pl.program_id(0) == 0)
    def _():
        for src, which, dst in mlp_pieces(pack_ref.shape[1]):
            weights[(which,) + dst] = pack_ref[src]

    mid = mid_ref[...]
    xhat, _ = normalize(mid)
    gain = small_ref[layer : layer + 1, 2 * D : 3 * D]
    shift = small_ref[layer : layer + 1, 3 * D : 4 * D]
    normed = (xhat * gain + shift).astype(BF16)
    total = mid + small_ref[layer : layer + 1, 5 * D : 6 * D]
    for c in range(CHUNKS):
        bias = small_ref[layer : layer + 1, 9 * D + c * CHUNK : 9 * D + (c + 1) * CHUNK]
        act, slope = gelu_both(mm_t(normed, weights[0, c]) + bias)
        act = act.astype(BF16)
        act_ref[c] = act
        slope_ref[c] = slope.astype(BF16)
        total = total + mm_t(act, weights[1, c])
    rows_to_grid(total, slots, y_ref)


def mlp_backward_kernel(layer, forward, *refs):
    if forward:
        mid_ref, dy_ref, pack_ref, small_ref, y_ref = refs[:5]
        rest = refs[5:]
    else:
        mid_ref, dy_ref, act_ref, slope_ref, pack_ref, small_ref = refs[:6]
        rest = refs[6:]
    gm_ref, dpack_ref, dgain_ref, dshift_ref, dbtwo_ref, dbone_ref, slots, weights, accs = rest
    step = pl.program_id(0)

    @pl.when(step == 0)
    def _():
        for src, which, dst in mlp_pieces(pack_ref.shape[1]):
            weights[(which,) + dst] = pack_ref[src]
        for ref in (dgain_ref, dshift_ref, dbtwo_ref, dbone_ref, accs):
            ref[...] = jnp.zeros(ref.shape, ref.dtype)

    mid = mid_ref[...]
    xhat, rstd = normalize(mid)
    gain = small_ref[layer : layer + 1, 2 * D : 3 * D]
    shift = small_ref[layer : layer + 1, 3 * D : 4 * D]
    normed = (xhat * gain + shift).astype(BF16)
    dy = grid_to_rows(dy_ref, slots)
    dy_low = dy.astype(BF16)
    dbtwo_ref[...] += col_sum(dy_low.astype(F32))
    total = None
    if forward:
        total = mid + small_ref[layer : layer + 1, 5 * D : 6 * D]
    grad_normed = None
    for c in range(CHUNKS):
        if forward:
            bias = small_ref[layer : layer + 1, 9 * D + c * CHUNK : 9 * D + (c + 1) * CHUNK]
            act, slope = gelu_both(mm_t(normed, weights[0, c]) + bias)
            act = act.astype(BF16)
            total = total + mm_t(act, weights[1, c])
        else:
            act = act_ref[c]
            slope = slope_ref[c].astype(F32)
        grad_pre = (mm(dy_low, weights[1, c]) * slope).astype(BF16)
        dbone_ref[c] += col_sum(grad_pre.astype(F32))
        term = mm(grad_pre, weights[0, c])
        grad_normed = term if grad_normed is None else grad_normed + term
        accs[0, c] += t_mm(grad_pre, normed)
        accs[1, c] += t_mm(dy_low, act)
    dgain_ref[...] += col_sum(grad_normed * xhat)
    dshift_ref[...] += col_sum(grad_normed)
    gm_ref[...] = dy + norm_back(grad_normed, xhat, rstd, gain)
    if forward:
        rows_to_grid(total, slots, y_ref)

    @pl.when(step == pl.num_programs(0) - 1)
    def _():
        for src, which, dst in mlp_pieces(dpack_ref.shape[1]):
            dpack_ref[src] = accs[(which,) + dst].astype(BF16)


def fixed(shape):
    return pl.BlockSpec(shape, lambda s: (0,) * len(shape))


def stepped(shape, axis=0):
    return pl.BlockSpec(shape, lambda s: tuple(s if d == axis else 0 for d in range(len(shape))))


def call(kernel, steps, ins, in_specs, out_shapes, out_specs, scratch, flops, moved):
    return pl.pallas_call(
        kernel,
        grid=(steps,),
        in_specs=in_specs,
        out_shape=[jax.ShapeDtypeStruct(shape, kind) for shape, kind in out_shapes],
        out_specs=out_specs,
        scratch_shapes=scratch,
        compiler_params=pltpu.CompilerParams(
            dimension_semantics=("arbitrary",), vmem_limit_bytes=VMEM_LIMIT
        ),
        cost_estimate=pl.CostEstimate(flops=int(flops), bytes_accessed=int(moved), transcendentals=0),
    )(*ins)


STEP_WINDOWS = 4 * PER_STEP
STEP_ROWS = STEP_WINDOWS * WROWS
GRID_BLOCK = (PER_STEP, 2 * WIN, 2 * WIN, D)
SLOTS = pltpu.VMEM((STEP_WINDOWS, WIN, SLOT, D), F32)


def attention_forward(layer, grid_field, pack, small, bias):
    images = grid_field.shape[0]
    steps = images // PER_STEP
    rows = images * 4 * WROWS
    variants = bias.shape[0]
    return call(
        partial(attention_forward_kernel, layer, variants),
        steps,
        (grid_field, pack, small, bias),
        [stepped(GRID_BLOCK), fixed(pack.shape), fixed(small.shape), fixed(bias.shape)],
        [
            ((rows, D), F32),
            ((images * 4, AROWS, 3 * D), BF16),
            ((images * 4, 2, 4 * AROWS, 128), BF16),
            ((rows, D), BF16),
            ((rows, D), F32),
        ],
        [
            stepped((STEP_ROWS, D)),
            stepped((STEP_WINDOWS, AROWS, 3 * D)),
            stepped((STEP_WINDOWS, 2, 4 * AROWS, 128)),
            stepped((STEP_ROWS, D)),
            stepped((STEP_ROWS, D)),
        ],
        [
            SLOTS,
            pltpu.VMEM((3 * D, D), BF16),
            pltpu.VMEM((D, D), BF16),
            pltpu.VMEM((STEP_ROWS, D), F32),
        ],
        2 * rows * 4 * D * D * 2,
        30e6,
    )


def attention_backward(layer, grad_mid, saved, pack, small):
    xw, qkv, probs, att = saved
    rows = xw.shape[0]
    images = rows // (4 * WROWS)
    return call(
        partial(attention_backward_kernel, layer),
        images // PER_STEP,
        (grad_mid, xw, qkv, probs, att, pack, small),
        [
            stepped((STEP_ROWS, D)),
            stepped((STEP_ROWS, D)),
            stepped((STEP_WINDOWS, AROWS, 3 * D)),
            stepped((STEP_WINDOWS, 2, 4 * AROWS, 128)),
            stepped((STEP_ROWS, D)),
            fixed(pack.shape),
            fixed(small.shape),
        ],
        [
            ((images, 2 * WIN, 2 * WIN, D), F32),
            (pack.shape, BF16),
            ((2, 4, WROWS, 128), F32),
            ((1, D), F32),
            ((1, D), F32),
            ((1, D), F32),
            ((1, 3 * D), F32),
        ],
        [
            stepped(GRID_BLOCK),
            fixed(pack.shape),
            fixed((2, 4, WROWS, 128)),
            fixed((1, D)),
            fixed((1, D)),
            fixed((1, D)),
            fixed((1, 3 * D)),
        ],
        [
            SLOTS,
            pltpu.VMEM((3 * D, D), BF16),
            pltpu.VMEM((D, D), BF16),
            pltpu.VMEM((STEP_WINDOWS, AROWS, D), BF16),
            pltpu.VMEM((STEP_ROWS, 3 * D), F32),
            pltpu.VMEM((3 * D, D), F32),
            pltpu.VMEM((D, D), F32),
        ],
        2 * rows * 4 * D * D * 5,
        30e6,
    )


def mlp_forward(layer, mid, pack, small):
    rows = mid.shape[0]
    images = rows // (4 * WROWS)
    return call(
        partial(mlp_forward_kernel, layer),
        images // PER_STEP,
        (mid, pack, small),
        [stepped((STEP_ROWS, D)), fixed(pack.shape), fixed(small.shape)],
        [
            ((images, 2 * WIN, 2 * WIN, D), F32),
            ((CHUNKS, rows, CHUNK), BF16),
            ((CHUNKS, rows, CHUNK), BF16),
        ],
        [
            stepped(GRID_BLOCK),
            stepped((CHUNKS, STEP_ROWS, CHUNK), 1),
            stepped((CHUNKS, STEP_ROWS, CHUNK), 1),
        ],
        [SLOTS, pltpu.VMEM((2, CHUNKS, CHUNK, D), BF16)],
        2 * rows * 2 * D * MLP,
        26e6,
    )


def mlp_backward(layer, mid, dy, saved, pack, small):
    rows = mid.shape[0]
    images = rows // (4 * WROWS)
    forward = not saved
    hidden = stepped((CHUNKS, STEP_ROWS, CHUNK), 1)
    outs = [
        ((rows, D), F32),
        (pack.shape, BF16),
        ((1, D), F32),
        ((1, D), F32),
        ((1, D), F32),
        ((CHUNKS, 1, CHUNK), F32),
    ]
    out_specs = [
        stepped((STEP_ROWS, D)),
        fixed(pack.shape),
        fixed((1, D)),
        fixed((1, D)),
        fixed((1, D)),
        fixed((CHUNKS, 1, CHUNK)),
    ]
    if forward:
        outs = [((images, 2 * WIN, 2 * WIN, D), F32)] + outs
        out_specs = [stepped(GRID_BLOCK)] + out_specs
    return call(
        partial(mlp_backward_kernel, layer, forward),
        images // PER_STEP,
        (mid, dy) + tuple(saved) + (pack, small),
        [stepped((STEP_ROWS, D)), stepped(GRID_BLOCK)]
        + [hidden] * len(saved)
        + [fixed(pack.shape), fixed(small.shape)],
        outs,
        out_specs,
        [SLOTS, pltpu.VMEM((2, CHUNKS, CHUNK, D), BF16), pltpu.VMEM((2, CHUNKS, CHUNK, D), F32)],
        2 * rows * (6 if forward else 4) * D * MLP,
        30e6,
    )


def passed_along(x, axis, by):
    size = lax.axis_size(axis)
    return lax.ppermute(x, axis, [(i, (i + by) % size) for i in range(size)])


def pull_next(grid_field):
    from_below = passed_along(grid_field[:, :SHIFT].astype(BF16), "row", -1).astype(F32)
    grid_field = jnp.concatenate([grid_field[:, SHIFT:], from_below], axis=1)
    from_right = passed_along(grid_field[:, :, :SHIFT].astype(BF16), "col", -1).astype(F32)
    return jnp.concatenate([grid_field[:, :, SHIFT:], from_right], axis=2)


def pull_prev(grid_field):
    from_above = passed_along(grid_field[:, -SHIFT:].astype(BF16), "row", 1).astype(F32)
    grid_field = jnp.concatenate([from_above, grid_field[:, :-SHIFT]], axis=1)
    from_left = passed_along(grid_field[:, :, -SHIFT:].astype(BF16), "col", 1).astype(F32)
    return jnp.concatenate([from_left, grid_field[:, :, :-SHIFT]], axis=2)


def tile_labels(tile_side):
    whole_side = tile_side * lax.axis_size("row")
    local = jnp.arange(tile_side, dtype=jnp.int32)

    def band(axis):
        at = lax.axis_index(axis) * tile_side + local
        return (at >= whole_side - WIN).astype(jnp.int32) + (at >= whole_side - SHIFT).astype(
            jnp.int32
        )

    return 3 * band("row")[:, None] + band("col")[None, :]


def padded_pairs(pairs, fill):
    lead = pairs.shape[:-2]
    swapped = jnp.swapaxes(pairs, -1, -2).reshape(lead + (WIN, WIN, WIN, WIN))
    none = [(0, 0)] * len(lead)
    swapped = jnp.pad(swapped, none + [(0, 0), (0, SLOT - WIN), (0, 0), (0, 0)], constant_values=fill)
    swapped = jnp.pad(
        swapped,
        none + [(0, 0), (0, 0), (0, AROWS // SLOT - WIN), (0, SLOT - WIN)],
        constant_values=0 if fill == MASKED else fill,
    )
    return swapped.reshape(lead + (WROWS, AROWS))


def score_bias(table, rel_index, same_region):
    values = table.T[:, rel_index.reshape(-1)].reshape(HEADS, WIN * WIN, WIN * WIN) * LOG2E
    if same_region is None:
        values = values[None]
    else:
        values = jnp.where(same_region[:, None], values[None], MASKED)
    padded = padded_pairs(values, MASKED)
    variants = padded.shape[0]
    padded = padded.reshape(variants, 2, 2, 4, WROWS, AROWS).transpose(0, 1, 3, 4, 2, 5)
    return padded.reshape(variants, 2, 4, WROWS, 2 * AROWS)


def table_grad(dtab, rel_index):
    index = padded_pairs(rel_index, -1).reshape(-1)
    onehot = (index[:, None] == jnp.arange(RELPOS, dtype=jnp.int32)[None, :]).astype(F32)
    sums = dtab.reshape(2, 4, WROWS, 2, AROWS).transpose(0, 3, 1, 2, 4).reshape(HEADS, -1)
    return jnp.dot(sums, onehot, precision=lax.Precision.HIGHEST).T.reshape(-1)


def gather_pack(pack):
    size = lax.axis_size("img")
    ranks = lax.axis_size("row") * lax.axis_size("col")
    whole = lax.all_gather(pack, AXES, axis=0, tiled=False)
    return whole.reshape((size, ranks) + pack.shape)


def scatter_pack(whole, rows, cols):
    return lax.psum_scatter(
        whole.reshape(-1, cols), AXES, scatter_dimension=0, tiled=True
    ).astype(F32)


def attention_pack(w_qkv, w_proj):
    return jnp.concatenate([w_qkv.astype(BF16).T, w_proj.astype(BF16).T], axis=0)


def mlp_pack(w_fc1, w_fc2):
    cols = w_fc1.shape[0]
    second = w_fc2.astype(BF16).T
    second = second.reshape(second.shape[0], 4, cols).transpose(1, 0, 2).reshape(-1, cols)
    return jnp.concatenate([w_fc1.astype(BF16).T, second], axis=0)


def attention_canonical(whole):
    size, ranks, rows, cols = whole.shape
    if size == 2:
        return whole
    whole = whole.transpose(1, 2, 0, 3).reshape(ranks, rows, 2, HALF)
    return whole.transpose(2, 0, 1, 3)


def attention_shards(pack, size):
    if size == 2:
        return pack
    _, ranks, rows, _ = pack.shape
    pack = pack.transpose(1, 2, 0, 3).reshape(ranks, rows, size, D // size)
    return pack.transpose(2, 0, 1, 3)


def mlp_canonical(whole):
    size, ranks, _, cols = whole.shape
    if size == 2:
        return whole
    n_one = MLP // ranks
    n_two = D // ranks
    first = attention_canonical(whole[:, :, :n_one])
    second = whole[:, :, n_one:].reshape(size, ranks, 4, n_two, cols)
    second = second.transpose(1, 3, 0, 2, 4).reshape(ranks, n_two, 2, 4, HALF)
    second = second.transpose(2, 0, 3, 1, 4).reshape(2, ranks, 4 * n_two, HALF)
    return jnp.concatenate([first, second], axis=2)


def mlp_shards(pack, size):
    if size == 2:
        return pack
    _, ranks, _, _ = pack.shape
    n_one = MLP // ranks
    n_two = D // ranks
    cols = D // size
    first = attention_shards(pack[:, :, :n_one], size)
    second = pack[:, :, n_one:].reshape(2, ranks, 4, n_two, HALF)
    second = second.transpose(1, 3, 0, 2, 4).reshape(ranks, n_two, size, 4, cols)
    second = second.transpose(2, 0, 3, 1, 4).reshape(size, ranks, 4 * n_two, cols)
    return jnp.concatenate([first, second], axis=2)


def adam_step(weight, moment_one, second, gradient, rate_value, decay_rate):
    moment_one = BETA_ONE * moment_one + (1.0 - BETA_ONE) * gradient
    second = BETA_TWO * second + (1.0 - BETA_TWO) * gradient * gradient
    update = (
        moment_one / (1.0 - BETA_ONE**STEP) / (jnp.sqrt(second / (1.0 - BETA_TWO**STEP)) + EPS_ADAM)
    )
    return (weight - rate_value * (update + decay_rate * weight), moment_one, second)


def shards(
    images,
    grad_out,
    w_qkv,
    w_proj,
    w_fc1,
    w_fc2,
    first_qkv,
    first_proj,
    first_fc1,
    first_fc2,
    second_qkv,
    second_proj,
    second_fc1,
    second_fc2,
    small_params,
    small_first,
    small_second,
    rel_index,
):
    grid_side = images.shape[1]
    size = lax.axis_size("img")
    packs_a = [
        attention_canonical(gather_pack(attention_pack(w_qkv[l], w_proj[l]))) for l in range(2)
    ]
    packs_b = [mlp_canonical(gather_pack(mlp_pack(w_fc1[l], w_fc2[l]))) for l in range(2)]

    labels = tile_labels(grid_side).reshape(2, WIN, 2, WIN).transpose(0, 2, 1, 3).reshape(4, -1)
    same_region = labels[:, :, None] == labels[:, None, :]
    tables = [small_params[l, 9 * D + MLP :].reshape(RELPOS, HEADS) for l in range(2)]
    biases = [
        score_bias(tables[0], rel_index, None),
        score_bias(tables[1], rel_index, same_region),
    ]
    grad_shifted = pull_next(grad_out)

    *saved_zero, mid_zero = attention_forward(0, images, packs_a[0], small_params, biases[0])
    out_zero, act_zero, slope_zero = mlp_forward(0, mid_zero, packs_b[0], small_params)
    shifted = pull_next(out_zero)
    *saved_one, mid_one = attention_forward(1, shifted, packs_a[1], small_params, biases[1])
    out_one, gm_one, dpack_b_one, *small_b_one = mlp_backward(
        1, mid_one, grad_shifted, (), packs_b[1], small_params
    )
    outputs = pull_prev(out_one)
    dx_one, dpack_a_one, dtab_one, *small_a_one = attention_backward(
        1, gm_one, saved_one, packs_a[1], small_params
    )
    grad_mid = pull_prev(dx_one)
    gm_zero, dpack_b_zero, *small_b_zero = mlp_backward(
        0, mid_zero, grad_mid, (act_zero, slope_zero), packs_b[0], small_params
    )
    grad_input, dpack_a_zero, dtab_zero, *small_a_zero = attention_backward(
        0, gm_zero, saved_zero, packs_a[0], small_params
    )

    cols = D // size
    sums_a, sums_b = [], []
    for dpack_a, dpack_b in ((dpack_a_zero, dpack_b_zero), (dpack_a_one, dpack_b_one)):
        sums_a.append(scatter_pack(attention_shards(dpack_a, size), None, cols))
        sums_b.append(scatter_pack(mlp_shards(dpack_b, size), None, cols))
    n_qkv = w_qkv.shape[2]
    n_one = w_fc1.shape[2]
    n_two = w_fc2.shape[2]
    grads = (
        jnp.stack([s[:n_qkv].T for s in sums_a]),
        jnp.stack([s[n_qkv:].T for s in sums_a]),
        jnp.stack([s[:n_one].T for s in sums_b]),
        jnp.stack(
            [s[n_one:].reshape(4, n_two, cols).transpose(0, 2, 1).reshape(4 * cols, n_two) for s in sums_b]
        ),
    )

    small_grads = []
    for (dgain, dshift, dbproj, dbqkv), (dgain2, dshift2, dbtwo, dbone), dtab in (
        (small_a_zero, small_b_zero, dtab_zero),
        (small_a_one, small_b_one, dtab_one),
    ):
        pieces = (dgain, dshift, dgain2, dshift2, dbproj, dbtwo, dbqkv, dbone)
        small_grads.append(
            jnp.concatenate([piece.reshape(-1) for piece in pieces] + [table_grad(dtab, rel_index)])
        )
    small_grad = lax.psum(jnp.stack(small_grads), AXES)

    masters = (w_qkv, w_proj, w_fc1, w_fc2)
    firsts = (first_qkv, first_proj, first_fc1, first_fc2)
    seconds = (second_qkv, second_proj, second_fc1, second_fc2)
    updated = [
        adam_step(masters[k], firsts[k], seconds[k], grads[k], RATE_MATRIX, DECAY_MATRIX)
        for k in range(4)
    ]
    small_new = adam_step(small_params, small_first, small_second, small_grad, RATE_SMALL, 0.0)
    return (
        (outputs, grad_input)
        + tuple(new[0] for new in updated)
        + tuple(new[1] for new in updated)
        + tuple(new[2] for new in updated)
        + tuple(small_new)
    )


def solution(mesh):
    grid_spec = P("img", "row", "col", None)
    matrix = P(None, "img", ("row", "col"))
    in_specs = (grid_spec,) * 2 + (matrix,) * 12 + (P(),) * 4
    out_specs = (grid_spec,) * 2 + (matrix,) * 12 + (P(),) * 3
    return jax.shard_map(shards, mesh=mesh, in_specs=in_specs, out_specs=out_specs, check_vma=False)
```

```python
from functools import partial

import jax
import jax.numpy as jnp
from jax import lax
from jax.experimental import pallas as pl
from jax.experimental.pallas import tpu as pltpu
from jax.sharding import PartitionSpec as P

D = 512
HEADS = 16
HEAD_DIM = 32
MLP = 2048
WIN = 7
SHIFT = 3
STEP = 10
RELPOS = 169

EPS_NORM = 1e-05
BETA_ONE = 0.9
BETA_TWO = 0.999
EPS_ADAM = 1e-08
RATE_MATRIX = 0.05
RATE_SMALL = 0.3
DECAY_MATRIX = 0.05
MASKED = -1e30

AXES = ("img", "row", "col")
F32 = jnp.float32
BF16 = jnp.bfloat16
LOG2E = 1.4426950408889634
SCALE = HEAD_DIM ** (-0.5)

SLOT = 8
WROWS = WIN * SLOT
AROWS = 64
PER_STEP = 2
CHUNK = 512
CHUNKS = MLP // CHUNK
HALF = D // 2
VMEM_LIMIT = 60 * 1024 * 1024


def mm(left, right):
    return lax.dot_general(left, right, (((1,), (0,)), ((), ())), preferred_element_type=F32)


def mm_t(left, right):
    return lax.dot_general(left, right, (((1,), (1,)), ((), ())), preferred_element_type=F32)


def t_mm(left, right):
    return lax.dot_general(left, right, (((0,), (0,)), ((), ())), preferred_element_type=F32)


def col_sum(value):
    return jnp.sum(value, axis=0, keepdims=True)


def normalize(rows):
    center = rows - jnp.mean(rows, axis=-1, keepdims=True)
    spread = jnp.mean(center * center, axis=-1, keepdims=True)
    rstd = lax.rsqrt(spread + EPS_NORM)
    return center * rstd, rstd


def norm_back(grad, xhat, rstd, gain):
    scaled = grad * gain
    mean_one = jnp.mean(scaled, axis=-1, keepdims=True)
    mean_two = jnp.mean(scaled * xhat, axis=-1, keepdims=True)
    return rstd * (scaled - mean_one - xhat * mean_two)


def gelu_both(pre):
    size = jnp.abs(pre)
    t = 1.0 / (1.0 + size * (0.3275911 * 0.7071067811865476))
    bell = jnp.exp2(pre * pre * (-0.5 * LOG2E))
    poly = 0.5 * 1.061405429
    poly = poly * t + 0.5 * -1.453152027
    poly = poly * t + 0.5 * 1.421413741
    poly = poly * t + 0.5 * -0.284496736
    poly = poly * t + 0.5 * 0.254829592
    tail = poly * t * bell
    cdf = jnp.where(pre >= 0.0, 1.0 - tail, tail)
    return pre * cdf, cdf + pre * bell * 0.3989422804014327


def clear_padding(slots):
    slots[:, :, WIN:, :] = jnp.zeros(slots[:, :, WIN:, :].shape, F32)


def slot_rows(slots):
    return slots[...].reshape(4 * PER_STEP * WROWS, D)


def grid_to_rows(grid_ref, slots):
    clear_padding(slots)
    for n in range(PER_STEP):
        for a in range(2):
            for b in range(2):
                slots[4 * n + 2 * a + b, :, :WIN, :] = grid_ref[
                    n, WIN * a : WIN * (a + 1), WIN * b : WIN * (b + 1), :
                ]
    return slot_rows(slots)


def next_to_rows(grid_ref, strip_refs, slots):
    clear_padding(slots)
    rows_ref, cols_ref, corner_ref = strip_refs
    side, kept = 2 * WIN, WIN - SHIFT
    for n in range(PER_STEP):
        low = rows_ref[n].astype(F32)
        right = cols_ref[n].astype(F32)
        corner = corner_ref[n].astype(F32)
        w = 4 * n
        slots[w, :, :WIN, :] = grid_ref[n, SHIFT : SHIFT + WIN, SHIFT : SHIFT + WIN, :]
        slots[w + 1, :, :kept, :] = grid_ref[n, SHIFT : SHIFT + WIN, SHIFT + WIN : side, :]
        slots[w + 1, :, kept:WIN, :] = right[:WIN]
        slots[w + 2, :kept, :WIN, :] = grid_ref[n, SHIFT + WIN : side, SHIFT : SHIFT + WIN, :]
        slots[w + 2, kept:, :WIN, :] = low[:, :WIN]
        slots[w + 3, :kept, :kept, :] = grid_ref[n, SHIFT + WIN : side, SHIFT + WIN : side, :]
        slots[w + 3, :kept, kept:WIN, :] = right[WIN:]
        slots[w + 3, kept:, :kept, :] = low[:, WIN:]
        slots[w + 3, kept:, kept:WIN, :] = corner
    return slot_rows(slots)


def prev_to_rows(grid_ref, strip_refs, slots):
    clear_padding(slots)
    rows_ref, cols_ref, corner_ref = strip_refs
    kept = WIN - SHIFT
    for n in range(PER_STEP):
        high = rows_ref[n].astype(F32)
        left = cols_ref[n].astype(F32)
        corner = corner_ref[n].astype(F32)
        w = 4 * n
        slots[w, :SHIFT, :SHIFT, :] = corner
        slots[w, :SHIFT, SHIFT:WIN, :] = high[:, :kept]
        slots[w, SHIFT:, :SHIFT, :] = left[:kept]
        slots[w, SHIFT:, SHIFT:WIN, :] = grid_ref[n, :kept, :kept, :]
        slots[w + 1, :SHIFT, :WIN, :] = high[:, kept:]
        slots[w + 1, SHIFT:, :WIN, :] = grid_ref[n, :kept, kept : kept + WIN, :]
        slots[w + 2, :, :SHIFT, :] = left[kept:]
        slots[w + 2, :, SHIFT:WIN, :] = grid_ref[n, kept : kept + WIN, :kept, :]
        slots[w + 3, :, :WIN, :] = grid_ref[n, kept : kept + WIN, kept : kept + WIN, :]
    return slot_rows(slots)


def rows_to_grid(rows, slots, grid_ref):
    slots[...] = rows.reshape(4 * PER_STEP, WIN, SLOT, D)
    for n in range(PER_STEP):
        for a in range(2):
            for b in range(2):
                grid_ref[n, WIN * a : WIN * (a + 1), WIN * b : WIN * (b + 1), :] = slots[
                    4 * n + 2 * a + b, :, :WIN, :
                ]


def first_strips(grid_ref, strip_refs):
    rows_ref, cols_ref, corner_ref = strip_refs
    rows_ref[...] = grid_ref[:, :SHIFT, SHIFT:, :].astype(BF16)
    cols_ref[...] = grid_ref[:, SHIFT:, :SHIFT, :].astype(BF16)
    corner_ref[...] = grid_ref[:, :SHIFT, :SHIFT, :].astype(BF16)


def last_strips(grid_ref, strip_refs):
    rows_ref, cols_ref, corner_ref = strip_refs
    kept = 2 * WIN - SHIFT
    rows_ref[...] = grid_ref[:, kept:, :kept, :].astype(BF16)
    cols_ref[...] = grid_ref[:, :kept, kept:, :].astype(BF16)
    corner_ref[...] = grid_ref[:, kept:, kept:, :].astype(BF16)


def to_sixty_four(rows):
    windows = rows.shape[0] // WROWS
    channels = rows.shape[1]
    grouped = rows.reshape(windows, WROWS, channels)
    padding = jnp.zeros((windows, AROWS - WROWS, channels), F32)
    return jnp.concatenate([grouped, padding], axis=1).astype(BF16)


def head_masks():
    lane = lax.broadcasted_iota(jnp.int32, (16, HALF), 1)
    head = jnp.bitwise_and(lax.shift_right_logical(lane, 5), 3)
    return [jnp.where(head == a, 1.0, 0.0).astype(BF16) for a in range(4)]


def stack_heads(part, masks):
    split = part.reshape(AROWS // 16, 16, HALF)
    return jnp.concatenate(
        [(split * mask[None]).reshape(AROWS, HALF) for mask in masks], axis=0
    )


def stack_halves(part):
    zero = jnp.zeros((AROWS, HALF // 2), part.dtype)
    return jnp.concatenate(
        [
            jnp.concatenate([part[:, : HALF // 2], zero], axis=1),
            jnp.concatenate([zero, part[:, HALF // 2 :]], axis=1),
        ],
        axis=0,
    )


def pick_halves(result):
    return jnp.concatenate(
        [result[:WROWS, : HALF // 2], result[AROWS : AROWS + WROWS, HALF // 2 :]], axis=1
    )


def pick_heads(result):
    lane = lax.broadcasted_iota(jnp.int32, (WROWS, HALF), 1)
    head = jnp.bitwise_and(lax.shift_right_logical(lane, 5), 3)
    picked = result[3 * AROWS : 3 * AROWS + WROWS]
    for a in (2, 1, 0):
        picked = jnp.where(head == a, result[a * AROWS : a * AROWS + WROWS], picked)
    return picked


def pad_keys(value):
    padding = jnp.zeros((4, AROWS - WROWS, 128), F32)
    return jnp.concatenate([value, padding], axis=1).astype(BF16).reshape(4 * AROWS, 128)


def places(at_ref):
    for core in range(2):
        for quad in range(4):
            for across in range(4):
                i = jnp.bitwise_xor(at_ref[0], quad >> 1)
                y = jnp.bitwise_xor(at_ref[1], quad & 1)
                c = jnp.bitwise_xor(at_ref[2], core)
                z = jnp.bitwise_xor(at_ref[3], across)
                yield core, (quad, across), i, (2 * y + c) * 4 + z


def piece(start, length):
    return pl.ds(pl.multiple_of(start * length, length), length)


N_QKV = 3 * D // 16
N_OUT = D // 16
N_FC1 = MLP // 16


def unpack_attention(at_ref, packs, w_qkv, w_proj):
    for core, at, i, r in places(at_ref):
        cols = piece(i, HALF)
        w_qkv[piece(r, N_QKV), cols] = packs[core][at + (slice(0, N_QKV),)]
        w_proj[piece(r, N_OUT), cols] = packs[core][at + (slice(N_QKV, None),)]


def pack_attention(at_ref, g_qkv, g_proj, packs):
    for core, at, i, r in places(at_ref):
        cols = piece(i, HALF)
        packs[core][at + (slice(0, N_QKV),)] = g_qkv[piece(r, N_QKV), cols].astype(BF16)
        packs[core][at + (slice(N_QKV, None),)] = g_proj[piece(r, N_OUT), cols].astype(BF16)


def unpack_mlp(at_ref, packs, w_one, w_two):
    for core, at, i, r in places(at_ref):
        w_one[piece(r, N_FC1), piece(i, HALF)] = packs[core][at + (slice(0, N_FC1),)]
        for k in range(4):
            w_two[2 * i + k // 2, piece(r, N_OUT), (k % 2) * HALF : (k % 2 + 1) * HALF] = packs[core][
                at + (slice(N_FC1 + k * N_OUT, N_FC1 + (k + 1) * N_OUT),)
            ]


def pack_mlp(at_ref, g_one, g_two, packs):
    for core, at, i, r in places(at_ref):
        packs[core][at + (slice(0, N_FC1),)] = g_one[piece(r, N_FC1), piece(i, HALF)].astype(BF16)
        for k in range(4):
            packs[core][at + (slice(N_FC1 + k * N_OUT, N_FC1 + (k + 1) * N_OUT),)] = g_two[
                2 * i + k // 2, piece(r, N_OUT), (k % 2) * HALF : (k % 2 + 1) * HALF
            ].astype(BF16)


def spread_bias(layer, at_ref, base_ref, bias):
    row = lax.broadcasted_iota(jnp.int32, (WROWS, 2 * AROWS), 0)
    lane = jnp.bitwise_and(lax.broadcasted_iota(jnp.int32, (WROWS, 2 * AROWS), 1), AROWS - 1)
    key_row, key_col = row // SLOT, jnp.bitwise_and(row, SLOT - 1)
    query_row, query_col = lane // SLOT, jnp.bitwise_and(lane, SLOT - 1)
    kept = WIN - SHIFT
    other_row = ((key_row >= kept) != (query_row >= kept)).astype(jnp.int32)
    other_col = ((key_col >= kept) != (query_col >= kept)).astype(jnp.int32)
    padding = (key_col == WIN).astype(jnp.int32)
    for v in range(bias.shape[0]):
        hidden = padding
        if layer == 1:
            if v >> 1:
                hidden = hidden + other_row * at_ref[4]
            if v & 1:
                hidden = hidden + other_col * at_ref[5]
        for g in range(2):
            for a in range(4):
                both = jnp.concatenate([base_ref[8 * g + a], base_ref[8 * g + 4 + a]], axis=1)
                bias[v, g, a] = jnp.where(hidden > 0, MASKED, both)


def attention_forward_kernel(layer, at_ref, x_ref, *refs):
    strips = refs[: 3 * layer]
    packs = refs[3 * layer : 3 * layer + 2]
    small_ref, base_ref, xw_ref, qkv_ref, p_ref, att_ref, mid_ref = refs[3 * layer + 2 : 3 * layer + 9]
    slots, w_qkv, w_proj, attf, bias_ref = refs[3 * layer + 9 :]
    variants = bias_ref.shape[0]

    @pl.when(pl.program_id(0) == 0)
    def _():
        unpack_attention(at_ref, packs, w_qkv, w_proj)
        spread_bias(layer, at_ref, base_ref, bias_ref)

    gain = small_ref[layer : layer + 1, 0:D]
    shift = small_ref[layer : layer + 1, D : 2 * D]
    rows = next_to_rows(x_ref, strips, slots) if layer else grid_to_rows(x_ref, slots)
    xw_ref[...] = rows
    xhat, _ = normalize(rows)
    normed = (xhat * gain + shift).astype(BF16)
    for part in range(3):
        cols = slice(part * D, (part + 1) * D)
        bias = small_ref[layer : layer + 1, 6 * D + part * D : 7 * D + part * D]
        qkv_ref[:, :, cols] = to_sixty_four(mm_t(normed, w_qkv[cols, :]) + bias)
    masks = head_masks()

    def windows(at, carry):
        for k in range(2):
            w = 2 * at + k
            v = lax.rem(w, 4) if variants == 4 else 0
            for g in range(2):
                q = qkv_ref[w, :, g * HALF : (g + 1) * HALF]
                key = qkv_ref[w, :, D + g * HALF : D + (g + 1) * HALF]
                val = qkv_ref[w, :, 2 * D + g * HALF : 2 * D + (g + 1) * HALF]
                scores = mm_t(stack_heads(key, masks), stack_halves(q))
                scores = scores.reshape(4, AROWS, 128)[:, :WROWS] * (SCALE * LOG2E) + bias_ref[v, g]
                largest = jnp.max(scores, axis=1, keepdims=True)
                powers = jnp.exp2(scores - largest)
                total = jnp.sum(powers, axis=1, keepdims=True)
                probs = pad_keys(powers * (1.0 / total))
                p_ref[w, g] = probs
                attended = pick_halves(t_mm(probs, stack_heads(val, masks)))
                attf[pl.ds(pl.multiple_of(w * WROWS, 8), WROWS), g * HALF : (g + 1) * HALF] = attended
        return carry

    lax.fori_loop(0, 2 * PER_STEP, windows, 0)
    att = attf[...].astype(BF16)
    att_ref[...] = att
    bias = small_ref[layer : layer + 1, 4 * D : 5 * D]
    mid_ref[...] = rows + (mm_t(att, w_proj[...]) + bias)


def attention_backward_kernel(layer, at_ref, gm_ref, xw_ref, qkv_ref, p_ref, att_ref, *refs):
    packs, refs = refs[:2], refs[2:]
    small_ref, rest_ref, dx_ref = refs[:3]
    strips, refs = refs[3 : 3 + 3 * layer], refs[3 + 3 * layer :]
    dpacks, refs = refs[:2], refs[2:]
    dtab_ref, dsmall_ref, slots, w_qkv, w_proj, gat, dqkv, acc_qkv, acc_proj, acc_tab = refs
    step = pl.program_id(0)

    @pl.when(step == 0)
    def _():
        unpack_attention(at_ref, packs, w_qkv, w_proj)
        dsmall_ref[...] = rest_ref[...]
        for ref in (acc_tab, acc_qkv, acc_proj):
            ref[...] = jnp.zeros(ref.shape, ref.dtype)

    gain = small_ref[layer : layer + 1, 0:D]
    shift = small_ref[layer : layer + 1, D : 2 * D]
    grad_mid = gm_ref[...]
    mid_low = grad_mid.astype(BF16)
    dsmall_ref[:, 4 * D : 5 * D] += col_sum(mid_low.astype(F32))
    acc_proj[...] += t_mm(mid_low, att_ref[...])
    gat[...] = to_sixty_four(mm(mid_low, w_proj[...]))
    masks = head_masks()

    def windows(at, carry):
        for g in range(2):
            total = None
            for k in range(2):
                w = 2 * at + k
                q = qkv_ref[w, :, g * HALF : (g + 1) * HALF]
                key = qkv_ref[w, :, D + g * HALF : D + (g + 1) * HALF]
                val = qkv_ref[w, :, 2 * D + g * HALF : 2 * D + (g + 1) * HALF]
                grad = stack_halves(gat[w, :, g * HALF : (g + 1) * HALF])
                probs = p_ref[w, g]
                dprobs = mm_t(stack_heads(val, masks), grad).reshape(4, AROWS, 128)[:, :WROWS]
                p = probs.astype(F32).reshape(4, AROWS, 128)[:, :WROWS]
                delta = jnp.sum(p * dprobs, axis=1, keepdims=True)
                dscores = p * (dprobs - delta)
                total = dscores if total is None else total + dscores
                low = pad_keys(dscores)
                at_row = pl.ds(pl.multiple_of(w * WROWS, 8), WROWS)
                dqkv[at_row, g * HALF : (g + 1) * HALF] = (
                    pick_halves(t_mm(low, stack_heads(key, masks))) * SCALE
                )
                dqkv[at_row, D + g * HALF : D + (g + 1) * HALF] = (
                    pick_heads(mm(low, stack_halves(q))) * SCALE
                )
                dqkv[at_row, 2 * D + g * HALF : 2 * D + (g + 1) * HALF] = pick_heads(mm(probs, grad))
            acc_tab[g] += total
        return carry

    lax.fori_loop(0, 2 * PER_STEP, windows, 0)
    xhat, rstd = normalize(xw_ref[...])
    normed = (xhat * gain + shift).astype(BF16)
    grad_normed = None
    for part in range(3):
        cols = slice(part * D, (part + 1) * D)
        low = dqkv[:, cols].astype(BF16)
        dsmall_ref[:, 6 * D + part * D : 7 * D + part * D] += col_sum(low.astype(F32))
        acc_qkv[cols, :] += t_mm(low, normed)
        term = mm(low, w_qkv[cols, :])
        grad_normed = term if grad_normed is None else grad_normed + term
    dsmall_ref[:, :D] += col_sum(grad_normed * xhat)
    dsmall_ref[:, D : 2 * D] += col_sum(grad_normed)
    rows_to_grid(grad_mid + norm_back(grad_normed, xhat, rstd, gain), slots, dx_ref)
    if layer:
        last_strips(dx_ref, strips)

    @pl.when(step == pl.num_programs(0) - 1)
    def _():
        pack_attention(at_ref, acc_qkv, acc_proj, dpacks)
        for g in range(2):
            for a in range(4):
                dtab_ref[8 * g + a] = acc_tab[g, a, :, :AROWS]
                dtab_ref[8 * g + 4 + a] = acc_tab[g, a, :, AROWS:]


def mlp_forward_kernel(layer, at_ref, mid_ref, *refs):
    packs, refs = refs[:2], refs[2:]
    small_ref, y_ref, *strips, act_ref, slope_ref, slots, w_one, w_two = refs

    @pl.when(pl.program_id(0) == 0)
    def _():
        unpack_mlp(at_ref, packs, w_one, w_two)

    mid = mid_ref[...]
    xhat, _ = normalize(mid)
    gain = small_ref[layer : layer + 1, 2 * D : 3 * D]
    shift = small_ref[layer : layer + 1, 3 * D : 4 * D]
    normed = (xhat * gain + shift).astype(BF16)
    total = mid + small_ref[layer : layer + 1, 5 * D : 6 * D]
    for c in range(CHUNKS):
        bias = small_ref[layer : layer + 1, 9 * D + c * CHUNK : 9 * D + (c + 1) * CHUNK]
        act, slope = gelu_both(mm_t(normed, w_one[c * CHUNK : (c + 1) * CHUNK, :]) + bias)
        act = act.astype(BF16)
        act_ref[c] = act
        slope_ref[c] = slope.astype(BF16)
        total = total + mm_t(act, w_two[c])
    rows_to_grid(total, slots, y_ref)
    first_strips(y_ref, strips)


def mlp_backward_kernel(layer, forward, at_ref, mid_ref, dy_ref, *refs):
    strips, refs = refs[:3], refs[3:]
    if not forward:
        (act_ref, slope_ref), refs = refs[:2], refs[2:]
    packs, small_ref, refs = refs[:2], refs[2], refs[3:]
    if forward:
        (y_ref, *out_strips), refs = refs[:4], refs[4:]
    gm_ref, dpacks, refs = refs[0], refs[1:3], refs[3:]
    dsmall_ref, slots, w_one, w_two, acc_one, acc_two = refs
    step = pl.program_id(0)

    @pl.when(step == 0)
    def _():
        unpack_mlp(at_ref, packs, w_one, w_two)
        for ref in (dsmall_ref, acc_one, acc_two):
            ref[...] = jnp.zeros(ref.shape, ref.dtype)

    mid = mid_ref[...]
    xhat, rstd = normalize(mid)
    gain = small_ref[layer : layer + 1, 2 * D : 3 * D]
    shift = small_ref[layer : layer + 1, 3 * D : 4 * D]
    normed = (xhat * gain + shift).astype(BF16)
    dy = (next_to_rows if forward else prev_to_rows)(dy_ref, strips, slots)
    dy_low = dy.astype(BF16)
    dsmall_ref[:, 5 * D : 6 * D] += col_sum(dy_low.astype(F32))
    total = None
    if forward:
        total = mid + small_ref[layer : layer + 1, 5 * D : 6 * D]
    grad_normed = None
    for c in range(CHUNKS):
        if forward:
            bias = small_ref[layer : layer + 1, 9 * D + c * CHUNK : 9 * D + (c + 1) * CHUNK]
            act, slope = gelu_both(mm_t(normed, w_one[c * CHUNK : (c + 1) * CHUNK, :]) + bias)
            act = act.astype(BF16)
            total = total + mm_t(act, w_two[c])
        else:
            act = act_ref[c]
            slope = slope_ref[c].astype(F32)
        grad_pre = (mm(dy_low, w_two[c]) * slope).astype(BF16)
        dsmall_ref[:, 9 * D + c * CHUNK : 9 * D + (c + 1) * CHUNK] += col_sum(grad_pre.astype(F32))
        term = mm(grad_pre, w_one[c * CHUNK : (c + 1) * CHUNK, :])
        grad_normed = term if grad_normed is None else grad_normed + term
        acc_one[c * CHUNK : (c + 1) * CHUNK, :] += t_mm(grad_pre, normed)
        acc_two[c] += t_mm(dy_low, act)
    dsmall_ref[:, 2 * D : 3 * D] += col_sum(grad_normed * xhat)
    dsmall_ref[:, 3 * D : 4 * D] += col_sum(grad_normed)
    gm_ref[...] = dy + norm_back(grad_normed, xhat, rstd, gain)
    if forward:
        rows_to_grid(total, slots, y_ref)
        last_strips(y_ref, out_strips)

    @pl.when(step == pl.num_programs(0) - 1)
    def _():
        pack_mlp(at_ref, acc_one, acc_two, dpacks)


def fixed(shape):
    return pl.BlockSpec(shape, lambda s: (0,) * len(shape))


def stepped(shape, axis=0):
    return pl.BlockSpec(shape, lambda s: tuple(s if d == axis else 0 for d in range(len(shape))))


def call(kernel, steps, ins, in_specs, out_shapes, out_specs, scratch, flops, moved):
    return pl.pallas_call(
        kernel,
        grid=(steps,),
        in_specs=in_specs,
        out_shape=[jax.ShapeDtypeStruct(shape, kind) for shape, kind in out_shapes],
        out_specs=out_specs,
        scratch_shapes=scratch,
        compiler_params=pltpu.CompilerParams(
            dimension_semantics=("arbitrary",), vmem_limit_bytes=VMEM_LIMIT
        ),
        cost_estimate=pl.CostEstimate(flops=int(flops), bytes_accessed=int(moved), transcendentals=0),
    )(*ins)


STEP_WINDOWS = 4 * PER_STEP
STEP_ROWS = STEP_WINDOWS * WROWS
GRID_BLOCK = (PER_STEP, 2 * WIN, 2 * WIN, D)
SLOTS = pltpu.VMEM((STEP_WINDOWS, WIN, SLOT, D), F32)
KEPT = 2 * WIN - SHIFT
STRIPS = ((SHIFT, KEPT, D), (KEPT, SHIFT, D), (SHIFT, SHIFT, D))
STRIP_SPECS = [stepped((PER_STEP,) + shape) for shape in STRIPS]
SCALARS = pl.BlockSpec(memory_space=pltpu.SMEM)
PACK_A = (4, 4, N_QKV + N_OUT, HALF)
PACK_B = (4, 4, N_FC1 + 4 * N_OUT, HALF)


def pack_specs(packs, shape):
    whole = packs[0].shape[2]
    at = 0 if shape == PACK_B else whole // shape[2] - 1
    return [pl.BlockSpec(shape, lambda s: (0, 0, at, 0))] * 2


ROW_SUMS = 9 * D + MLP


def strip_shapes(images):
    return [((images,) + shape, BF16) for shape in STRIPS]


def attention_forward(layer, at, grid_field, strips, packs, small, base):
    images = grid_field.shape[0]
    rows = images * 4 * WROWS
    return call(
        partial(attention_forward_kernel, layer),
        images // PER_STEP,
        (at, grid_field, *strips, *packs, small, base),
        [SCALARS, stepped(GRID_BLOCK)]
        + STRIP_SPECS[: len(strips)]
        + pack_specs(packs, PACK_A)
        + [fixed(small.shape), fixed(base.shape)],
        [
            ((rows, D), F32),
            ((images * 4, AROWS, 3 * D), BF16),
            ((images * 4, 2, 4 * AROWS, 128), BF16),
            ((rows, D), BF16),
            ((rows, D), F32),
        ],
        [
            stepped((STEP_ROWS, D)),
            stepped((STEP_WINDOWS, AROWS, 3 * D)),
            stepped((STEP_WINDOWS, 2, 4 * AROWS, 128)),
            stepped((STEP_ROWS, D)),
            stepped((STEP_ROWS, D)),
        ],
        [
            SLOTS,
            pltpu.VMEM((3 * D, D), BF16),
            pltpu.VMEM((D, D), BF16),
            pltpu.VMEM((STEP_ROWS, D), F32),
            pltpu.VMEM((4 if layer else 1, 2, 4, WROWS, 2 * AROWS), F32),
        ],
        2 * rows * 4 * D * D * 2,
        30e6,
    )


def attention_backward(layer, at, grad_mid, saved, packs, small, rest):
    rows = grad_mid.shape[0]
    images = rows // (4 * WROWS)
    out = call(
        partial(attention_backward_kernel, layer),
        images // PER_STEP,
        (at, grad_mid, *saved, *packs, small, rest),
        [
            SCALARS,
            stepped((STEP_ROWS, D)),
            stepped((STEP_ROWS, D)),
            stepped((STEP_WINDOWS, AROWS, 3 * D)),
            stepped((STEP_WINDOWS, 2, 4 * AROWS, 128)),
            stepped((STEP_ROWS, D)),
        ]
        + pack_specs(packs, PACK_A)
        + [fixed(small.shape), fixed(rest.shape)],
        [((images, 2 * WIN, 2 * WIN, D), F32)]
        + strip_shapes(images)[: 3 * layer]
        + [(PACK_A, BF16)] * 2
        + [((HEADS, WROWS, AROWS), F32), ((1, ROW_SUMS), F32)],
        [stepped(GRID_BLOCK)]
        + STRIP_SPECS[: 3 * layer]
        + [fixed(PACK_A)] * 2
        + [fixed((HEADS, WROWS, AROWS)), fixed((1, ROW_SUMS))],
        [
            SLOTS,
            pltpu.VMEM((3 * D, D), BF16),
            pltpu.VMEM((D, D), BF16),
            pltpu.VMEM((STEP_WINDOWS, AROWS, D), BF16),
            pltpu.VMEM((STEP_ROWS, 3 * D), F32),
            pltpu.VMEM((3 * D, D), F32),
            pltpu.VMEM((D, D), F32),
            pltpu.VMEM((2, 4, WROWS, 2 * AROWS), F32),
        ],
        2 * rows * 4 * D * D * 5,
        30e6,
    )
    at_pack = 1 + 3 * layer
    return out[0], out[1:at_pack], out[at_pack : at_pack + 2], out[-2], out[-1]


MLP_SCRATCH = [SLOTS, pltpu.VMEM((MLP, D), BF16), pltpu.VMEM((CHUNKS, D, CHUNK), BF16)]


def mlp_forward(layer, at, mid, packs, small):
    rows = mid.shape[0]
    images = rows // (4 * WROWS)
    out = call(
        partial(mlp_forward_kernel, layer),
        images // PER_STEP,
        (at, mid, *packs, small),
        [SCALARS, stepped((STEP_ROWS, D))] + pack_specs(packs, PACK_B) + [fixed(small.shape)],
        [((images, 2 * WIN, 2 * WIN, D), F32)]
        + strip_shapes(images)
        + [((CHUNKS, rows, CHUNK), BF16)] * 2,
        [stepped(GRID_BLOCK)] + STRIP_SPECS + [stepped((CHUNKS, STEP_ROWS, CHUNK), 1)] * 2,
        MLP_SCRATCH,
        2 * rows * 2 * D * MLP,
        26e6,
    )
    return out[0], out[1:4], out[4:]


def mlp_backward(layer, at, mid, dy, strips, saved, packs, small):
    rows = mid.shape[0]
    images = rows // (4 * WROWS)
    forward = not saved
    extra = 4 if forward else 0
    out = call(
        partial(mlp_backward_kernel, layer, forward),
        images // PER_STEP,
        (at, mid, dy, *strips, *saved, *packs, small),
        [SCALARS, stepped((STEP_ROWS, D)), stepped(GRID_BLOCK)]
        + STRIP_SPECS
        + [stepped((CHUNKS, STEP_ROWS, CHUNK), 1)] * len(saved)
        + pack_specs(packs, PACK_B)
        + [fixed(small.shape)],
        ([((images, 2 * WIN, 2 * WIN, D), F32)] + strip_shapes(images))[:extra]
        + [((rows, D), F32)]
        + [(PACK_B, BF16)] * 2
        + [((1, ROW_SUMS), F32)],
        ([stepped(GRID_BLOCK)] + STRIP_SPECS)[:extra]
        + [stepped((STEP_ROWS, D))]
        + [fixed(PACK_B)] * 2
        + [fixed((1, ROW_SUMS))],
        MLP_SCRATCH + [pltpu.VMEM((MLP, D), F32), pltpu.VMEM((CHUNKS, D, CHUNK), F32)],
        2 * rows * (6 if forward else 4) * D * MLP,
        30e6,
    )
    return out[:extra], out[extra], out[extra + 1 : extra + 3], out[-1]


def moved(x, step_of):
    sizes = [lax.axis_size(axis) for axis in AXES]

    def flat(i, r, c):
        return (i * sizes[1] + r) * sizes[2] + c

    pairs = [
        (flat(i, r, c), flat(*step_of(i, r, c)))
        for i in range(sizes[0])
        for r in range(sizes[1])
        for c in range(sizes[2])
    ]
    return lax.ppermute(x, AXES, pairs)


def swapped(x, img=0, down=0, core=0, across=0):
    return moved(x, lambda i, r, c: (i ^ img, r ^ (2 * down + core), c ^ across))


def send_strips(strips, by):
    rows, cols = lax.axis_size("row"), lax.axis_size("col")
    low, right, corner = strips
    return (
        moved(low, lambda i, r, c: (i, (r + by) % rows, c)),
        moved(right, lambda i, r, c: (i, r, (c + by) % cols)),
        moved(corner, lambda i, r, c: (i, (r + by) % rows, (c + by) % cols)),
    )


def join_prev(grid_field, strips):
    high, left, corner = (strip.astype(F32) for strip in strips)
    top = jnp.concatenate([corner, high], axis=2)
    rest = jnp.concatenate([left, grid_field[:, :KEPT, :KEPT]], axis=2)
    return jnp.concatenate([top, rest], axis=1)


QUADS = ((0, 0), (0, 1), (1, 0), (1, 1))


def after(values, *others):
    return lax.optimization_barrier((values, others))[0]


def together(*values):
    return lax.optimization_barrier(values)


def is_small():
    return lax.axis_size("img") == 2


def gather_line(pack):
    if not is_small():
        return pack
    return jnp.stack([pack] + [swapped(pack, across=m) for m in (1, 2, 3)])


def gather_near(pack):
    return jnp.stack([pack, swapped(pack, across=1)]) if is_small() else pack


def gather_far(pack):
    return jnp.concatenate([pack, swapped(pack, across=2)]) if is_small() else pack


def gather_quad(line):
    if not is_small():
        return line
    return jnp.stack([line] + [swapped(line, img=i, down=y) for i, y in QUADS[1:]])


def gather_pair(quad, canonical):
    if is_small():
        return quad, swapped(quad, core=1)
    whole = lax.all_gather(quad, AXES, axis=0, tiled=False)
    whole = canonical(whole.reshape((lax.axis_size("img"), 16) + quad.shape))
    whole = whole.reshape((2, 2, 2, 4) + whole.shape[2:]).transpose(2, 0, 1, 3, 4, 5)
    whole = whole.reshape((2, 4, 4) + whole.shape[4:])
    return whole[0], whole[1]


def scatter_pair(packs):
    if not is_small():
        return packs
    keep, send = packs
    half = keep.astype(F32) + swapped(send, core=1).astype(F32)
    return [half[0]] + [half[m].astype(BF16) for m in (1, 2, 3)]


def quad_swaps(halves):
    if not is_small():
        return []
    return [swapped(h, img=i, down=y) for h, (i, y) in zip(halves[1:], QUADS[1:])]


def scatter_quad(halves, got):
    if not is_small():
        return halves
    got = [g.astype(F32) for g in got]
    line = (halves[0] + got[0]) + (got[1] + got[2])
    return line[:2], line[2:].astype(BF16)


def scatter_far(line):
    if not is_small():
        return line
    keep, send = line
    ends = keep + swapped(send, across=2).astype(F32)
    return ends[0], ends[1].astype(BF16)


def scatter_near(ends, in_shards):
    if is_small():
        keep, send = ends
        return keep + swapped(send, across=1).astype(F32)
    whole = jnp.stack(ends).reshape((2, 2, 2) + ends[0].shape[1:]).transpose(1, 2, 0, 3, 4, 5)
    size = lax.axis_size("img")
    whole = in_shards(whole.reshape((2, 16) + ends[0].shape[2:]), size)
    flat = whole.reshape(-1, whole.shape[-1])
    return lax.psum_scatter(flat, AXES, scatter_dimension=0, tiled=True).astype(F32)


def sum_swaps(x):
    if not is_small():
        return lax.psum(x, AXES)
    for step in ({"core": 1}, {"img": 1}, {"down": 1}, {"across": 2}, {"across": 1}):
        x = x + swapped(x, **step)
    return x


def padded_index(rel_index):
    cells = rel_index.T.reshape(WIN, WIN, WIN, WIN)
    gap = (0, SLOT - WIN)
    cells = jnp.pad(cells, [(0, 0), gap, (0, AROWS // SLOT - WIN), gap], constant_values=-1)
    return cells.reshape(1, WROWS * AROWS)


def attention_pack(w_qkv, w_proj):
    return jnp.concatenate([w_qkv.astype(BF16).T, w_proj.astype(BF16).T], axis=0)


def mlp_pack(w_fc1, w_fc2):
    cols = w_fc1.shape[0]
    second = w_fc2.astype(BF16).T
    second = second.reshape(second.shape[0], 4, cols).transpose(1, 0, 2).reshape(-1, cols)
    return jnp.concatenate([w_fc1.astype(BF16).T, second], axis=0)


def attention_canonical(whole):
    _, ranks, rows, _ = whole.shape
    whole = whole.transpose(1, 2, 0, 3).reshape(ranks, rows, 2, HALF)
    return whole.transpose(2, 0, 1, 3)


def both_canonical(whole):
    rows = N_FC1 + 4 * N_OUT
    return jnp.concatenate(
        [mlp_canonical(whole[:, :, :rows]), attention_canonical(whole[:, :, rows:])], axis=2
    )


def attention_shards(pack, size):
    _, ranks, rows, _ = pack.shape
    pack = pack.transpose(1, 2, 0, 3).reshape(ranks, rows, size, D // size)
    return pack.transpose(2, 0, 1, 3)


def mlp_canonical(whole):
    size, ranks, _, cols = whole.shape
    first = attention_canonical(whole[:, :, :N_FC1])
    second = whole[:, :, N_FC1:].reshape(size, ranks, 4, N_OUT, cols)
    second = second.transpose(1, 3, 0, 2, 4).reshape(ranks, N_OUT, 2, 4, HALF)
    second = second.transpose(2, 0, 3, 1, 4).reshape(2, ranks, 4 * N_OUT, HALF)
    return jnp.concatenate([first, second], axis=2)


def mlp_shards(pack, size):
    _, ranks, _, _ = pack.shape
    cols = D // size
    first = attention_shards(pack[:, :, :N_FC1], size)
    second = pack[:, :, N_FC1:].reshape(2, ranks, 4, N_OUT, HALF)
    second = second.transpose(1, 3, 0, 2, 4).reshape(ranks, N_OUT, size, 4, cols)
    second = second.transpose(2, 0, 3, 1, 4).reshape(size, ranks, 4 * N_OUT, cols)
    return jnp.concatenate([first, second], axis=2)


def adam_step(weight, moment_one, second, gradient, rate_value, decay_rate):
    moment_one = BETA_ONE * moment_one + (1.0 - BETA_ONE) * gradient
    second = BETA_TWO * second + (1.0 - BETA_TWO) * gradient * gradient
    update = (
        moment_one / (1.0 - BETA_ONE**STEP) / (jnp.sqrt(second / (1.0 - BETA_TWO**STEP)) + EPS_ADAM)
    )
    return (weight - rate_value * (update + decay_rate * weight), moment_one, second)


def shards(
    images,
    grad_out,
    w_qkv,
    w_proj,
    w_fc1,
    w_fc2,
    first_qkv,
    first_proj,
    first_fc1,
    first_fc2,
    second_qkv,
    second_proj,
    second_fc1,
    second_fc2,
    small_params,
    small_first,
    small_second,
    rel_index,
):
    size = lax.axis_size("img")
    row, col = lax.axis_index("row"), lax.axis_index("col")
    last = [row == lax.axis_size("row") - 1, col == lax.axis_size("col") - 1]
    if size == 2:
        place = [lax.axis_index("img"), row // 2, row % 2, col]
    else:
        place = [jnp.int32(0)] * 4
    at = jnp.stack([jnp.asarray(value, jnp.int32) for value in place + last])

    attention_packs = [attention_pack(w_qkv[l], w_proj[l]) for l in range(2)]
    mlp_packs = [mlp_pack(w_fc1[l], w_fc2[l]) for l in range(2)]
    mixed = jnp.concatenate([mlp_packs[0], attention_packs[1]], axis=0)
    line_a, mixed, last_pack = together(
        gather_line(attention_packs[0]), gather_near(mixed), gather_near(mlp_packs[1])
    )
    quad_a, mixed = together(gather_quad(line_a), gather_far(mixed))
    packs_a = gather_pair(quad_a, attention_canonical)

    onehot = (
        jnp.arange(RELPOS, dtype=jnp.int32)[:, None] == padded_index(rel_index)
    ).astype(F32)
    tables = small_params[:, 9 * D + MLP :].reshape(2, RELPOS, HEADS)
    base = jnp.einsum("lrh,rp->lhp", tables * LOG2E, onehot, precision=lax.Precision.HIGHEST)
    base = base.reshape(2, HEADS, WROWS, AROWS)
    grad_strips = (
        grad_out[:, :SHIFT, SHIFT:].astype(BF16),
        grad_out[:, SHIFT:, :SHIFT].astype(BF16),
        grad_out[:, :SHIFT, :SHIFT].astype(BF16),
    )

    def table_row(sums, dtab):
        table = jnp.einsum(
            "hp,rp->rh", dtab.reshape(HEADS, -1), onehot, precision=lax.Precision.HIGHEST
        )
        return jnp.concatenate([sums, table.reshape(1, -1)], axis=1)

    packs_a = after(packs_a, base, grad_strips)
    *saved_zero, mid_zero = attention_forward(0, at, images, (), packs_a, small_params, base[0])
    mixed, last_pack = together(gather_quad(mixed), gather_far(last_pack))
    packs_mixed = gather_pair(after(mixed, mid_zero), both_canonical)
    last_pack = after(last_pack, packs_mixed)
    out_zero, strips, hidden_zero = mlp_forward(0, at, mid_zero, packs_mixed, small_params)
    last_pack, strips = together(gather_quad(last_pack), strips)
    packs_last = gather_pair(last_pack, mlp_canonical)
    strips, packs_last = together(send_strips(strips, -1), packs_last)
    *saved_one, mid_one = attention_forward(
        1, at, out_zero, strips, packs_mixed, small_params, base[1]
    )
    grad_strips = send_strips(after(grad_strips, strips), -1)
    (out_one, *out_strips), gm_one, dpacks, rest = mlp_backward(
        1, at, mid_one, grad_out, grad_strips, (), packs_last, small_params
    )

    halves_b_one, out_strips, gm_one = together(
        scatter_pair(dpacks), send_strips(out_strips, 1), gm_one
    )
    dx_one, strips, dpacks, dtab_one, sums = attention_backward(
        1, at, gm_one, saved_one, packs_mixed, small_params, rest
    )
    strips, dpacks, got = together(strips, dpacks, quad_swaps(halves_b_one))
    line_b_one = scatter_quad(halves_b_one, got)
    halves_a_one = scatter_pair(dpacks)
    outputs = join_prev(out_one, out_strips)
    strips, halves_a_one, line_b_one, outputs = together(
        send_strips(strips, 1), halves_a_one, line_b_one, outputs
    )
    _, gm_zero, dpacks, rest = mlp_backward(
        0, at, mid_zero, dx_one, strips, hidden_zero, packs_mixed, small_params
    )

    dpacks, got, ends_b_one = together(dpacks, quad_swaps(halves_a_one), scatter_far(line_b_one))
    halves_b_zero = scatter_pair(dpacks)
    line_a_one = scatter_quad(halves_a_one, got)
    row_one = table_row(sums, dtab_one)
    gm_zero, halves_b_zero, ends_b_one, line_a_one, row_one = together(
        gm_zero, halves_b_zero, ends_b_one, line_a_one, row_one
    )
    grad_input, _, dpacks, dtab_zero, sums = attention_backward(
        0, at, gm_zero, saved_zero, packs_a, small_params, rest
    )

    dpacks, got, ends_a_one, sum_b_one = together(
        dpacks, quad_swaps(halves_b_zero), scatter_far(line_a_one), scatter_near(ends_b_one, mlp_shards)
    )
    halves_a_zero = scatter_pair(dpacks)
    line_b_zero = scatter_quad(halves_b_zero, got)
    ends_b_zero = scatter_far(line_b_zero)
    sum_a_one = scatter_near(ends_a_one, attention_shards)
    ends_a_zero = scatter_far(scatter_quad(halves_a_zero, quad_swaps(halves_a_zero)))
    sum_b_zero = scatter_near(ends_b_zero, mlp_shards)
    sum_a_zero = scatter_near(ends_a_zero, attention_shards)
    sums_b = [sum_b_zero, sum_b_one]
    sums_a = [sum_a_zero, sum_a_one]
    small_grad = sum_swaps(jnp.concatenate([table_row(sums, dtab_zero), row_one], axis=0))

    cols = D // size
    grads = (
        jnp.stack([s[:N_QKV].T for s in sums_a]),
        jnp.stack([s[N_QKV:].T for s in sums_a]),
        jnp.stack([s[:N_FC1].T for s in sums_b]),
        jnp.stack(
            [s[N_FC1:].reshape(4, N_OUT, cols).transpose(0, 2, 1).reshape(4 * cols, N_OUT) for s in sums_b]
        ),
    )

    masters = (w_qkv, w_proj, w_fc1, w_fc2)
    firsts = (first_qkv, first_proj, first_fc1, first_fc2)
    seconds = (second_qkv, second_proj, second_fc1, second_fc2)
    updated = [
        adam_step(masters[k], firsts[k], seconds[k], grads[k], RATE_MATRIX, DECAY_MATRIX)
        for k in range(4)
    ]
    small_new = adam_step(small_params, small_first, small_second, small_grad, RATE_SMALL, 0.0)
    return (
        (outputs, grad_input)
        + tuple(new[0] for new in updated)
        + tuple(new[1] for new in updated)
        + tuple(new[2] for new in updated)
        + tuple(small_new)
    )


def solution(mesh):
    grid_spec = P("img", "row", "col", None)
    matrix = P(None, "img", ("row", "col"))
    in_specs = (grid_spec,) * 2 + (matrix,) * 12 + (P(),) * 4
    out_specs = (grid_spec,) * 2 + (matrix,) * 12 + (P(),) * 3
    return jax.shard_map(shards, mesh=mesh, in_specs=in_specs, out_specs=out_specs, check_vma=False)
```

```python
from functools import partial

import jax
import jax.numpy as jnp
from jax import lax
from jax.experimental import pallas as pl
from jax.experimental.pallas import tpu as pltpu
from jax.sharding import PartitionSpec as P

D = 512
HEADS = 16
HEAD_DIM = 32
MLP = 2048
WIN = 7
SHIFT = 3
STEP = 10
RELPOS = 169

EPS_NORM = 1e-05
BETA_ONE = 0.9
BETA_TWO = 0.999
EPS_ADAM = 1e-08
RATE_MATRIX = 0.05
RATE_SMALL = 0.3
DECAY_MATRIX = 0.05
MASKED = -1e30

AXES = ("img", "row", "col")
F32 = jnp.float32
BF16 = jnp.bfloat16
LOG2E = 1.4426950408889634
SCALE = HEAD_DIM ** (-0.5)

SIDE = 2 * WIN
IMAGES = 8
SLOT = 8
WROWS = WIN * SLOT
AROWS = 64
STEPS = 2
STEP_ROWS = WIN * SIDE * IMAGES
ROWS = STEPS * STEP_ROWS
STEP_WINDOWS = 2 * IMAGES
KEPT = SIDE - SHIFT
CHUNK = 512
CHUNKS = MLP // CHUNK
HALF = D // 2
LANES = 128
VMEM_LIMIT = 60 * 1024 * 1024


def mm(left, right):
    return lax.dot_general(left, right, (((1,), (0,)), ((), ())), preferred_element_type=F32)


def mm_t(left, right):
    return lax.dot_general(left, right, (((1,), (1,)), ((), ())), preferred_element_type=F32)


def t_mm(left, right):
    return lax.dot_general(left, right, (((0,), (0,)), ((), ())), preferred_element_type=F32)


def col_sum(value):
    return jnp.sum(value, axis=0, keepdims=True)


def normalize(rows):
    center = rows - jnp.mean(rows, axis=-1, keepdims=True)
    spread = jnp.mean(center * center, axis=-1, keepdims=True)
    rstd = lax.rsqrt(spread + EPS_NORM)
    return center * rstd, rstd


def norm_back(grad, xhat, rstd, gain):
    scaled = grad * gain
    mean_one = jnp.mean(scaled, axis=-1, keepdims=True)
    mean_two = jnp.mean(scaled * xhat, axis=-1, keepdims=True)
    return rstd * (scaled - mean_one - xhat * mean_two)


def gelu_both(pre):
    size = jnp.abs(pre)
    t = 1.0 / (1.0 + size * (0.3275911 * 0.7071067811865476))
    bell = jnp.exp2(pre * pre * (-0.5 * LOG2E))
    poly = 0.5 * 1.061405429
    poly = poly * t + 0.5 * -1.453152027
    poly = poly * t + 0.5 * 1.421413741
    poly = poly * t + 0.5 * -0.284496736
    poly = poly * t + 0.5 * 0.254829592
    tail = poly * t * bell
    cdf = jnp.where(pre >= 0.0, 1.0 - tail, tail)
    return pre * cdf, cdf + pre * bell * 0.3989422804014327


def both_steps(body):
    for a in range(STEPS):
        pl.when(pl.program_id(0) == a)(partial(body, a))


def next_rows(grid_ref, strip_refs, rows_ref):
    low_ref, right_ref, corner_ref = strip_refs

    def body(a):
        if a == 0:
            rows_ref[:, :KEPT] = grid_ref[SHIFT : SHIFT + WIN, SHIFT:]
            rows_ref[:, KEPT:] = right_ref[:WIN].astype(F32)
        else:
            rows_ref[: WIN - SHIFT, :KEPT] = grid_ref[SHIFT + WIN :, SHIFT:]
            rows_ref[: WIN - SHIFT, KEPT:] = right_ref[WIN:].astype(F32)
            rows_ref[WIN - SHIFT :, :KEPT] = low_ref[...].astype(F32)
            rows_ref[WIN - SHIFT :, KEPT:] = corner_ref[...].astype(F32)

    both_steps(body)
    return rows_ref[...].reshape(STEP_ROWS, D)


def prev_rows(grid_ref, strip_refs, rows_ref):
    high_ref, left_ref, corner_ref = strip_refs

    def body(a):
        if a == 0:
            rows_ref[:SHIFT, SHIFT:] = high_ref[...].astype(F32)
            rows_ref[:SHIFT, :SHIFT] = corner_ref[...].astype(F32)
            rows_ref[SHIFT:, SHIFT:] = grid_ref[: WIN - SHIFT, :KEPT]
            rows_ref[SHIFT:, :SHIFT] = left_ref[: WIN - SHIFT].astype(F32)
        else:
            rows_ref[:, SHIFT:] = grid_ref[WIN - SHIFT : KEPT, :KEPT]
            rows_ref[:, :SHIFT] = left_ref[WIN - SHIFT :].astype(F32)

    both_steps(body)
    return rows_ref[...].reshape(STEP_ROWS, D)


def first_strips(block_ref, strip_refs):
    rows_ref, cols_ref, corner_ref = strip_refs

    def body(a):
        if a == 0:
            rows_ref[...] = block_ref[:SHIFT, SHIFT:].astype(BF16)
            cols_ref[: WIN - SHIFT] = block_ref[SHIFT:, :SHIFT].astype(BF16)
            corner_ref[...] = block_ref[:SHIFT, :SHIFT].astype(BF16)
        else:
            cols_ref[WIN - SHIFT :] = block_ref[:, :SHIFT].astype(BF16)

    both_steps(body)


def last_strips(block_ref, strip_refs):
    rows_ref, cols_ref, corner_ref = strip_refs

    def body(a):
        if a == 0:
            cols_ref[:WIN] = block_ref[:, KEPT:].astype(BF16)
        else:
            cols_ref[WIN:] = block_ref[: WIN - SHIFT, KEPT:].astype(BF16)
            rows_ref[...] = block_ref[WIN - SHIFT :, :KEPT].astype(BF16)
            corner_ref[...] = block_ref[WIN - SHIFT :, KEPT:].astype(BF16)

    both_steps(body)


def put_tiles(tiles, first, value):
    for t in range(value.shape[1] // LANES):
        tiles[first + t, :STEP_ROWS, :] = value[:, t * LANES : (t + 1) * LANES]


def get_tiles(tiles, first, count):
    return jnp.concatenate([tiles[first + t, :STEP_ROWS, :] for t in range(count)], axis=1)


def clear_tail(tiles):
    tiles[:, STEP_ROWS:, :] = jnp.zeros(tiles[:, STEP_ROWS:, :].shape, F32)


def window_at(b, n, r):
    return b * WIN * IMAGES + r * SIDE * IMAGES + n


def get_window(tiles, first, b, n):
    return jnp.concatenate(
        [
            jnp.concatenate(
                [
                    tiles[first + t, pl.ds(window_at(b, n, r), SLOT, stride=IMAGES), :]
                    for r in range(WIN)
                ],
                axis=0,
            )
            for t in range(2)
        ],
        axis=1,
    )


def put_window(tiles, first, b, n, value):
    for t in range(2):
        for r in range(WIN):
            tiles[first + t, pl.ds(window_at(b, n, r), WIN, stride=IMAGES), :] = value[
                r * SLOT : r * SLOT + WIN, t * LANES : (t + 1) * LANES
            ]


def to_sixty_four(window):
    padding = jnp.zeros((AROWS - WROWS, window.shape[1]), F32)
    return jnp.concatenate([window, padding], axis=0).astype(BF16)


def head_masks():
    lane = lax.broadcasted_iota(jnp.int32, (16, HALF), 1)
    head = jnp.bitwise_and(lax.shift_right_logical(lane, 5), 3)
    return [jnp.where(head == a, 1.0, 0.0).astype(BF16) for a in range(4)]


def stack_heads(part, masks):
    split = part.reshape(AROWS // 16, 16, HALF)
    return jnp.concatenate(
        [(split * mask[None]).reshape(AROWS, HALF) for mask in masks], axis=0
    )


def stack_halves(part):
    zero = jnp.zeros((AROWS, HALF // 2), part.dtype)
    return jnp.concatenate(
        [
            jnp.concatenate([part[:, : HALF // 2], zero], axis=1),
            jnp.concatenate([zero, part[:, HALF // 2 :]], axis=1),
        ],
        axis=0,
    )


def pick_halves(result):
    return jnp.concatenate(
        [result[:WROWS, : HALF // 2], result[AROWS : AROWS + WROWS, HALF // 2 :]], axis=1
    )


def pick_heads(result):
    lane = lax.broadcasted_iota(jnp.int32, (WROWS, HALF), 1)
    head = jnp.bitwise_and(lax.shift_right_logical(lane, 5), 3)
    picked = result[3 * AROWS : 3 * AROWS + WROWS]
    for a in (2, 1, 0):
        picked = jnp.where(head == a, result[a * AROWS : a * AROWS + WROWS], picked)
    return picked


def pad_keys(value):
    padding = jnp.zeros((4, AROWS - WROWS, 128), F32)
    return jnp.concatenate([value, padding], axis=1).astype(BF16).reshape(4 * AROWS, 128)


def places(at_ref, packs):
    if len(packs) == 1:
        for shard in range(packs[0].shape[0]):
            yield 0, (shard,), shard // 16, shard % 16
        return
    for core in range(2):
        for quad in range(4):
            for across in range(4):
                i = jnp.bitwise_xor(at_ref[0], quad >> 1)
                y = jnp.bitwise_xor(at_ref[1], quad & 1)
                c = jnp.bitwise_xor(at_ref[2], core)
                z = jnp.bitwise_xor(at_ref[3], across)
                yield core, (quad, across), i, (2 * y + c) * 4 + z


def piece(start, length):
    if isinstance(start, int):
        return pl.ds(start * length, length)
    return pl.ds(pl.multiple_of(start * length, length), length)


N_QKV = 3 * D // 16
N_OUT = D // 16
N_FC1 = MLP // 16


def unpack_attention(at_ref, packs, w_qkv, w_proj):
    for core, at, i, r in places(at_ref, packs):
        cols = piece(i, HALF)
        w_qkv[piece(r, N_QKV), cols] = packs[core][at + (slice(0, N_QKV),)]
        w_proj[piece(r, N_OUT), cols] = packs[core][at + (slice(N_QKV, None),)]


def pack_attention(at_ref, g_qkv, g_proj, packs):
    for core, at, i, r in places(at_ref, packs):
        cols = piece(i, HALF)
        packs[core][at + (slice(0, N_QKV),)] = g_qkv[piece(r, N_QKV), cols].astype(BF16)
        packs[core][at + (slice(N_QKV, None),)] = g_proj[piece(r, N_OUT), cols].astype(BF16)


def unpack_mlp(at_ref, packs, w_one, w_two):
    for core, at, i, r in places(at_ref, packs):
        w_one[piece(r, N_FC1), piece(i, HALF)] = packs[core][at + (slice(0, N_FC1),)]
        for k in range(4):
            w_two[2 * i + k // 2, piece(r, N_OUT), (k % 2) * HALF : (k % 2 + 1) * HALF] = packs[core][
                at + (slice(N_FC1 + k * N_OUT, N_FC1 + (k + 1) * N_OUT),)
            ]


def pack_mlp(at_ref, g_one, g_two, packs):
    for core, at, i, r in places(at_ref, packs):
        packs[core][at + (slice(0, N_FC1),)] = g_one[piece(r, N_FC1), piece(i, HALF)].astype(BF16)
        for k in range(4):
            packs[core][at + (slice(N_FC1 + k * N_OUT, N_FC1 + (k + 1) * N_OUT),)] = g_two[
                2 * i + k // 2, piece(r, N_OUT), (k % 2) * HALF : (k % 2 + 1) * HALF
            ].astype(BF16)


def spread_bias(layer, at_ref, base_ref, bias):
    row = lax.broadcasted_iota(jnp.int32, (WROWS, 2 * AROWS), 0)
    lane = jnp.bitwise_and(lax.broadcasted_iota(jnp.int32, (WROWS, 2 * AROWS), 1), AROWS - 1)
    key_row, key_col = row // SLOT, jnp.bitwise_and(row, SLOT - 1)
    query_row, query_col = lane // SLOT, jnp.bitwise_and(lane, SLOT - 1)
    kept = WIN - SHIFT
    other_row = ((key_row >= kept) != (query_row >= kept)).astype(jnp.int32)
    other_col = ((key_col >= kept) != (query_col >= kept)).astype(jnp.int32)
    padding = (key_col == WIN).astype(jnp.int32)
    for v in range(bias.shape[0]):
        hidden = padding
        if layer == 1:
            if v >> 1:
                hidden = hidden + other_row * at_ref[4]
            if v & 1:
                hidden = hidden + other_col * at_ref[5]
        for g in range(2):
            for a in range(4):
                both = jnp.concatenate([base_ref[8 * g + a], base_ref[8 * g + 4 + a]], axis=1)
                bias[v, g, a] = jnp.where(hidden > 0, MASKED, both)


def attention_forward_kernel(layer, n_packs, at_ref, x_ref, *refs):
    strips, refs = refs[: 3 * layer], refs[3 * layer :]
    packs, refs = refs[:n_packs], refs[n_packs:]
    small_ref, base_ref, refs = refs[0], refs[1], refs[2:]
    if layer:
        xs_ref, refs = refs[0], refs[1:]
    qkv_ref, p_ref, att_ref, mid_ref, w_qkv, w_proj, tiles, att_tiles, bias_ref, *moved = refs
    step = pl.program_id(0)

    @pl.when(step == 0)
    def _():
        unpack_attention(at_ref, packs, w_qkv, w_proj)
        spread_bias(layer, at_ref, base_ref, bias_ref)
        clear_tail(tiles)

    gain = small_ref[layer : layer + 1, 0:D]
    shift = small_ref[layer : layer + 1, D : 2 * D]
    if layer:
        rows = next_rows(x_ref, strips, moved[0])
        xs_ref[...] = rows
    else:
        rows = x_ref[...].reshape(STEP_ROWS, D)
    xhat, _ = normalize(rows)
    normed = (xhat * gain + shift).astype(BF16)
    for part in range(3):
        cols = slice(part * D, (part + 1) * D)
        bias = small_ref[layer : layer + 1, 6 * D + part * D : 7 * D + part * D]
        put_tiles(tiles, 4 * part, mm_t(normed, w_qkv[cols, :]) + bias)
    masks = head_masks()
    lane = jnp.bitwise_and(lax.broadcasted_iota(jnp.int32, (4, 1, LANES), 2), AROWS - 1)
    no_query = (jnp.bitwise_and(lane, SLOT - 1) == WIN) | (lane >= WROWS)

    def windows(n, carry):
        places_of = [(b, g) for b in range(2) for g in range(2)]
        scores, values = [], []
        for b, g in places_of:
            q, key, val = (
                to_sixty_four(get_window(tiles, 4 * part + 2 * g, b, n)) for part in range(3)
            )
            for part, value in enumerate((q, key, val)):
                at = part * D + g * HALF
                qkv_ref[b * IMAGES + n, :, at : at + HALF] = value
            scores.append(mm_t(stack_heads(key, masks), stack_halves(q)))
            values.append(val)
        probs = []
        for (b, g), score in zip(places_of, scores):
            v = 2 * step + b if layer else 0
            score = score.reshape(4, AROWS, LANES)[:, :WROWS] * (SCALE * LOG2E) + bias_ref[v, g]
            powers = jnp.exp2(score - jnp.max(score, axis=1, keepdims=True))
            total = jnp.sum(powers, axis=1, keepdims=True)
            prob = pad_keys(powers * jnp.where(no_query, 0.0, 1.0 / total))
            p_ref[b * IMAGES + n, g] = prob
            probs.append(prob)
        for (b, g), prob, val in zip(places_of, probs, values):
            put_window(att_tiles, 2 * g, b, n, pick_halves(t_mm(prob, stack_heads(val, masks))))
        return carry

    lax.fori_loop(0, IMAGES, windows, 0)
    att = get_tiles(att_tiles, 0, 4).astype(BF16)
    att_ref[...] = att
    bias = small_ref[layer : layer + 1, 4 * D : 5 * D]
    mid_ref[...] = rows + (mm_t(att, w_proj[...]) + bias)


def attention_backward_kernel(layer, n_packs, n_out, at_ref, gm_ref, x_ref, qkv_ref, p_ref, att_ref, *refs):
    packs, refs = refs[:n_packs], refs[n_packs:]
    small_ref, rest_ref, dx_ref, refs = refs[0], refs[1], refs[2], refs[3:]
    strips, refs = refs[: 3 * layer], refs[3 * layer :]
    dpacks, refs = refs[:n_out], refs[n_out:]
    dtab_ref, dsmall_ref, w_qkv, w_proj, g_tiles, d_tiles, acc_qkv, acc_proj, acc_tab = refs
    step = pl.program_id(0)

    @pl.when(step == 0)
    def _():
        unpack_attention(at_ref, packs, w_qkv, w_proj)
        dsmall_ref[...] = rest_ref[...]
        clear_tail(g_tiles)
        for ref in (acc_tab, acc_qkv, acc_proj):
            ref[...] = jnp.zeros(ref.shape, ref.dtype)

    gain = small_ref[layer : layer + 1, 0:D]
    shift = small_ref[layer : layer + 1, D : 2 * D]
    grad_mid = gm_ref[...]
    mid_low = grad_mid.astype(BF16)
    dsmall_ref[:, 4 * D : 5 * D] += col_sum(mid_low.astype(F32))
    acc_proj[...] += t_mm(mid_low, att_ref[...])
    put_tiles(g_tiles, 0, mm(mid_low, w_proj[...]))
    masks = head_masks()

    def windows(n, carry):
        places_of = [(b, g) for b in range(2) for g in range(2)]
        loaded, dprobs = [], []
        for b, g in places_of:
            w = b * IMAGES + n
            q, key, val = (
                qkv_ref[w, :, part * D + g * HALF : part * D + (g + 1) * HALF] for part in range(3)
            )
            grad = stack_halves(to_sixty_four(get_window(g_tiles, 2 * g, b, n)))
            dprobs.append(mm_t(stack_heads(val, masks), grad))
            loaded.append((q, key, grad, p_ref[w, g]))
        lows = []
        sums = [None, None]
        for (b, g), dprob, (_, _, _, prob) in zip(places_of, dprobs, loaded):
            dprob = dprob.reshape(4, AROWS, LANES)[:, :WROWS]
            p = prob.astype(F32).reshape(4, AROWS, LANES)[:, :WROWS]
            delta = jnp.sum(p * dprob, axis=1, keepdims=True)
            dscore = p * (dprob - delta)
            sums[g] = dscore if sums[g] is None else sums[g] + dscore
            lows.append(pad_keys(dscore))
        for g in range(2):
            acc_tab[g] += sums[g]
        for (b, g), low, (q, key, grad, prob) in zip(places_of, lows, loaded):
            put_window(d_tiles, 2 * g, b, n, pick_halves(t_mm(low, stack_heads(key, masks))) * SCALE)
            put_window(d_tiles, 4 + 2 * g, b, n, pick_heads(mm(low, stack_halves(q))) * SCALE)
            put_window(d_tiles, 8 + 2 * g, b, n, pick_heads(mm(prob, grad)))
        return carry

    lax.fori_loop(0, IMAGES, windows, 0)
    xhat, rstd = normalize(x_ref[...].reshape(STEP_ROWS, D))
    normed = (xhat * gain + shift).astype(BF16)
    grad_normed = None
    for part in range(3):
        cols = slice(part * D, (part + 1) * D)
        low = get_tiles(d_tiles, 4 * part, 4).astype(BF16)
        dsmall_ref[:, 6 * D + part * D : 7 * D + part * D] += col_sum(low.astype(F32))
        acc_qkv[cols, :] += t_mm(low, normed)
        term = mm(low, w_qkv[cols, :])
        grad_normed = term if grad_normed is None else grad_normed + term
    dsmall_ref[:, :D] += col_sum(grad_normed * xhat)
    dsmall_ref[:, D : 2 * D] += col_sum(grad_normed)
    grad_x = grad_mid + norm_back(grad_normed, xhat, rstd, gain)
    dx_ref[...] = grad_x.reshape(WIN, SIDE, IMAGES, D)
    if layer:
        last_strips(dx_ref, strips)

    @pl.when(step == STEPS - 1)
    def _():
        pack_attention(at_ref, acc_qkv, acc_proj, dpacks)
        for g in range(2):
            for a in range(4):
                dtab_ref[8 * g + a] = acc_tab[g, a, :, :AROWS]
                dtab_ref[8 * g + 4 + a] = acc_tab[g, a, :, AROWS:]


def mlp_forward_kernel(layer, n_packs, at_ref, mid_ref, *refs):
    packs, refs = refs[:n_packs], refs[n_packs:]
    small_ref, y_ref, *strips, act_ref, slope_ref, w_one, w_two = refs

    @pl.when(pl.program_id(0) == 0)
    def _():
        unpack_mlp(at_ref, packs, w_one, w_two)

    mid = mid_ref[...]
    xhat, _ = normalize(mid)
    gain = small_ref[layer : layer + 1, 2 * D : 3 * D]
    shift = small_ref[layer : layer + 1, 3 * D : 4 * D]
    normed = (xhat * gain + shift).astype(BF16)
    total = mid + small_ref[layer : layer + 1, 5 * D : 6 * D]
    for c in range(CHUNKS):
        bias = small_ref[layer : layer + 1, 9 * D + c * CHUNK : 9 * D + (c + 1) * CHUNK]
        act, slope = gelu_both(mm_t(normed, w_one[c * CHUNK : (c + 1) * CHUNK, :]) + bias)
        act = act.astype(BF16)
        act_ref[c] = act
        slope_ref[c] = slope.astype(BF16)
        total = total + mm_t(act, w_two[c])
    y_ref[...] = total.reshape(WIN, SIDE, IMAGES, D)
    first_strips(y_ref, strips)


def mlp_backward_kernel(layer, forward, n_packs, n_out, at_ref, mid_ref, dy_ref, *refs):
    strips, refs = refs[:3], refs[3:]
    if not forward:
        (act_ref, slope_ref), refs = refs[:2], refs[2:]
    packs, small_ref, refs = refs[:n_packs], refs[n_packs], refs[n_packs + 1 :]
    if forward:
        (y_ref, *out_strips), refs = refs[:4], refs[4:]
    gm_ref, dpacks, refs = refs[0], refs[1 : 1 + n_out], refs[1 + n_out :]
    dsmall_ref, w_one, w_two, acc_one, acc_two, moved = refs
    step = pl.program_id(0)

    @pl.when(step == 0)
    def _():
        unpack_mlp(at_ref, packs, w_one, w_two)
        for ref in (dsmall_ref, acc_one, acc_two):
            ref[...] = jnp.zeros(ref.shape, ref.dtype)

    mid = mid_ref[...]
    xhat, rstd = normalize(mid)
    gain = small_ref[layer : layer + 1, 2 * D : 3 * D]
    shift = small_ref[layer : layer + 1, 3 * D : 4 * D]
    normed = (xhat * gain + shift).astype(BF16)
    dy = (next_rows if forward else prev_rows)(dy_ref, strips, moved)
    dy_low = dy.astype(BF16)
    dsmall_ref[:, 5 * D : 6 * D] += col_sum(dy_low.astype(F32))
    total = None
    if forward:
        total = mid + small_ref[layer : layer + 1, 5 * D : 6 * D]
    grad_normed = None
    for c in range(CHUNKS):
        if forward:
            bias = small_ref[layer : layer + 1, 9 * D + c * CHUNK : 9 * D + (c + 1) * CHUNK]
            act, slope = gelu_both(mm_t(normed, w_one[c * CHUNK : (c + 1) * CHUNK, :]) + bias)
            act = act.astype(BF16)
            total = total + mm_t(act, w_two[c])
        else:
            act = act_ref[c]
            slope = slope_ref[c].astype(F32)
        grad_pre = (mm(dy_low, w_two[c]) * slope).astype(BF16)
        dsmall_ref[:, 9 * D + c * CHUNK : 9 * D + (c + 1) * CHUNK] += col_sum(grad_pre.astype(F32))
        term = mm(grad_pre, w_one[c * CHUNK : (c + 1) * CHUNK, :])
        grad_normed = term if grad_normed is None else grad_normed + term
        acc_one[c * CHUNK : (c + 1) * CHUNK, :] += t_mm(grad_pre, normed)
        acc_two[c] += t_mm(dy_low, act)
    dsmall_ref[:, 2 * D : 3 * D] += col_sum(grad_normed * xhat)
    dsmall_ref[:, 3 * D : 4 * D] += col_sum(grad_normed)
    gm_ref[...] = dy + norm_back(grad_normed, xhat, rstd, gain)
    if forward:
        moved[...] = total.reshape(WIN, SIDE, IMAGES, D)
        last_strips(moved, out_strips)

        def place(a):
            if a == 0:
                y_ref[SHIFT : SHIFT + WIN, SHIFT:] = moved[:, :KEPT]
            else:
                y_ref[SHIFT + WIN :, SHIFT:] = moved[: WIN - SHIFT, :KEPT]

        both_steps(place)

    @pl.when(step == STEPS - 1)
    def _():
        pack_mlp(at_ref, acc_one, acc_two, dpacks)


def fixed(shape):
    return pl.BlockSpec(shape, lambda s: (0,) * len(shape), pipeline_mode=pl.Buffered(1))


def stepped(shape, axis=0):
    return pl.BlockSpec(shape, lambda s: tuple(s if d == axis else 0 for d in range(len(shape))))


def call(kernel, ins, in_specs, outs, scratch, flops, moved_bytes):
    return pl.pallas_call(
        kernel,
        grid=(STEPS,),
        in_specs=in_specs,
        out_shape=[jax.ShapeDtypeStruct(shape, kind) for shape, kind, _ in outs],
        out_specs=[spec for _, _, spec in outs],
        scratch_shapes=scratch,
        compiler_params=pltpu.CompilerParams(
            dimension_semantics=("arbitrary",), vmem_limit_bytes=VMEM_LIMIT
        ),
        cost_estimate=pl.CostEstimate(
            flops=int(flops), bytes_accessed=int(moved_bytes), transcendentals=0
        ),
    )(*ins)


GRID = (SIDE, SIDE, IMAGES, D)
GRID_STEP = stepped((WIN, SIDE, IMAGES, D))
ROWS_STEP = stepped((STEP_ROWS, D))
WINDOWS_STEP = stepped((STEP_WINDOWS, AROWS, 3 * D))
PROBS_STEP = stepped((STEP_WINDOWS, 2, 4 * AROWS, LANES))
HIDDEN_STEP = stepped((CHUNKS, STEP_ROWS, CHUNK), 1)
STRIPS = ((SHIFT, KEPT, IMAGES, D), (KEPT, SHIFT, IMAGES, D), (SHIFT, SHIFT, IMAGES, D))
STRIP_SPECS = [fixed(shape) for shape in STRIPS]
STRIP_OUTS = [(shape, BF16, fixed(shape)) for shape in STRIPS]
SCALARS = pl.BlockSpec(memory_space=pltpu.SMEM)
SHARD_A = (N_QKV + N_OUT, HALF)
SHARD_B = (N_FC1 + 4 * N_OUT, HALF)
ROW_SUMS = 9 * D + MLP
MOVED = pltpu.VMEM((WIN, SIDE, IMAGES, D), F32)


def tiles_of(features):
    return pltpu.VMEM((features // LANES, STEP_ROWS + IMAGES, LANES), F32)


def pack_specs(packs, shard):
    at = 0 if shard == SHARD_B else packs[0].shape[-2] // shard[0] - 1
    lead = packs[0].shape[:-2]
    return [
        pl.BlockSpec(
            lead + shard, lambda s: (0,) * len(lead) + (at, 0), pipeline_mode=pl.Buffered(1)
        )
    ] * len(packs)


def pack_outs(shard, single):
    if single:
        return [((32,) + shard, BF16, fixed((32,) + shard))]
    return [((4, 4) + shard, BF16, fixed((4, 4) + shard))] * 2


def attention_forward(layer, at, grid_field, strips, packs, small, base):
    out = call(
        partial(attention_forward_kernel, layer, len(packs)),
        (at, grid_field, *strips, *packs, small, base),
        [SCALARS, fixed(GRID) if layer else GRID_STEP]
        + STRIP_SPECS[: len(strips)]
        + pack_specs(packs, SHARD_A)
        + [fixed(small.shape), fixed(base.shape)],
        [((ROWS, D), F32, ROWS_STEP)] * layer
        + [
            ((STEPS * STEP_WINDOWS, AROWS, 3 * D), BF16, WINDOWS_STEP),
            ((STEPS * STEP_WINDOWS, 2, 4 * AROWS, LANES), BF16, PROBS_STEP),
            ((ROWS, D), BF16, ROWS_STEP),
            ((ROWS, D), F32, ROWS_STEP),
        ],
        [
            pltpu.VMEM((3 * D, D), BF16),
            pltpu.VMEM((D, D), BF16),
            tiles_of(3 * D),
            tiles_of(D),
            pltpu.VMEM((4 if layer else 1, 2, 4, WROWS, 2 * AROWS), F32),
        ]
        + [MOVED] * layer,
        2 * ROWS * 4 * D * D * 2,
        30e6,
    )
    return (list(out[:-1]) if layer else [grid_field] + list(out[:-1])), out[-1]


def attention_backward(layer, at, grad_mid, saved, packs, small, rest, single):
    outs = pack_outs(SHARD_A, single)
    out = call(
        partial(attention_backward_kernel, layer, len(packs), len(outs)),
        (at, grad_mid, *saved, *packs, small, rest),
        [
            SCALARS,
            ROWS_STEP,
            ROWS_STEP if layer else GRID_STEP,
            WINDOWS_STEP,
            PROBS_STEP,
            ROWS_STEP,
        ]
        + pack_specs(packs, SHARD_A)
        + [fixed(small.shape), fixed(rest.shape)],
        [(GRID, F32, GRID_STEP)]
        + STRIP_OUTS[: 3 * layer]
        + outs
        + [
            ((HEADS, WROWS, AROWS), F32, fixed((HEADS, WROWS, AROWS))),
            ((1, ROW_SUMS), F32, fixed((1, ROW_SUMS))),
        ],
        [
            pltpu.VMEM((3 * D, D), BF16),
            pltpu.VMEM((D, D), BF16),
            tiles_of(D),
            tiles_of(3 * D),
            pltpu.VMEM((3 * D, D), F32),
            pltpu.VMEM((D, D), F32),
            pltpu.VMEM((2, 4, WROWS, 2 * AROWS), F32),
        ],
        2 * ROWS * 4 * D * D * 5,
        30e6,
    )
    at_pack = 1 + 3 * layer
    return out[0], out[1:at_pack], out[at_pack:-2], out[-2], out[-1]


MLP_WEIGHTS = [pltpu.VMEM((MLP, D), BF16), pltpu.VMEM((CHUNKS, D, CHUNK), BF16)]


def mlp_forward(layer, at, mid, packs, small):
    out = call(
        partial(mlp_forward_kernel, layer, len(packs)),
        (at, mid, *packs, small),
        [SCALARS, ROWS_STEP] + pack_specs(packs, SHARD_B) + [fixed(small.shape)],
        [(GRID, F32, GRID_STEP)]
        + STRIP_OUTS
        + [((CHUNKS, ROWS, CHUNK), BF16, HIDDEN_STEP)] * 2,
        MLP_WEIGHTS,
        2 * ROWS * 2 * D * MLP,
        26e6,
    )
    return out[0], out[1:4], out[4:]


def mlp_backward(layer, at, mid, dy, strips, saved, packs, small, single):
    outs = pack_outs(SHARD_B, single)
    forward = not saved
    extra = 4 if forward else 0
    out = call(
        partial(mlp_backward_kernel, layer, forward, len(packs), len(outs)),
        (at, mid, dy, *strips, *saved, *packs, small),
        [SCALARS, ROWS_STEP, fixed(GRID)]
        + STRIP_SPECS
        + [HIDDEN_STEP] * len(saved)
        + pack_specs(packs, SHARD_B)
        + [fixed(small.shape)],
        ([(GRID, F32, fixed(GRID))] + STRIP_OUTS)[:extra]
        + [((ROWS, D), F32, ROWS_STEP)]
        + outs
        + [((1, ROW_SUMS), F32, fixed((1, ROW_SUMS)))],
        MLP_WEIGHTS
        + [pltpu.VMEM((MLP, D), F32), pltpu.VMEM((CHUNKS, D, CHUNK), F32), MOVED],
        2 * ROWS * (6 if forward else 4) * D * MLP,
        30e6,
    )
    return out[:extra], out[extra], out[extra + 1 : -1], out[-1]


def moved(x, step_of):
    sizes = [lax.axis_size(axis) for axis in AXES]

    def flat(i, r, c):
        return (i * sizes[1] + r) * sizes[2] + c

    pairs = [
        (flat(i, r, c), flat(*step_of(i, r, c)))
        for i in range(sizes[0])
        for r in range(sizes[1])
        for c in range(sizes[2])
    ]
    return lax.ppermute(x, AXES, pairs)


def swapped(x, img=0, down=0, core=0, across=0):
    return moved(x, lambda i, r, c: (i ^ img, r ^ (2 * down + core), c ^ across))


def send_strips(strips, by):
    rows, cols = lax.axis_size("row"), lax.axis_size("col")
    low, right, corner = strips
    return (
        moved(low, lambda i, r, c: (i, (r + by) % rows, c)),
        moved(right, lambda i, r, c: (i, r, (c + by) % cols)),
        moved(corner, lambda i, r, c: (i, (r + by) % rows, (c + by) % cols)),
    )


def fill_prev(grid_field, strips):
    high, left, corner = (strip.astype(F32) for strip in strips)
    grid_field = lax.dynamic_update_slice(grid_field, high, (0, SHIFT, 0, 0))
    grid_field = lax.dynamic_update_slice(grid_field, left, (SHIFT, 0, 0, 0))
    return lax.dynamic_update_slice(grid_field, corner, (0, 0, 0, 0))


QUADS = ((0, 0), (0, 1), (1, 0), (1, 1))


def after(values, *others):
    return lax.optimization_barrier((values, others))[0]


def together(*values):
    return lax.optimization_barrier(values)


def is_small():
    return lax.axis_size("img") == 2


def gather_line(pack):
    return jnp.stack([pack] + [swapped(pack, across=m) for m in (1, 2, 3)])


def gather_quad(line):
    return jnp.stack([line] + [swapped(line, img=i, down=y) for i, y in QUADS[1:]])


def gather_whole(pack, canonical):
    whole = lax.all_gather(pack, AXES, axis=0, tiled=False)
    if not is_small():
        whole = canonical(whole.reshape((lax.axis_size("img"), 16) + pack.shape))
        whole = whole.reshape((32,) + whole.shape[2:])
    return (whole,)


def gather_swaps(pack, canonical):
    if not is_small():
        return gather_whole(pack, canonical)
    quad = gather_quad(gather_line(pack))
    return quad, swapped(quad, core=1)


def scatter_whole(whole, in_shards):
    if not is_small():
        whole = in_shards(whole.reshape((2, 16) + whole.shape[1:]), lax.axis_size("img"))
    flat = whole.reshape(-1, whole.shape[-1])
    return lax.psum_scatter(flat, AXES, scatter_dimension=0, tiled=True)


def scatter_plane(whole):
    if not is_small():
        return whole
    flat = whole.reshape(-1, whole.shape[-1])
    part = lax.psum_scatter(flat, ("img", "row"), scatter_dimension=0, tiled=True)
    return part.reshape((4,) + whole.shape[1:])


def scatter_cols(parts):
    rows = parts[0].shape[1]
    if not is_small():
        return [scatter_whole(part, in_shards) for part, in_shards in zip(parts, (mlp_shards, attention_shards))]
    flat = jnp.concatenate(parts, axis=1).reshape(-1, parts[0].shape[-1])
    whole = lax.psum_scatter(flat, "col", scatter_dimension=0, tiled=True)
    return [whole[:rows], whole[rows:]]


def pair_swap(packs):
    return swapped(packs[1], core=1) if is_small() else packs


def scatter_pair(packs, got):
    if not is_small():
        return packs
    half = packs[0].astype(F32) + got.astype(F32)
    return [half[0]] + [half[m].astype(BF16) for m in (1, 2, 3)]


def quad_swaps(halves):
    if not is_small():
        return []
    return [swapped(h, img=i, down=y) for h, (i, y) in zip(halves[1:], QUADS[1:])]


def scatter_quad(halves, got):
    if not is_small():
        return halves
    got = [g.astype(F32) for g in got]
    line = (halves[0] + got[0]) + (got[1] + got[2])
    return line[:2], line[2:].astype(BF16)


def far_swap(line):
    return swapped(line[1], across=2) if is_small() else line


def scatter_far(line, got):
    if not is_small():
        return line
    ends = line[0] + got.astype(F32)
    return ends[0], ends[1].astype(BF16)


def near_swap(ends):
    return swapped(ends[1], across=1) if is_small() else ends


def scatter_near(ends, got, in_shards):
    if is_small():
        return ends[0] + got.astype(F32)
    return scatter_whole(ends[0], in_shards).astype(F32)


SUM_STEPS = ({"core": 1}, {"img": 1}, {"down": 1}, {"across": 2}, {"across": 1})


def padded_index(rel_index):
    cells = rel_index.T.reshape(WIN, WIN, WIN, WIN)
    gap = (0, SLOT - WIN)
    cells = jnp.pad(cells, [(0, 0), gap, (0, AROWS // SLOT - WIN), gap], constant_values=-1)
    return cells.reshape(1, WROWS * AROWS)


def attention_pack(w_qkv, w_proj):
    return jnp.concatenate([w_qkv.astype(BF16).T, w_proj.astype(BF16).T], axis=0)


def mlp_pack(w_fc1, w_fc2):
    cols = w_fc1.shape[0]
    second = w_fc2.astype(BF16).T
    second = second.reshape(second.shape[0], 4, cols).transpose(1, 0, 2).reshape(-1, cols)
    return jnp.concatenate([w_fc1.astype(BF16).T, second], axis=0)


def attention_canonical(whole):
    _, ranks, rows, _ = whole.shape
    whole = whole.transpose(1, 2, 0, 3).reshape(ranks, rows, 2, HALF)
    return whole.transpose(2, 0, 1, 3)


def both_canonical(whole):
    rows = N_FC1 + 4 * N_OUT
    return jnp.concatenate(
        [mlp_canonical(whole[:, :, :rows]), attention_canonical(whole[:, :, rows:])], axis=2
    )


def attention_shards(pack, size):
    _, ranks, rows, _ = pack.shape
    pack = pack.transpose(1, 2, 0, 3).reshape(ranks, rows, size, D // size)
    return pack.transpose(2, 0, 1, 3)


def mlp_canonical(whole):
    size, ranks, _, cols = whole.shape
    first = attention_canonical(whole[:, :, :N_FC1])
    second = whole[:, :, N_FC1:].reshape(size, ranks, 4, N_OUT, cols)
    second = second.transpose(1, 3, 0, 2, 4).reshape(ranks, N_OUT, 2, 4, HALF)
    second = second.transpose(2, 0, 3, 1, 4).reshape(2, ranks, 4 * N_OUT, HALF)
    return jnp.concatenate([first, second], axis=2)


def mlp_shards(pack, size):
    _, ranks, _, _ = pack.shape
    cols = D // size
    first = attention_shards(pack[:, :, :N_FC1], size)
    second = pack[:, :, N_FC1:].reshape(2, ranks, 4, N_OUT, HALF)
    second = second.transpose(1, 3, 0, 2, 4).reshape(ranks, N_OUT, size, 4, cols)
    second = second.transpose(2, 0, 3, 1, 4).reshape(size, ranks, 4 * N_OUT, cols)
    return jnp.concatenate([first, second], axis=2)


def adam_step(weight, moment_one, second, gradient, rate_value, decay_rate):
    moment_one = BETA_ONE * moment_one + (1.0 - BETA_ONE) * gradient
    second = BETA_TWO * second + (1.0 - BETA_TWO) * gradient * gradient
    update = (
        moment_one / (1.0 - BETA_ONE**STEP) / (jnp.sqrt(second / (1.0 - BETA_TWO**STEP)) + EPS_ADAM)
    )
    return (weight - rate_value * (update + decay_rate * weight), moment_one, second)


def shards(
    images,
    grad_out,
    w_qkv,
    w_proj,
    w_fc1,
    w_fc2,
    first_qkv,
    first_proj,
    first_fc1,
    first_fc2,
    second_qkv,
    second_proj,
    second_fc1,
    second_fc2,
    small_params,
    small_first,
    small_second,
    rel_index,
):
    assert images.shape == (IMAGES, SIDE, SIDE, D)
    size = lax.axis_size("img")
    small = is_small()
    row, col = lax.axis_index("row"), lax.axis_index("col")
    last = [row == lax.axis_size("row") - 1, col == lax.axis_size("col") - 1]
    place = [lax.axis_index("img"), row // 2, row % 2, col]
    at = jnp.stack([jnp.asarray(value, jnp.int32) for value in place + last])
    images = images.transpose(1, 2, 0, 3)
    grad_out = grad_out.transpose(1, 2, 0, 3)

    attention_packs = [attention_pack(w_qkv[l], w_proj[l]) for l in range(2)]
    mlp_packs = [mlp_pack(w_fc1[l], w_fc2[l]) for l in range(2)]
    packs_mixed = gather_whole(
        jnp.concatenate([mlp_packs[0], attention_packs[1]], axis=0), both_canonical
    )
    packs_a = gather_swaps(attention_packs[0], attention_canonical)
    packs_last = gather_whole(mlp_packs[1], mlp_canonical)

    onehot = (
        jnp.arange(RELPOS, dtype=jnp.int32)[:, None] == padded_index(rel_index)
    ).astype(F32)
    tables = small_params[:, 9 * D + MLP :].reshape(2, RELPOS, HEADS)
    base = jnp.einsum("lrh,rp->lhp", tables * LOG2E, onehot, precision=lax.Precision.HIGHEST)
    base = base.reshape(2, HEADS, WROWS, AROWS)
    grad_strips = (
        grad_out[:SHIFT, SHIFT:].astype(BF16),
        grad_out[SHIFT:, :SHIFT].astype(BF16),
        grad_out[:SHIFT, :SHIFT].astype(BF16),
    )

    def table_row(sums, dtab):
        table = jnp.einsum(
            "hp,rp->rh", dtab.reshape(HEADS, -1), onehot, precision=lax.Precision.HIGHEST
        )
        return jnp.concatenate([sums, table.reshape(1, -1)], axis=1)

    packs_a = after(packs_a, base, grad_strips)
    saved_zero, mid_zero = attention_forward(0, at, images, (), packs_a, small_params, base[0])
    out_zero, strips, hidden_zero = mlp_forward(0, at, mid_zero, packs_mixed, small_params)
    strips = send_strips(strips, -1)
    saved_one, mid_one = attention_forward(
        1, at, out_zero, strips, packs_mixed, small_params, base[1]
    )
    grad_strips = send_strips(after(grad_strips, strips), -1)
    mid_one, grad_strips = together(mid_one, grad_strips)
    (out_one, *out_strips), gm_one, dpacks, rest = mlp_backward(
        1, at, mid_one, grad_out, grad_strips, (), packs_last, small_params, True
    )

    plane_b_one = scatter_plane(dpacks[0])
    out_strips = send_strips(out_strips, 1)
    dx_one, strips, dpacks, dtab_one, sums = attention_backward(
        1, at, gm_one, saved_one, packs_mixed, small_params, rest, True
    )
    strips, dpacks, out_strips = together(strips, dpacks, out_strips)
    plane_a_one = scatter_plane(dpacks[0])
    strips, plane_b_one, out_one, row_one = together(
        send_strips(strips, 1),
        plane_b_one,
        fill_prev(out_one, out_strips),
        table_row(sums, dtab_one),
    )
    outputs = out_one.transpose(2, 0, 1, 3)
    _, gm_zero, dpacks, rest = mlp_backward(
        0, at, mid_zero, dx_one, strips, hidden_zero, packs_mixed, small_params, not small
    )

    halves_b_zero = scatter_pair(dpacks, pair_swap(dpacks))
    gm_zero, halves_b_zero, plane_a_one = together(gm_zero, halves_b_zero, plane_a_one)
    sums_one = scatter_cols((plane_b_one, plane_a_one))
    grad_input, _, dpacks, dtab_zero, sums = attention_backward(
        0, at, gm_zero, saved_zero, packs_a, small_params, rest, not small
    )
    grad_input = grad_input.transpose(2, 0, 1, 3)

    dpacks, got, sums_one = together(dpacks, quad_swaps(halves_b_zero), sums_one)
    line_b_zero = scatter_quad(halves_b_zero, got)
    got, small_row = together(pair_swap(dpacks), table_row(sums, dtab_zero))
    halves_a_zero = scatter_pair(dpacks, got)
    small_grad = jnp.concatenate([small_row, row_one], axis=0)

    def small_swap(k):
        return swapped(small_grad, **SUM_STEPS[k]) if small else jnp.zeros_like(small_grad)

    got, far, part = together(quad_swaps(halves_a_zero), far_swap(line_b_zero), small_swap(0))
    small_grad = small_grad + part
    line_a_zero = scatter_quad(halves_a_zero, got)
    ends_b_zero = scatter_far(line_b_zero, far)
    far, near, part = together(far_swap(line_a_zero), near_swap(ends_b_zero), small_swap(1))
    small_grad = small_grad + part
    ends_a_zero = scatter_far(line_a_zero, far)
    sum_b_zero = scatter_near(ends_b_zero, near, mlp_shards)
    near, part = together(near_swap(ends_a_zero), small_swap(2))
    small_grad = small_grad + part
    sum_a_zero = scatter_near(ends_a_zero, near, attention_shards)
    for k in (3, 4):
        small_grad = small_grad + small_swap(k)
    if not small:
        small_grad = lax.psum(small_grad, AXES)
    sums_b = [sum_b_zero, sums_one[0].astype(F32)]
    sums_a = [sum_a_zero, sums_one[1].astype(F32)]

    cols = D // size
    grads = (
        jnp.stack([s[:N_QKV].T for s in sums_a]),
        jnp.stack([s[N_QKV:].T for s in sums_a]),
        jnp.stack([s[:N_FC1].T for s in sums_b]),
        jnp.stack(
            [s[N_FC1:].reshape(4, N_OUT, cols).transpose(0, 2, 1).reshape(4 * cols, N_OUT) for s in sums_b]
        ),
    )

    masters = (w_qkv, w_proj, w_fc1, w_fc2)
    firsts = (first_qkv, first_proj, first_fc1, first_fc2)
    seconds = (second_qkv, second_proj, second_fc1, second_fc2)
    updated = [
        adam_step(masters[k], firsts[k], seconds[k], grads[k], RATE_MATRIX, DECAY_MATRIX)
        for k in range(4)
    ]
    small_new = adam_step(small_params, small_first, small_second, small_grad, RATE_SMALL, 0.0)
    return (
        (outputs, grad_input)
        + tuple(new[0] for new in updated)
        + tuple(new[1] for new in updated)
        + tuple(new[2] for new in updated)
        + tuple(small_new)
    )


def solution(mesh):
    grid_spec = P("img", "row", "col", None)
    matrix = P(None, "img", ("row", "col"))
    in_specs = (grid_spec,) * 2 + (matrix,) * 12 + (P(),) * 4
    out_specs = (grid_spec,) * 2 + (matrix,) * 12 + (P(),) * 3
    return jax.shard_map(shards, mesh=mesh, in_specs=in_specs, out_specs=out_specs, check_vma=False)
```

```python
from functools import partial

import jax
import jax.numpy as jnp
from jax import lax
from jax.experimental import pallas as pl
from jax.experimental.pallas import tpu as pltpu
from jax.sharding import PartitionSpec as P

D = 512
HEADS = 16
HEAD_DIM = 32
MLP = 2048
WIN = 7
SHIFT = 3
STEP = 10
RELPOS = 169

EPS_NORM = 1e-05
BETA_ONE = 0.9
BETA_TWO = 0.999
EPS_ADAM = 1e-08
RATE_MATRIX = 0.05
RATE_SMALL = 0.3
DECAY_MATRIX = 0.05
MASKED = -1e30

AXES = ("img", "row", "col")
F32 = jnp.float32
BF16 = jnp.bfloat16
LOG2E = 1.4426950408889634
SCALE = HEAD_DIM ** (-0.5)

SIDE = 2 * WIN
IMAGES = 8
SLOT = 8
WROWS = WIN * SLOT
AROWS = 64
STEPS = 2
STEP_ROWS = WIN * SIDE * IMAGES
ROWS = STEPS * STEP_ROWS
STEP_WINDOWS = 2 * IMAGES
KEPT = SIDE - SHIFT
CHUNK = 512
CHUNKS = MLP // CHUNK
HALF = D // 2
LANES = 128
VMEM_LIMIT = 60 * 1024 * 1024


def mm(left, right):
    return lax.dot_general(left, right, (((1,), (0,)), ((), ())), preferred_element_type=F32)


def mm_t(left, right):
    return lax.dot_general(left, right, (((1,), (1,)), ((), ())), preferred_element_type=F32)


def t_mm(left, right):
    return lax.dot_general(left, right, (((0,), (0,)), ((), ())), preferred_element_type=F32)


def col_sum(value):
    return jnp.sum(value, axis=0, keepdims=True)


def normalize(rows):
    center = rows - jnp.mean(rows, axis=-1, keepdims=True)
    spread = jnp.mean(center * center, axis=-1, keepdims=True)
    rstd = lax.rsqrt(spread + EPS_NORM)
    return center * rstd, rstd


def norm_back(grad, xhat, rstd, gain):
    scaled = grad * gain
    mean_one = jnp.mean(scaled, axis=-1, keepdims=True)
    mean_two = jnp.mean(scaled * xhat, axis=-1, keepdims=True)
    return rstd * (scaled - mean_one - xhat * mean_two)


def gelu_both(pre):
    size = jnp.abs(pre)
    t = 1.0 / (1.0 + size * (0.3275911 * 0.7071067811865476))
    bell = jnp.exp2(pre * pre * (-0.5 * LOG2E))
    poly = 0.5 * 1.061405429
    poly = poly * t + 0.5 * -1.453152027
    poly = poly * t + 0.5 * 1.421413741
    poly = poly * t + 0.5 * -0.284496736
    poly = poly * t + 0.5 * 0.254829592
    tail = poly * t * bell
    cdf = jnp.where(pre >= 0.0, 1.0 - tail, tail)
    return pre * cdf, cdf + pre * bell * 0.3989422804014327


def both_steps(body):
    for a in range(STEPS):
        pl.when(pl.program_id(0) == a)(partial(body, a))


def next_rows(grid_ref, strip_refs, rows_ref):
    low_ref, right_ref, corner_ref = strip_refs

    def body(a):
        if a == 0:
            rows_ref[:, :KEPT] = grid_ref[SHIFT : SHIFT + WIN, SHIFT:]
            rows_ref[:, KEPT:] = right_ref[:WIN].astype(F32)
        else:
            rows_ref[: WIN - SHIFT, :KEPT] = grid_ref[SHIFT + WIN :, SHIFT:]
            rows_ref[: WIN - SHIFT, KEPT:] = right_ref[WIN:].astype(F32)
            rows_ref[WIN - SHIFT :, :KEPT] = low_ref[...].astype(F32)
            rows_ref[WIN - SHIFT :, KEPT:] = corner_ref[...].astype(F32)

    both_steps(body)
    return rows_ref[...].reshape(STEP_ROWS, D)


def prev_rows(grid_ref, strip_refs, rows_ref):
    high_ref, left_ref, corner_ref = strip_refs

    def body(a):
        if a == 0:
            rows_ref[:SHIFT, SHIFT:] = high_ref[...].astype(F32)
            rows_ref[:SHIFT, :SHIFT] = corner_ref[...].astype(F32)
            rows_ref[SHIFT:, SHIFT:] = grid_ref[: WIN - SHIFT, :KEPT]
            rows_ref[SHIFT:, :SHIFT] = left_ref[: WIN - SHIFT].astype(F32)
        else:
            rows_ref[:, SHIFT:] = grid_ref[WIN - SHIFT : KEPT, :KEPT]
            rows_ref[:, :SHIFT] = left_ref[WIN - SHIFT :].astype(F32)

    both_steps(body)
    return rows_ref[...].reshape(STEP_ROWS, D)


def first_strips(block_ref, strip_refs):
    rows_ref, cols_ref, corner_ref = strip_refs

    def body(a):
        if a == 0:
            rows_ref[...] = block_ref[:SHIFT, SHIFT:].astype(BF16)
            cols_ref[: WIN - SHIFT] = block_ref[SHIFT:, :SHIFT].astype(BF16)
            corner_ref[...] = block_ref[:SHIFT, :SHIFT].astype(BF16)
        else:
            cols_ref[WIN - SHIFT :] = block_ref[:, :SHIFT].astype(BF16)

    both_steps(body)


def last_strips(block_ref, strip_refs):
    rows_ref, cols_ref, corner_ref = strip_refs

    def body(a):
        if a == 0:
            cols_ref[:WIN] = block_ref[:, KEPT:].astype(BF16)
        else:
            cols_ref[WIN:] = block_ref[: WIN - SHIFT, KEPT:].astype(BF16)
            rows_ref[...] = block_ref[WIN - SHIFT :, :KEPT].astype(BF16)
            corner_ref[...] = block_ref[WIN - SHIFT :, KEPT:].astype(BF16)

    both_steps(body)


def put_tiles(tiles, first, value):
    for t in range(value.shape[1] // LANES):
        tiles[first + t, :STEP_ROWS, :] = value[:, t * LANES : (t + 1) * LANES]


def get_tiles(tiles, first, count):
    return jnp.concatenate([tiles[first + t, :STEP_ROWS, :] for t in range(count)], axis=1)


def clear_tail(tiles):
    tiles[:, STEP_ROWS:, :] = jnp.zeros(tiles[:, STEP_ROWS:, :].shape, F32)


def window_at(b, n, r):
    return b * WIN * IMAGES + r * SIDE * IMAGES + n


def get_window(tiles, first, b, n):
    return jnp.concatenate(
        [
            jnp.concatenate(
                [
                    tiles[first + t, pl.ds(window_at(b, n, r), SLOT, stride=IMAGES), :]
                    for r in range(WIN)
                ],
                axis=0,
            )
            for t in range(2)
        ],
        axis=1,
    )


def put_window(tiles, first, b, n, value):
    for t in range(2):
        for r in range(WIN):
            tiles[first + t, pl.ds(window_at(b, n, r), WIN, stride=IMAGES), :] = value[
                r * SLOT : r * SLOT + WIN, t * LANES : (t + 1) * LANES
            ]


def to_sixty_four(window):
    padding = jnp.zeros((AROWS - WROWS, window.shape[1]), F32)
    return jnp.concatenate([window, padding], axis=0).astype(BF16)


def head_masks():
    lane = lax.broadcasted_iota(jnp.int32, (16, HALF), 1)
    head = jnp.bitwise_and(lax.shift_right_logical(lane, 5), 3)
    return [jnp.where(head == a, 1.0, 0.0).astype(BF16) for a in range(4)]


def stack_heads(part, masks):
    split = part.reshape(AROWS // 16, 16, HALF)
    return jnp.concatenate(
        [(split * mask[None]).reshape(AROWS, HALF) for mask in masks], axis=0
    )


def stack_halves(part):
    zero = jnp.zeros((AROWS, HALF // 2), part.dtype)
    return jnp.concatenate(
        [
            jnp.concatenate([part[:, : HALF // 2], zero], axis=1),
            jnp.concatenate([zero, part[:, HALF // 2 :]], axis=1),
        ],
        axis=0,
    )


def pick_halves(result):
    return jnp.concatenate(
        [result[:WROWS, : HALF // 2], result[AROWS : AROWS + WROWS, HALF // 2 :]], axis=1
    )


def pick_heads(result):
    lane = lax.broadcasted_iota(jnp.int32, (WROWS, HALF), 1)
    head = jnp.bitwise_and(lax.shift_right_logical(lane, 5), 3)
    picked = result[3 * AROWS : 3 * AROWS + WROWS]
    for a in (2, 1, 0):
        picked = jnp.where(head == a, result[a * AROWS : a * AROWS + WROWS], picked)
    return picked


def pad_keys(value):
    padding = jnp.zeros((4, AROWS - WROWS, 128), F32)
    return jnp.concatenate([value, padding], axis=1).astype(BF16).reshape(4 * AROWS, 128)


def places(at_ref, packs):
    if len(packs) == 1:
        for shard in range(packs[0].shape[0]):
            yield 0, (shard,), shard // 16, shard % 16
        return
    for core in range(2):
        for quad in range(4):
            for across in range(4):
                i = jnp.bitwise_xor(at_ref[0], quad >> 1)
                y = jnp.bitwise_xor(at_ref[1], quad & 1)
                c = jnp.bitwise_xor(at_ref[2], core)
                z = jnp.bitwise_xor(at_ref[3], across)
                yield core, (quad, across), i, (2 * y + c) * 4 + z


def piece(start, length):
    if isinstance(start, int):
        return pl.ds(start * length, length)
    return pl.ds(pl.multiple_of(start * length, length), length)


N_QKV = 3 * D // 16
N_OUT = D // 16
N_FC1 = MLP // 16


def unpack_attention(at_ref, packs, w_qkv, w_proj):
    for core, at, i, r in places(at_ref, packs):
        cols = piece(i, HALF)
        w_qkv[piece(r, N_QKV), cols] = packs[core][at + (slice(0, N_QKV),)]
        w_proj[piece(r, N_OUT), cols] = packs[core][at + (slice(N_QKV, None),)]


def pack_attention(at_ref, g_qkv, g_proj, packs):
    for core, at, i, r in places(at_ref, packs):
        cols = piece(i, HALF)
        packs[core][at + (slice(0, N_QKV),)] = g_qkv[piece(r, N_QKV), cols].astype(BF16)
        packs[core][at + (slice(N_QKV, None),)] = g_proj[piece(r, N_OUT), cols].astype(BF16)


def unpack_mlp(at_ref, packs, w_one, w_two):
    for core, at, i, r in places(at_ref, packs):
        for h in range(2):
            w_one[piece(2 * i + h, LANES), piece(r, N_FC1)] = packs[core][
                at + (slice(0, N_FC1), slice(h * LANES, (h + 1) * LANES))
            ]
        for k in range(4):
            w_two[2 * i + k // 2, piece(r, N_OUT), (k % 2) * HALF : (k % 2 + 1) * HALF] = packs[core][
                at + (slice(N_FC1 + k * N_OUT, N_FC1 + (k + 1) * N_OUT),)
            ]


def pack_mlp(at_ref, g_one, g_two, packs):
    for core, at, i, r in places(at_ref, packs):
        for h in range(2):
            packs[core][at + (slice(0, N_FC1), slice(h * LANES, (h + 1) * LANES))] = g_one[
                piece(2 * i + h, LANES), piece(r, N_FC1)
            ].astype(BF16)
        for k in range(4):
            packs[core][at + (slice(N_FC1 + k * N_OUT, N_FC1 + (k + 1) * N_OUT),)] = g_two[
                2 * i + k // 2, piece(r, N_OUT), (k % 2) * HALF : (k % 2 + 1) * HALF
            ].astype(BF16)


def spread_bias(layer, at_ref, base_ref, bias):
    row = lax.broadcasted_iota(jnp.int32, (WROWS, 2 * AROWS), 0)
    lane = jnp.bitwise_and(lax.broadcasted_iota(jnp.int32, (WROWS, 2 * AROWS), 1), AROWS - 1)
    key_row, key_col = row // SLOT, jnp.bitwise_and(row, SLOT - 1)
    query_row, query_col = lane // SLOT, jnp.bitwise_and(lane, SLOT - 1)
    kept = WIN - SHIFT
    other_row = ((key_row >= kept) != (query_row >= kept)).astype(jnp.int32)
    other_col = ((key_col >= kept) != (query_col >= kept)).astype(jnp.int32)
    padding = (key_col == WIN).astype(jnp.int32)
    for v in range(bias.shape[0]):
        hidden = padding
        if layer == 1:
            if v >> 1:
                hidden = hidden + other_row * at_ref[4]
            if v & 1:
                hidden = hidden + other_col * at_ref[5]
        for g in range(2):
            for a in range(4):
                both = jnp.concatenate([base_ref[8 * g + a], base_ref[8 * g + 4 + a]], axis=1)
                bias[v, g, a] = jnp.where(hidden > 0, MASKED, both)


def attention_forward_kernel(layer, n_packs, at_ref, x_ref, *refs):
    strips, refs = refs[: 3 * layer], refs[3 * layer :]
    packs, refs = refs[:n_packs], refs[n_packs:]
    small_ref, base_ref, refs = refs[0], refs[1], refs[2:]
    if layer:
        xs_ref, refs = refs[0], refs[1:]
    qkv_ref, p_ref, att_ref, mid_ref, w_qkv, w_proj, tiles, att_tiles, bias_ref, *moved = refs
    step = pl.program_id(0)

    @pl.when(step == 0)
    def _():
        unpack_attention(at_ref, packs, w_qkv, w_proj)
        spread_bias(layer, at_ref, base_ref, bias_ref)
        clear_tail(tiles)

    gain = small_ref[layer : layer + 1, 0:D]
    shift = small_ref[layer : layer + 1, D : 2 * D]
    if layer:
        rows = next_rows(x_ref, strips, moved[0])
        xs_ref[...] = rows
    else:
        rows = x_ref[...].reshape(STEP_ROWS, D)
    xhat, _ = normalize(rows)
    normed = (xhat * gain + shift).astype(BF16)
    for part in range(3):
        cols = slice(part * D, (part + 1) * D)
        bias = small_ref[layer : layer + 1, 6 * D + part * D : 7 * D + part * D]
        put_tiles(tiles, 4 * part, mm_t(normed, w_qkv[cols, :]) + bias)
    masks = head_masks()
    lane = jnp.bitwise_and(lax.broadcasted_iota(jnp.int32, (4, 1, LANES), 2), AROWS - 1)
    no_query = (jnp.bitwise_and(lane, SLOT - 1) == WIN) | (lane >= WROWS)

    def windows(pair, carry):
        places_of = [(b, g, 2 * pair + k) for k in range(2) for b in range(2) for g in range(2)]
        scores, values = [], []
        for b, g, n in places_of:
            q, key, val = (
                to_sixty_four(get_window(tiles, 4 * part + 2 * g, b, n)) for part in range(3)
            )
            for part, value in enumerate((q, key, val)):
                at = part * D + g * HALF
                qkv_ref[b * IMAGES + n, :, at : at + HALF] = value
            scores.append(mm_t(stack_heads(key, masks), stack_halves(q)))
            values.append(val)
        probs = []
        for (b, g, n), score in zip(places_of, scores):
            v = 2 * step + b if layer else 0
            score = score.reshape(4, AROWS, LANES)[:, :WROWS] * (SCALE * LOG2E) + bias_ref[v, g]
            powers = jnp.exp2(score - jnp.max(score, axis=1, keepdims=True))
            total = jnp.sum(powers, axis=1, keepdims=True)
            prob = pad_keys(powers * jnp.where(no_query, 0.0, 1.0 / total))
            p_ref[b * IMAGES + n, g] = prob
            probs.append(prob)
        for (b, g, n), prob, val in zip(places_of, probs, values):
            put_window(att_tiles, 2 * g, b, n, pick_halves(t_mm(prob, stack_heads(val, masks))))
        return carry

    lax.fori_loop(0, IMAGES // 2, windows, 0)
    att = get_tiles(att_tiles, 0, 4).astype(BF16)
    att_ref[...] = att
    bias = small_ref[layer : layer + 1, 4 * D : 5 * D]
    mid_ref[...] = rows + (mm_t(att, w_proj[...]) + bias)


def attention_backward_kernel(layer, n_packs, n_out, at_ref, gm_ref, x_ref, qkv_ref, p_ref, att_ref, *refs):
    packs, refs = refs[:n_packs], refs[n_packs:]
    small_ref, rest_ref, dx_ref, refs = refs[0], refs[1], refs[2], refs[3:]
    strips, refs = refs[: 3 * layer], refs[3 * layer :]
    dpacks, refs = refs[:n_out], refs[n_out:]
    dtab_ref, dsmall_ref, w_qkv, w_proj, g_tiles, d_tiles, acc_qkv, acc_proj, acc_tab = refs
    step = pl.program_id(0)

    @pl.when(step == 0)
    def _():
        unpack_attention(at_ref, packs, w_qkv, w_proj)
        dsmall_ref[...] = rest_ref[...]
        clear_tail(g_tiles)
        for ref in (acc_tab, acc_qkv, acc_proj):
            ref[...] = jnp.zeros(ref.shape, ref.dtype)

    gain = small_ref[layer : layer + 1, 0:D]
    shift = small_ref[layer : layer + 1, D : 2 * D]
    grad_mid = gm_ref[...]
    mid_low = grad_mid.astype(BF16)
    dsmall_ref[:, 4 * D : 5 * D] += col_sum(mid_low.astype(F32))
    acc_proj[...] += t_mm(mid_low, att_ref[...])
    put_tiles(g_tiles, 0, mm(mid_low, w_proj[...]))
    masks = head_masks()

    def windows(pair, carry):
        places_of = [(b, g, 2 * pair + k) for k in range(2) for b in range(2) for g in range(2)]
        loaded, dprobs = [], []
        for b, g, n in places_of:
            w = b * IMAGES + n
            q, key, val = (
                qkv_ref[w, :, part * D + g * HALF : part * D + (g + 1) * HALF] for part in range(3)
            )
            grad = stack_halves(to_sixty_four(get_window(g_tiles, 2 * g, b, n)))
            dprobs.append(mm_t(stack_heads(val, masks), grad))
            loaded.append((q, key, grad, p_ref[w, g]))
        lows = []
        sums = [None, None]
        for (b, g, _), dprob, (_, _, _, prob) in zip(places_of, dprobs, loaded):
            dprob = dprob.reshape(4, AROWS, LANES)[:, :WROWS]
            p = prob.astype(F32).reshape(4, AROWS, LANES)[:, :WROWS]
            delta = jnp.sum(p * dprob, axis=1, keepdims=True)
            dscore = p * (dprob - delta)
            sums[g] = dscore if sums[g] is None else sums[g] + dscore
            lows.append(pad_keys(dscore))
        for g in range(2):
            acc_tab[g] += sums[g]
        for (b, g, n), low, (q, key, grad, prob) in zip(places_of, lows, loaded):
            put_window(d_tiles, 2 * g, b, n, pick_halves(t_mm(low, stack_heads(key, masks))) * SCALE)
            put_window(d_tiles, 4 + 2 * g, b, n, pick_heads(mm(low, stack_halves(q))) * SCALE)
            put_window(d_tiles, 8 + 2 * g, b, n, pick_heads(mm(prob, grad)))
        return carry

    lax.fori_loop(0, IMAGES // 2, windows, 0)
    xhat, rstd = normalize(x_ref[...].reshape(STEP_ROWS, D))
    normed = (xhat * gain + shift).astype(BF16)
    grad_normed = None
    for part in range(3):
        cols = slice(part * D, (part + 1) * D)
        low = get_tiles(d_tiles, 4 * part, 4).astype(BF16)
        dsmall_ref[:, 6 * D + part * D : 7 * D + part * D] += col_sum(low.astype(F32))
        acc_qkv[cols, :] += t_mm(low, normed)
        term = mm(low, w_qkv[cols, :])
        grad_normed = term if grad_normed is None else grad_normed + term
    dsmall_ref[:, :D] += col_sum(grad_normed * xhat)
    dsmall_ref[:, D : 2 * D] += col_sum(grad_normed)
    grad_x = grad_mid + norm_back(grad_normed, xhat, rstd, gain)
    dx_ref[...] = grad_x.reshape(WIN, SIDE, IMAGES, D)
    if layer:
        last_strips(dx_ref, strips)

    @pl.when(step == STEPS - 1)
    def _():
        pack_attention(at_ref, acc_qkv, acc_proj, dpacks)
        for g in range(2):
            for a in range(4):
                dtab_ref[8 * g + a] = acc_tab[g, a, :, :AROWS]
                dtab_ref[8 * g + 4 + a] = acc_tab[g, a, :, AROWS:]


def mlp_forward_kernel(layer, n_packs, at_ref, mid_ref, *refs):
    packs, refs = refs[:n_packs], refs[n_packs:]
    small_ref, y_ref, *strips, act_ref, slope_ref, w_one, w_two = refs

    @pl.when(pl.program_id(0) == 0)
    def _():
        unpack_mlp(at_ref, packs, w_one, w_two)

    mid = mid_ref[...]
    xhat, _ = normalize(mid)
    gain = small_ref[layer : layer + 1, 2 * D : 3 * D]
    shift = small_ref[layer : layer + 1, 3 * D : 4 * D]
    normed = (xhat * gain + shift).astype(BF16)
    total = mid + small_ref[layer : layer + 1, 5 * D : 6 * D]

    def hidden(c):
        bias = small_ref[layer : layer + 1, 9 * D + c * CHUNK : 9 * D + (c + 1) * CHUNK]
        return mm(normed, w_one[:, c * CHUNK : (c + 1) * CHUNK]) + bias

    pre = hidden(0)
    for c in range(CHUNKS):
        following = hidden(c + 1) if c + 1 < CHUNKS else None
        act, slope = gelu_both(pre)
        act = act.astype(BF16)
        act_ref[c] = act
        slope_ref[c] = slope.astype(BF16)
        total = total + mm_t(act, w_two[c])
        pre = following
    y_ref[...] = total.reshape(WIN, SIDE, IMAGES, D)
    first_strips(y_ref, strips)


def mlp_backward_kernel(layer, forward, n_packs, n_out, at_ref, mid_ref, dy_ref, *refs):
    strips, refs = refs[:3], refs[3:]
    if not forward:
        (act_ref, slope_ref), refs = refs[:2], refs[2:]
    packs, small_ref, refs = refs[:n_packs], refs[n_packs], refs[n_packs + 1 :]
    if forward:
        (y_ref, *out_strips), refs = refs[:4], refs[4:]
    gm_ref, dpacks, refs = refs[0], refs[1 : 1 + n_out], refs[1 + n_out :]
    dsmall_ref, w_one, w_two, acc_one, acc_two, moved = refs
    step = pl.program_id(0)

    @pl.when(step == 0)
    def _():
        unpack_mlp(at_ref, packs, w_one, w_two)
        for ref in (dsmall_ref, acc_one, acc_two):
            ref[...] = jnp.zeros(ref.shape, ref.dtype)

    mid = mid_ref[...]
    xhat, rstd = normalize(mid)
    gain = small_ref[layer : layer + 1, 2 * D : 3 * D]
    shift = small_ref[layer : layer + 1, 3 * D : 4 * D]
    normed = (xhat * gain + shift).astype(BF16)
    dy = (next_rows if forward else prev_rows)(dy_ref, strips, moved)
    dy_low = dy.astype(BF16)
    dsmall_ref[:, 5 * D : 6 * D] += col_sum(dy_low.astype(F32))
    total = None
    if forward:
        total = mid + small_ref[layer : layer + 1, 5 * D : 6 * D]

    def products(c):
        grad_act = mm(dy_low, w_two[c])
        if not forward:
            return None, grad_act
        bias = small_ref[layer : layer + 1, 9 * D + c * CHUNK : 9 * D + (c + 1) * CHUNK]
        return mm(normed, w_one[:, c * CHUNK : (c + 1) * CHUNK]) + bias, grad_act

    grad_normed = None
    pre, grad_act = products(0)
    for c in range(CHUNKS):
        cols = slice(c * CHUNK, (c + 1) * CHUNK)
        following = products(c + 1) if c + 1 < CHUNKS else (None, None)
        if forward:
            act, slope = gelu_both(pre)
            act = act.astype(BF16)
            total = total + mm_t(act, w_two[c])
        else:
            act = act_ref[c]
            slope = slope_ref[c].astype(F32)
        grad_pre = (grad_act * slope).astype(BF16)
        dsmall_ref[:, 9 * D + c * CHUNK : 9 * D + (c + 1) * CHUNK] += col_sum(grad_pre.astype(F32))
        term = mm_t(grad_pre, w_one[:, cols])
        grad_normed = term if grad_normed is None else grad_normed + term
        acc_one[:, cols] += t_mm(normed, grad_pre)
        acc_two[c] += t_mm(dy_low, act)
        pre, grad_act = following
    dsmall_ref[:, 2 * D : 3 * D] += col_sum(grad_normed * xhat)
    dsmall_ref[:, 3 * D : 4 * D] += col_sum(grad_normed)
    gm_ref[...] = dy + norm_back(grad_normed, xhat, rstd, gain)
    if forward:
        moved[...] = total.reshape(WIN, SIDE, IMAGES, D)
        last_strips(moved, out_strips)

        def place(a):
            if a == 0:
                y_ref[SHIFT : SHIFT + WIN, SHIFT:] = moved[:, :KEPT]
            else:
                y_ref[SHIFT + WIN :, SHIFT:] = moved[: WIN - SHIFT, :KEPT]

        both_steps(place)

    @pl.when(step == STEPS - 1)
    def _():
        pack_mlp(at_ref, acc_one, acc_two, dpacks)


def fixed(shape):
    return pl.BlockSpec(shape, lambda s: (0,) * len(shape), pipeline_mode=pl.Buffered(1))


def stepped(shape, axis=0):
    return pl.BlockSpec(shape, lambda s: tuple(s if d == axis else 0 for d in range(len(shape))))


def call(kernel, ins, in_specs, outs, scratch, flops, moved_bytes):
    return pl.pallas_call(
        kernel,
        grid=(STEPS,),
        in_specs=in_specs,
        out_shape=[jax.ShapeDtypeStruct(shape, kind) for shape, kind, _ in outs],
        out_specs=[spec for _, _, spec in outs],
        scratch_shapes=scratch,
        compiler_params=pltpu.CompilerParams(
            dimension_semantics=("arbitrary",), vmem_limit_bytes=VMEM_LIMIT
        ),
        cost_estimate=pl.CostEstimate(
            flops=int(flops), bytes_accessed=int(moved_bytes), transcendentals=0
        ),
    )(*ins)


GRID = (SIDE, SIDE, IMAGES, D)
GRID_STEP = stepped((WIN, SIDE, IMAGES, D))
ROWS_STEP = stepped((STEP_ROWS, D))
WINDOWS_STEP = stepped((STEP_WINDOWS, AROWS, 3 * D))
PROBS_STEP = stepped((STEP_WINDOWS, 2, 4 * AROWS, LANES))
HIDDEN_STEP = stepped((CHUNKS, STEP_ROWS, CHUNK), 1)
STRIPS = ((SHIFT, KEPT, IMAGES, D), (KEPT, SHIFT, IMAGES, D), (SHIFT, SHIFT, IMAGES, D))
STRIP_SPECS = [fixed(shape) for shape in STRIPS]
STRIP_OUTS = [(shape, BF16, fixed(shape)) for shape in STRIPS]
SCALARS = pl.BlockSpec(memory_space=pltpu.SMEM)
SHARD_A = (N_QKV + N_OUT, HALF)
SHARD_B = (N_FC1 + 4 * N_OUT, HALF)
ROW_SUMS = 9 * D + MLP
MOVED = pltpu.VMEM((WIN, SIDE, IMAGES, D), F32)


def tiles_of(features):
    return pltpu.VMEM((features // LANES, STEP_ROWS + IMAGES, LANES), F32)


def pack_specs(packs, shard):
    at = 0 if shard == SHARD_B else packs[0].shape[-2] // shard[0] - 1
    lead = packs[0].shape[:-2]
    return [
        pl.BlockSpec(
            lead + shard, lambda s: (0,) * len(lead) + (at, 0), pipeline_mode=pl.Buffered(1)
        )
    ] * len(packs)


def pack_outs(shard, single):
    if single:
        return [((32,) + shard, BF16, fixed((32,) + shard))]
    return [((4, 4) + shard, BF16, fixed((4, 4) + shard))] * 2


def attention_forward(layer, at, grid_field, strips, packs, small, base):
    out = call(
        partial(attention_forward_kernel, layer, len(packs)),
        (at, grid_field, *strips, *packs, small, base),
        [SCALARS, fixed(GRID) if layer else GRID_STEP]
        + STRIP_SPECS[: len(strips)]
        + pack_specs(packs, SHARD_A)
        + [fixed(small.shape), fixed(base.shape)],
        [((ROWS, D), F32, ROWS_STEP)] * layer
        + [
            ((STEPS * STEP_WINDOWS, AROWS, 3 * D), BF16, WINDOWS_STEP),
            ((STEPS * STEP_WINDOWS, 2, 4 * AROWS, LANES), BF16, PROBS_STEP),
            ((ROWS, D), BF16, ROWS_STEP),
            ((ROWS, D), F32, ROWS_STEP),
        ],
        [
            pltpu.VMEM((3 * D, D), BF16),
            pltpu.VMEM((D, D), BF16),
            tiles_of(3 * D),
            tiles_of(D),
            pltpu.VMEM((4 if layer else 1, 2, 4, WROWS, 2 * AROWS), F32),
        ]
        + [MOVED] * layer,
        2 * ROWS * 4 * D * D * 2,
        30e6,
    )
    return (list(out[:-1]) if layer else [grid_field] + list(out[:-1])), out[-1]


def attention_backward(layer, at, grad_mid, saved, packs, small, rest, single):
    outs = pack_outs(SHARD_A, single)
    out = call(
        partial(attention_backward_kernel, layer, len(packs), len(outs)),
        (at, grad_mid, *saved, *packs, small, rest),
        [
            SCALARS,
            ROWS_STEP,
            ROWS_STEP if layer else GRID_STEP,
            WINDOWS_STEP,
            PROBS_STEP,
            ROWS_STEP,
        ]
        + pack_specs(packs, SHARD_A)
        + [fixed(small.shape), fixed(rest.shape)],
        [(GRID, F32, GRID_STEP)]
        + STRIP_OUTS[: 3 * layer]
        + outs
        + [
            ((HEADS, WROWS, AROWS), F32, fixed((HEADS, WROWS, AROWS))),
            ((1, ROW_SUMS), F32, fixed((1, ROW_SUMS))),
        ],
        [
            pltpu.VMEM((3 * D, D), BF16),
            pltpu.VMEM((D, D), BF16),
            tiles_of(D),
            tiles_of(3 * D),
            pltpu.VMEM((3 * D, D), F32),
            pltpu.VMEM((D, D), F32),
            pltpu.VMEM((2, 4, WROWS, 2 * AROWS), F32),
        ],
        2 * ROWS * 4 * D * D * 5,
        30e6,
    )
    at_pack = 1 + 3 * layer
    return out[0], out[1:at_pack], out[at_pack:-2], out[-2], out[-1]


MLP_WEIGHTS = [pltpu.VMEM((D, MLP), BF16), pltpu.VMEM((CHUNKS, D, CHUNK), BF16)]


def mlp_forward(layer, at, mid, packs, small):
    out = call(
        partial(mlp_forward_kernel, layer, len(packs)),
        (at, mid, *packs, small),
        [SCALARS, ROWS_STEP] + pack_specs(packs, SHARD_B) + [fixed(small.shape)],
        [(GRID, F32, GRID_STEP)]
        + STRIP_OUTS
        + [((CHUNKS, ROWS, CHUNK), BF16, HIDDEN_STEP)] * 2,
        MLP_WEIGHTS,
        2 * ROWS * 2 * D * MLP,
        26e6,
    )
    return out[0], out[1:4], out[4:]


def mlp_backward(layer, at, mid, dy, strips, saved, packs, small, single):
    outs = pack_outs(SHARD_B, single)
    forward = not saved
    extra = 4 if forward else 0
    out = call(
        partial(mlp_backward_kernel, layer, forward, len(packs), len(outs)),
        (at, mid, dy, *strips, *saved, *packs, small),
        [SCALARS, ROWS_STEP, fixed(GRID)]
        + STRIP_SPECS
        + [HIDDEN_STEP] * len(saved)
        + pack_specs(packs, SHARD_B)
        + [fixed(small.shape)],
        ([(GRID, F32, fixed(GRID))] + STRIP_OUTS)[:extra]
        + [((ROWS, D), F32, ROWS_STEP)]
        + outs
        + [((1, ROW_SUMS), F32, fixed((1, ROW_SUMS)))],
        MLP_WEIGHTS
        + [pltpu.VMEM((D, MLP), F32), pltpu.VMEM((CHUNKS, D, CHUNK), F32), MOVED],
        2 * ROWS * (6 if forward else 4) * D * MLP,
        30e6,
    )
    return out[:extra], out[extra], out[extra + 1 : -1], out[-1]


def moved(x, step_of):
    sizes = [lax.axis_size(axis) for axis in AXES]

    def flat(i, r, c):
        return (i * sizes[1] + r) * sizes[2] + c

    pairs = [
        (flat(i, r, c), flat(*step_of(i, r, c)))
        for i in range(sizes[0])
        for r in range(sizes[1])
        for c in range(sizes[2])
    ]
    return lax.ppermute(x, AXES, pairs)


def swapped(x, img=0, down=0, core=0, across=0):
    return moved(x, lambda i, r, c: (i ^ img, r ^ (2 * down + core), c ^ across))


def send_strips(strips, by):
    rows, cols = lax.axis_size("row"), lax.axis_size("col")
    low, right, corner = strips
    return (
        moved(low, lambda i, r, c: (i, (r + by) % rows, c)),
        moved(right, lambda i, r, c: (i, r, (c + by) % cols)),
        moved(corner, lambda i, r, c: (i, (r + by) % rows, (c + by) % cols)),
    )


def fill_prev(grid_field, strips):
    high, left, corner = (strip.astype(F32) for strip in strips)
    grid_field = lax.dynamic_update_slice(grid_field, high, (0, SHIFT, 0, 0))
    grid_field = lax.dynamic_update_slice(grid_field, left, (SHIFT, 0, 0, 0))
    return lax.dynamic_update_slice(grid_field, corner, (0, 0, 0, 0))


QUADS = ((0, 0), (0, 1), (1, 0), (1, 1))


def after(values, *others):
    return lax.optimization_barrier((values, others))[0]


def together(*values):
    return lax.optimization_barrier(values)


def is_small():
    return lax.axis_size("img") == 2


def gather_line(pack):
    if not is_small():
        return pack
    return jnp.stack([pack] + [swapped(pack, across=m) for m in (1, 2, 3)])


def gather_quad(line):
    return jnp.stack([line] + [swapped(line, img=i, down=y) for i, y in QUADS[1:]])


def gather_whole(pack, canonical):
    whole = lax.all_gather(pack, AXES, axis=0, tiled=False)
    if not is_small():
        whole = canonical(whole.reshape((lax.axis_size("img"), 16) + pack.shape))
        whole = whole.reshape((32,) + whole.shape[2:])
    return (whole,)


def gather_swaps(line, canonical):
    if not is_small():
        return gather_whole(line, canonical)
    quad = gather_quad(line)
    return quad, swapped(quad, core=1)


def scatter_whole(whole, in_shards):
    if not is_small():
        whole = in_shards(whole.reshape((2, 16) + whole.shape[1:]), lax.axis_size("img"))
    flat = whole.reshape(-1, whole.shape[-1])
    return lax.psum_scatter(flat, AXES, scatter_dimension=0, tiled=True)


def scatter_plane(whole):
    if not is_small():
        return whole
    flat = whole.reshape(-1, whole.shape[-1])
    part = lax.psum_scatter(flat, ("img", "row"), scatter_dimension=0, tiled=True)
    return part.reshape((4,) + whole.shape[1:])


def scatter_cols(parts):
    rows = parts[0].shape[1]
    if not is_small():
        return [scatter_whole(part, in_shards) for part, in_shards in zip(parts, (mlp_shards, attention_shards))]
    flat = jnp.concatenate(parts, axis=1).reshape(-1, parts[0].shape[-1])
    whole = lax.psum_scatter(flat, "col", scatter_dimension=0, tiled=True)
    return [whole[:rows], whole[rows:]]


def pair_swap(packs):
    return swapped(packs[1], core=1) if is_small() else packs


def scatter_pair(packs, got):
    if not is_small():
        return packs
    half = packs[0].astype(F32) + got.astype(F32)
    return [half[0]] + [half[m].astype(BF16) for m in (1, 2, 3)]


def quad_swaps(halves):
    if not is_small():
        return []
    return [swapped(h, img=i, down=y) for h, (i, y) in zip(halves[1:], QUADS[1:])]


def scatter_quad(halves, got):
    if not is_small():
        return halves
    got = [g.astype(F32) for g in got]
    line = (halves[0] + got[0]) + (got[1] + got[2])
    return line[:2], line[2:].astype(BF16)


def far_swap(line):
    return swapped(line[1], across=2) if is_small() else line


def scatter_far(line, got):
    if not is_small():
        return line
    ends = line[0] + got.astype(F32)
    return ends[0], ends[1].astype(BF16)


def near_swap(ends):
    return swapped(ends[1], across=1) if is_small() else ends


def scatter_near(ends, got, in_shards):
    if is_small():
        return ends[0] + got.astype(F32)
    return scatter_whole(ends[0], in_shards).astype(F32)


SUM_STEPS = ({"core": 1}, {"img": 1}, {"down": 1}, {"across": 2}, {"across": 1})


def padded_index(rel_index):
    cells = rel_index.T.reshape(WIN, WIN, WIN, WIN)
    gap = (0, SLOT - WIN)
    cells = jnp.pad(cells, [(0, 0), gap, (0, AROWS // SLOT - WIN), gap], constant_values=-1)
    return cells.reshape(1, WROWS * AROWS)


def packing_kernel(w_qkv, w_proj, w_fc1, w_fc2, first_a, second_a, first_b, second_b):
    for l, (pack_a, pack_b) in enumerate(((first_a, first_b), (second_a, second_b))):
        pack_a[:N_QKV] = w_qkv[l].astype(BF16)
        pack_a[N_QKV:] = w_proj[l].astype(BF16)
        for h in range(2):
            pack_b[:N_FC1, h * LANES : (h + 1) * LANES] = w_fc1[
                l, h * LANES : (h + 1) * LANES, :
            ].astype(BF16)
        for k in range(4):
            pack_b[N_FC1 + k * N_OUT : N_FC1 + (k + 1) * N_OUT] = w_fc2[
                l, :, k * HALF : (k + 1) * HALF
            ].astype(BF16)


def turned(matrices):
    w_qkv, w_proj, w_fc1, w_fc2 = matrices
    return w_qkv.swapaxes(1, 2), w_proj.swapaxes(1, 2), w_fc1, w_fc2.swapaxes(1, 2)


def make_packs(masters):
    w_qkv, w_proj, w_fc1, w_fc2 = turned(masters)
    if is_small():
        kinds = [jax.ShapeDtypeStruct(shape, BF16) for shape in (SHARD_A, SHARD_A, SHARD_B, SHARD_B)]
        return pl.pallas_call(
            packing_kernel,
            out_shape=kinds,
            compiler_params=pltpu.CompilerParams(vmem_limit_bytes=VMEM_LIMIT),
        )(w_qkv, w_proj, w_fc1, w_fc2)
    cols = w_qkv.shape[2]
    packs = [jnp.concatenate([w_qkv[l], w_proj[l]], axis=0).astype(BF16) for l in range(2)]
    for l in range(2):
        second = w_fc2[l].reshape(N_OUT, 4, cols).transpose(1, 0, 2).reshape(-1, cols)
        packs.append(jnp.concatenate([w_fc1[l].T, second], axis=0).astype(BF16))
    return packs


def update_kernel(kinds, rates, *refs):
    sums, refs = refs[:3], refs[3:]
    count = len(rates)
    ins, outs = refs[: 3 * count], refs[3 * count :]
    for l in range(2):
        total = sums[0][...] + sums[1][...].astype(F32) if l == 0 else sums[2][...].astype(F32)
        for k, grad in enumerate(kinds(total)):
            rate, decay = rates[k]
            new = adam_step(*(ins[3 * k + m][l] for m in range(3)), grad, rate, decay)
            for m in range(3):
                outs[3 * k + m][l] = new[m]


def attention_kinds(total):
    return total[:N_QKV], total[N_QKV:]


def mlp_kinds(total):
    first = jnp.concatenate([total[:N_FC1, :LANES], total[:N_FC1, LANES:]], axis=0)
    second = [total[N_FC1 + k * N_OUT : N_FC1 + (k + 1) * N_OUT] for k in range(4)]
    return first, jnp.concatenate(second, axis=1)


def update(kinds, sums, arrays):
    rates = ((RATE_MATRIX, DECAY_MATRIX),) * (len(arrays) // 3)
    return pl.pallas_call(
        partial(update_kernel, kinds, rates),
        out_shape=[jax.ShapeDtypeStruct(x.shape, F32) for x in arrays],
        compiler_params=pltpu.CompilerParams(vmem_limit_bytes=VMEM_LIMIT),
    )(*sums, *arrays)


def attention_canonical(whole):
    _, ranks, rows, _ = whole.shape
    whole = whole.transpose(1, 2, 0, 3).reshape(ranks, rows, 2, HALF)
    return whole.transpose(2, 0, 1, 3)


def attention_shards(pack, size):
    _, ranks, rows, _ = pack.shape
    pack = pack.transpose(1, 2, 0, 3).reshape(ranks, rows, size, D // size)
    return pack.transpose(2, 0, 1, 3)


def mlp_canonical(whole):
    size, ranks, _, cols = whole.shape
    first = attention_canonical(whole[:, :, :N_FC1]).swapaxes(2, 3)
    first = first.reshape(2, ranks, 2, LANES, N_FC1).transpose(0, 1, 3, 2, 4).reshape(2, ranks, LANES, HALF)
    second = whole[:, :, N_FC1:].reshape(size, ranks, 4, N_OUT, cols)
    second = second.transpose(1, 3, 0, 2, 4).reshape(ranks, N_OUT, 2, 4, HALF)
    second = second.transpose(2, 0, 3, 1, 4).reshape(2, ranks, 4 * N_OUT, HALF)
    return jnp.concatenate([first, second], axis=2)


def mlp_shards(pack, size):
    _, ranks, _, _ = pack.shape
    cols = D // size
    first = pack[:, :, :N_FC1].reshape(2, ranks, LANES, 2, N_FC1).transpose(0, 1, 3, 2, 4)
    first = attention_shards(first.reshape(2, ranks, HALF, N_FC1).swapaxes(2, 3), size)
    second = pack[:, :, N_FC1:].reshape(2, ranks, 4, N_OUT, HALF)
    second = second.transpose(1, 3, 0, 2, 4).reshape(ranks, N_OUT, size, 4, cols)
    second = second.transpose(2, 0, 3, 1, 4).reshape(size, ranks, 4 * N_OUT, cols)
    return jnp.concatenate([first, second], axis=2)


def adam_step(weight, moment_one, second, gradient, rate_value, decay_rate):
    moment_one = BETA_ONE * moment_one + (1.0 - BETA_ONE) * gradient
    second = BETA_TWO * second + (1.0 - BETA_TWO) * gradient * gradient
    update = (
        moment_one / (1.0 - BETA_ONE**STEP) / (jnp.sqrt(second / (1.0 - BETA_TWO**STEP)) + EPS_ADAM)
    )
    return (weight - rate_value * (update + decay_rate * weight), moment_one, second)


def shards(
    images,
    grad_out,
    w_qkv,
    w_proj,
    w_fc1,
    w_fc2,
    first_qkv,
    first_proj,
    first_fc1,
    first_fc2,
    second_qkv,
    second_proj,
    second_fc1,
    second_fc2,
    small_params,
    small_first,
    small_second,
    rel_index,
):
    assert images.shape == (IMAGES, SIDE, SIDE, D)
    size = lax.axis_size("img")
    small = is_small()
    row, col = lax.axis_index("row"), lax.axis_index("col")
    last = [row == lax.axis_size("row") - 1, col == lax.axis_size("col") - 1]
    place = [lax.axis_index("img"), row // 2, row % 2, col]
    at = jnp.stack([jnp.asarray(value, jnp.int32) for value in place + last])
    images = images.transpose(1, 2, 0, 3)
    grad_out = grad_out.transpose(1, 2, 0, 3)

    masters = (w_qkv, w_proj, w_fc1, w_fc2)
    pack_a_zero, pack_a_one, pack_b_zero, pack_b_one = make_packs(masters)
    packs_b_zero = gather_whole(pack_b_zero, mlp_canonical)
    packs_b_one = gather_whole(pack_b_one, mlp_canonical)
    line, near = together(gather_line(pack_a_zero), near_swap((None, pack_a_one)))
    packs_a_zero = gather_swaps(line, attention_canonical)
    pair = jnp.stack([pack_a_one, near]) if small else pack_a_one

    onehot = (
        jnp.arange(RELPOS, dtype=jnp.int32)[:, None] == padded_index(rel_index)
    ).astype(F32)
    tables = small_params[:, 9 * D + MLP :].reshape(2, RELPOS, HEADS)
    base = jnp.einsum("lrh,rp->lhp", tables * LOG2E, onehot, precision=lax.Precision.HIGHEST)
    base = base.reshape(2, HEADS, WROWS, AROWS)
    grad_strips = (
        grad_out[:SHIFT, SHIFT:].astype(BF16),
        grad_out[SHIFT:, :SHIFT].astype(BF16),
        grad_out[:SHIFT, :SHIFT].astype(BF16),
    )

    def table_row(sums, dtab):
        table = jnp.einsum(
            "hp,rp->rh", dtab.reshape(HEADS, -1), onehot, precision=lax.Precision.HIGHEST
        )
        return jnp.concatenate([sums, table.reshape(1, -1)], axis=1)

    packs_a_zero = after(packs_a_zero, base, grad_strips)
    saved_zero, mid_zero = attention_forward(0, at, images, (), packs_a_zero, small_params, base[0])
    mid_zero, grad_strips, far = together(
        mid_zero, send_strips(grad_strips, -1), far_swap((None, pair))
    )
    line = jnp.concatenate([pair, far]) if small else pair
    out_zero, strips, hidden_zero = mlp_forward(0, at, mid_zero, packs_b_zero, small_params)
    strips, got = together(strips, quad_swaps([line] * 4))
    quad = jnp.stack([line, *got]) if small else line
    strips, other = together(send_strips(strips, -1), pair_swap((None, quad)))
    packs_a_one = (quad, other) if small else gather_whole(quad, attention_canonical)
    saved_one, mid_one = attention_forward(
        1, at, out_zero, strips, packs_a_one, small_params, base[1]
    )
    (out_one, *out_strips), gm_one, dpacks, rest = mlp_backward(
        1, at, mid_one, grad_out, grad_strips, (), packs_b_one, small_params, True
    )

    plane_b_one = scatter_plane(dpacks[0])
    dx_one, strips, dpacks, dtab_one, sums = attention_backward(
        1, at, gm_one, saved_one, packs_a_one, small_params, rest, True
    )
    plane_a_one = scatter_plane(dpacks[0])
    strips, plane_b_one, row_one = together(
        send_strips(strips, 1), plane_b_one, table_row(sums, dtab_one)
    )
    out_strips = send_strips(after(out_strips, strips), 1)
    _, gm_zero, dpacks, rest = mlp_backward(
        0, at, mid_zero, dx_one, strips, hidden_zero, packs_b_zero, small_params, not small
    )

    dpacks, out_strips = together(dpacks, out_strips)
    got, out_one = together(pair_swap(dpacks), fill_prev(out_one, out_strips))
    outputs = out_one.transpose(2, 0, 1, 3)
    halves_b_zero = scatter_pair(dpacks, got)
    gm_zero, halves_b_zero, plane_a_one = together(gm_zero, halves_b_zero, plane_a_one)
    sums_one = scatter_cols((plane_b_one, plane_a_one))
    grad_input, _, dpacks, dtab_zero, sums = attention_backward(
        0, at, gm_zero, saved_zero, packs_a_zero, small_params, rest, not small
    )
    grad_input = grad_input.transpose(2, 0, 1, 3)

    dpacks, got, sums_one = together(dpacks, quad_swaps(halves_b_zero), sums_one)
    line_b = scatter_quad(halves_b_zero, got)
    got, row_zero = together(pair_swap(dpacks), table_row(sums, dtab_zero))
    halves_a = scatter_pair(dpacks, got)
    small_grad = jnp.concatenate([row_zero, row_one], axis=0)

    def small_swaps(*steps):
        return [swapped(small_grad, **step) for step in steps] if small else []

    got, far, parts = together(quad_swaps(halves_a), far_swap(line_b), small_swaps({"core": 1}))
    line_a = scatter_quad(halves_a, got)
    ends_b = scatter_far(line_b, far)
    small_grad = sum(parts, small_grad)
    steps = [{"img": i, "down": y} for i, y in QUADS[1:]]
    far, near_b, parts = together(far_swap(line_a), near_swap(ends_b), small_swaps(*steps))
    ends_a = scatter_far(line_a, far)
    if small:
        small_grad = (small_grad + parts[0]) + (parts[1] + parts[2])
    near_a, parts = together(near_swap(ends_a), small_swaps(*({"across": m} for m in (1, 2, 3))))
    if small:
        small_grad = (small_grad + parts[0]) + (parts[1] + parts[2])
    else:
        small_grad = lax.psum(small_grad, AXES)

    states = [turned(group) for group in (
        masters,
        (first_qkv, first_proj, first_fc1, first_fc2),
        (second_qkv, second_proj, second_fc1, second_fc2),
    )]
    if small:
        new_a = update(
            attention_kinds, (ends_a[0], near_a, sums_one[1]), [s[k] for k in (0, 1) for s in states]
        )
        new_b = update(
            mlp_kinds, (ends_b[0], near_b, sums_one[0]), [s[k] for k in (2, 3) for s in states]
        )
    else:
        cols = D // size
        total_a = [scatter_whole(ends_a[0], attention_shards), sums_one[1]]
        total_b = [scatter_whole(ends_b[0], mlp_shards), sums_one[0]]
        kinds = (
            [t[:N_QKV] for t in total_a],
            [t[N_QKV:] for t in total_a],
            [t[:N_FC1].T for t in total_b],
            [t[N_FC1:].reshape(4, N_OUT, cols).transpose(1, 0, 2).reshape(N_OUT, -1) for t in total_b],
        )
        new = []
        for k in range(4):
            grad = jnp.stack(kinds[k]).astype(F32)
            new += adam_step(*(s[k] for s in states), grad, RATE_MATRIX, DECAY_MATRIX)
        new_a, new_b = new[:6], new[6:]
    small_new = adam_step(small_params, small_first, small_second, small_grad, RATE_SMALL, 0.0)
    new = list(new_a) + list(new_b)
    new = [turned(new[m::3]) for m in range(3)]
    return (outputs, grad_input) + new[0] + new[1] + new[2] + tuple(small_new)


def solution(mesh):
    grid_spec = P("img", "row", "col", None)
    matrix = P(None, "img", ("row", "col"))
    in_specs = (grid_spec,) * 2 + (matrix,) * 12 + (P(),) * 4
    out_specs = (grid_spec,) * 2 + (matrix,) * 12 + (P(),) * 3
    return jax.shard_map(shards, mesh=mesh, in_specs=in_specs, out_specs=out_specs, check_vma=False)
```

```python
from functools import partial

import jax
import jax.numpy as jnp
from jax import lax
from jax.experimental import pallas as pl
from jax.experimental.pallas import tpu as pltpu
from jax.sharding import PartitionSpec as P

D = 512
HEADS = 16
HEAD_DIM = 32
MLP = 2048
WIN = 7
SHIFT = 3
STEP = 10
RELPOS = 169

EPS_NORM = 1e-05
BETA_ONE = 0.9
BETA_TWO = 0.999
EPS_ADAM = 1e-08
RATE_MATRIX = 0.05
RATE_SMALL = 0.3
DECAY_MATRIX = 0.05
MASKED = -1e30

AXES = ("img", "row", "col")
F32 = jnp.float32
BF16 = jnp.bfloat16
LOG2E = 1.4426950408889634
SCALE = HEAD_DIM ** (-0.5)

SIDE = 2 * WIN
IMAGES = 8
SLOT = 8
WROWS = WIN * SLOT
AROWS = 64
STEPS = 2
STEP_ROWS = WIN * SIDE * IMAGES
ROWS = STEPS * STEP_ROWS
STEP_WINDOWS = 2 * IMAGES
KEPT = SIDE - SHIFT
CHUNK = 512
CHUNKS = MLP // CHUNK
HALF = D // 2
LANES = 128
VMEM_LIMIT = 60 * 1024 * 1024


def mm(left, right):
    return lax.dot_general(left, right, (((1,), (0,)), ((), ())), preferred_element_type=F32)


def mm_t(left, right):
    return lax.dot_general(left, right, (((1,), (1,)), ((), ())), preferred_element_type=F32)


def t_mm(left, right):
    return lax.dot_general(left, right, (((0,), (0,)), ((), ())), preferred_element_type=F32)


def col_sum(value):
    return jnp.sum(value, axis=0, keepdims=True)


def normalize(rows):
    center = rows - jnp.mean(rows, axis=-1, keepdims=True)
    spread = jnp.mean(center * center, axis=-1, keepdims=True)
    rstd = lax.rsqrt(spread + EPS_NORM)
    return center * rstd, rstd


def norm_back(grad, xhat, rstd, gain):
    scaled = grad * gain
    mean_one = jnp.mean(scaled, axis=-1, keepdims=True)
    mean_two = jnp.mean(scaled * xhat, axis=-1, keepdims=True)
    return rstd * (scaled - mean_one - xhat * mean_two)


def gelu_both(pre):
    pre = pre.astype(BF16)
    t = 1.0 / (1.0 + jnp.abs(pre) * (0.3275911 * 0.7071067811865476))
    bell = jnp.exp2(pre * pre * (-0.5 * LOG2E))
    poly = t * (0.5 * 1.061405429) + 0.5 * -1.453152027
    poly = poly * t + 0.5 * 1.421413741
    poly = poly * t + 0.5 * -0.284496736
    poly = poly * t + 0.5 * 0.254829592
    tail = poly * t * bell
    cdf = jnp.where(pre >= 0.0, 1.0 - tail, tail)
    return pre * cdf, cdf + pre * bell * 0.3989422804014327


def both_steps(body):
    for a in range(STEPS):
        pl.when(pl.program_id(0) == a)(partial(body, a))


def next_rows(grid_ref, strip_refs, rows_ref):
    low_ref, right_ref, corner_ref = strip_refs

    def body(a):
        if a == 0:
            rows_ref[:, :KEPT] = grid_ref[SHIFT : SHIFT + WIN, SHIFT:]
            rows_ref[:, KEPT:] = right_ref[:WIN].astype(F32)
        else:
            rows_ref[: WIN - SHIFT, :KEPT] = grid_ref[SHIFT + WIN :, SHIFT:]
            rows_ref[: WIN - SHIFT, KEPT:] = right_ref[WIN:].astype(F32)
            rows_ref[WIN - SHIFT :, :KEPT] = low_ref[...].astype(F32)
            rows_ref[WIN - SHIFT :, KEPT:] = corner_ref[...].astype(F32)

    both_steps(body)
    return rows_ref[...].reshape(STEP_ROWS, D)


def prev_rows(grid_ref, strip_refs, rows_ref):
    high_ref, left_ref, corner_ref = strip_refs

    def body(a):
        if a == 0:
            rows_ref[:SHIFT, SHIFT:] = high_ref[...].astype(F32)
            rows_ref[:SHIFT, :SHIFT] = corner_ref[...].astype(F32)
            rows_ref[SHIFT:, SHIFT:] = grid_ref[: WIN - SHIFT, :KEPT]
            rows_ref[SHIFT:, :SHIFT] = left_ref[: WIN - SHIFT].astype(F32)
        else:
            rows_ref[:, SHIFT:] = grid_ref[WIN - SHIFT : KEPT, :KEPT]
            rows_ref[:, :SHIFT] = left_ref[WIN - SHIFT :].astype(F32)

    both_steps(body)
    return rows_ref[...].reshape(STEP_ROWS, D)


def first_strips(block_ref, strip_refs):
    rows_ref, cols_ref, corner_ref = strip_refs

    def body(a):
        if a == 0:
            rows_ref[...] = block_ref[:SHIFT, SHIFT:].astype(BF16)
            cols_ref[: WIN - SHIFT] = block_ref[SHIFT:, :SHIFT].astype(BF16)
            corner_ref[...] = block_ref[:SHIFT, :SHIFT].astype(BF16)
        else:
            cols_ref[WIN - SHIFT :] = block_ref[:, :SHIFT].astype(BF16)

    both_steps(body)


def last_strips(block_ref, strip_refs):
    rows_ref, cols_ref, corner_ref = strip_refs

    def body(a):
        if a == 0:
            cols_ref[:WIN] = block_ref[:, KEPT:].astype(BF16)
        else:
            cols_ref[WIN:] = block_ref[: WIN - SHIFT, KEPT:].astype(BF16)
            rows_ref[...] = block_ref[WIN - SHIFT :, :KEPT].astype(BF16)
            corner_ref[...] = block_ref[WIN - SHIFT :, KEPT:].astype(BF16)

    both_steps(body)


def put_tiles(tiles, first, value):
    for t in range(value.shape[1] // LANES):
        tiles[first + t, :STEP_ROWS, :] = value[:, t * LANES : (t + 1) * LANES]


def get_tiles(tiles, first, count):
    return jnp.concatenate([tiles[first + t, :STEP_ROWS, :] for t in range(count)], axis=1)


def clear_tail(tiles):
    tiles[:, STEP_ROWS:, :] = jnp.zeros(tiles[:, STEP_ROWS:, :].shape, F32)


def window_at(b, n, r):
    return b * WIN * IMAGES + r * SIDE * IMAGES + n


def get_window(tiles, first, b, n):
    return jnp.concatenate(
        [
            jnp.concatenate(
                [
                    tiles[first + t, pl.ds(window_at(b, n, r), SLOT, stride=IMAGES), :]
                    for r in range(WIN)
                ],
                axis=0,
            )
            for t in range(2)
        ],
        axis=1,
    )


def put_window(tiles, first, b, n, value):
    for t in range(2):
        for r in range(WIN):
            tiles[first + t, pl.ds(window_at(b, n, r), WIN, stride=IMAGES), :] = value[
                r * SLOT : r * SLOT + WIN, t * LANES : (t + 1) * LANES
            ]


def to_sixty_four(window):
    padding = jnp.zeros((AROWS - WROWS, window.shape[1]), F32)
    return jnp.concatenate([window, padding], axis=0).astype(BF16)


def head_masks():
    lane = lax.broadcasted_iota(jnp.int32, (16, HALF), 1)
    head = jnp.bitwise_and(lax.shift_right_logical(lane, 5), 3)
    return [jnp.where(head == a, 1.0, 0.0).astype(BF16) for a in range(4)]


def stack_heads(part, masks):
    split = part.reshape(AROWS // 16, 16, HALF)
    return jnp.concatenate(
        [(split * mask[None]).reshape(AROWS, HALF) for mask in masks], axis=0
    )


def stack_halves(part):
    zero = jnp.zeros((AROWS, HALF // 2), part.dtype)
    return jnp.concatenate(
        [
            jnp.concatenate([part[:, : HALF // 2], zero], axis=1),
            jnp.concatenate([zero, part[:, HALF // 2 :]], axis=1),
        ],
        axis=0,
    )


def pick_halves(result):
    return jnp.concatenate(
        [result[:WROWS, : HALF // 2], result[AROWS : AROWS + WROWS, HALF // 2 :]], axis=1
    )


def pick_heads(result):
    lane = lax.broadcasted_iota(jnp.int32, (WROWS, HALF), 1)
    head = jnp.bitwise_and(lax.shift_right_logical(lane, 5), 3)
    picked = result[3 * AROWS : 3 * AROWS + WROWS]
    for a in (2, 1, 0):
        picked = jnp.where(head == a, result[a * AROWS : a * AROWS + WROWS], picked)
    return picked


def pad_keys(value):
    padding = jnp.zeros((4, AROWS - WROWS, 128), F32)
    return jnp.concatenate([value, padding], axis=1).astype(BF16).reshape(4 * AROWS, 128)


def places(at_ref, packs):
    if len(packs) == 1:
        for shard in range(packs[0].shape[0]):
            yield 0, (shard,), shard // 16, shard % 16
        return
    for core in range(2):
        for quad in range(4):
            for across in range(4):
                i = jnp.bitwise_xor(at_ref[0], quad >> 1)
                y = jnp.bitwise_xor(at_ref[1], quad & 1)
                c = jnp.bitwise_xor(at_ref[2], core)
                z = jnp.bitwise_xor(at_ref[3], across)
                yield core, (quad, across), i, (2 * y + c) * 4 + z


def piece(start, length):
    if isinstance(start, int):
        return pl.ds(start * length, length)
    return pl.ds(pl.multiple_of(start * length, length), length)


N_QKV = 3 * D // 16
N_OUT = D // 16
N_FC1 = MLP // 16


def unpack_attention(at_ref, packs, w_qkv, w_proj):
    for core, at, i, r in places(at_ref, packs):
        cols = piece(i, HALF)
        w_qkv[piece(r, N_QKV), cols] = packs[core][at + (slice(0, N_QKV),)]
        w_proj[piece(r, N_OUT), cols] = packs[core][at + (slice(N_QKV, None),)]


def pack_attention(at_ref, g_qkv, g_proj, packs):
    for core, at, i, r in places(at_ref, packs):
        cols = piece(i, HALF)
        packs[core][at + (slice(0, N_QKV),)] = g_qkv[piece(r, N_QKV), cols].astype(BF16)
        packs[core][at + (slice(N_QKV, None),)] = g_proj[piece(r, N_OUT), cols].astype(BF16)


def unpack_mlp(at_ref, packs, w_one, w_two):
    for core, at, i, r in places(at_ref, packs):
        for h in range(2):
            w_one[piece(2 * i + h, LANES), piece(r, N_FC1)] = packs[core][
                at + (slice(0, N_FC1), slice(h * LANES, (h + 1) * LANES))
            ]
        for k in range(4):
            w_two[2 * i + k // 2, piece(r, N_OUT), (k % 2) * HALF : (k % 2 + 1) * HALF] = packs[core][
                at + (slice(N_FC1 + k * N_OUT, N_FC1 + (k + 1) * N_OUT),)
            ]


def pack_mlp(at_ref, g_one, g_two, packs):
    for core, at, i, r in places(at_ref, packs):
        for h in range(2):
            packs[core][at + (slice(0, N_FC1), slice(h * LANES, (h + 1) * LANES))] = g_one[
                piece(2 * i + h, LANES), piece(r, N_FC1)
            ].astype(BF16)
        for k in range(4):
            packs[core][at + (slice(N_FC1 + k * N_OUT, N_FC1 + (k + 1) * N_OUT),)] = g_two[
                2 * i + k // 2, piece(r, N_OUT), (k % 2) * HALF : (k % 2 + 1) * HALF
            ].astype(BF16)


def spread_bias(layer, at_ref, base_ref, bias):
    row = lax.broadcasted_iota(jnp.int32, (WROWS, 2 * AROWS), 0)
    lane = jnp.bitwise_and(lax.broadcasted_iota(jnp.int32, (WROWS, 2 * AROWS), 1), AROWS - 1)
    key_row, key_col = row // SLOT, jnp.bitwise_and(row, SLOT - 1)
    query_row, query_col = lane // SLOT, jnp.bitwise_and(lane, SLOT - 1)
    kept = WIN - SHIFT
    other_row = ((key_row >= kept) != (query_row >= kept)).astype(jnp.int32)
    other_col = ((key_col >= kept) != (query_col >= kept)).astype(jnp.int32)
    padding = (key_col == WIN).astype(jnp.int32)
    for v in range(bias.shape[0]):
        hidden = padding
        if layer == 1:
            if v >> 1:
                hidden = hidden + other_row * at_ref[4]
            if v & 1:
                hidden = hidden + other_col * at_ref[5]
        for g in range(2):
            for a in range(4):
                both = jnp.concatenate([base_ref[8 * g + a], base_ref[8 * g + 4 + a]], axis=1)
                bias[v, g, a] = jnp.where(hidden > 0, MASKED, both)


def attention_forward_kernel(layer, n_packs, at_ref, x_ref, *refs):
    strips, refs = refs[: 3 * layer], refs[3 * layer :]
    packs, refs = refs[:n_packs], refs[n_packs:]
    small_ref, base_ref, refs = refs[0], refs[1], refs[2:]
    if layer:
        xs_ref, refs = refs[0], refs[1:]
    qkv_ref, p_ref, att_ref, mid_ref, w_qkv, w_proj, tiles, att_tiles, bias_ref, *moved = refs
    step = pl.program_id(0)

    @pl.when(step == 0)
    def _():
        unpack_attention(at_ref, packs, w_qkv, w_proj)
        spread_bias(layer, at_ref, base_ref, bias_ref)
        clear_tail(tiles)

    gain = small_ref[layer : layer + 1, 0:D]
    shift = small_ref[layer : layer + 1, D : 2 * D]
    if layer:
        rows = next_rows(x_ref, strips, moved[0])
        xs_ref[...] = rows
    else:
        rows = x_ref[...].reshape(STEP_ROWS, D)
    xhat, _ = normalize(rows)
    normed = (xhat * gain + shift).astype(BF16)
    for part in range(3):
        cols = slice(part * D, (part + 1) * D)
        bias = small_ref[layer : layer + 1, 6 * D + part * D : 7 * D + part * D]
        put_tiles(tiles, 4 * part, mm_t(normed, w_qkv[cols, :]) + bias)
    masks = head_masks()
    lane = jnp.bitwise_and(lax.broadcasted_iota(jnp.int32, (4, 1, LANES), 2), AROWS - 1)
    no_query = (jnp.bitwise_and(lane, SLOT - 1) == WIN) | (lane >= WROWS)

    def windows(pair, carry):
        places_of = [(b, g, 2 * pair + k) for k in range(2) for b in range(2) for g in range(2)]
        scores, values = [], []
        for b, g, n in places_of:
            q, key, val = (
                to_sixty_four(get_window(tiles, 4 * part + 2 * g, b, n)) for part in range(3)
            )
            for part, value in enumerate((q, key, val)):
                at = part * D + g * HALF
                qkv_ref[b * IMAGES + n, :, at : at + HALF] = value
            scores.append(mm_t(stack_heads(key, masks), stack_halves(q)))
            values.append(val)
        probs = []
        for (b, g, n), score in zip(places_of, scores):
            v = 2 * step + b if layer else 0
            score = score.reshape(4, AROWS, LANES)[:, :WROWS] * (SCALE * LOG2E) + bias_ref[v, g]
            powers = jnp.exp2(score - jnp.max(score, axis=1, keepdims=True))
            total = jnp.sum(powers, axis=1, keepdims=True)
            prob = pad_keys(powers * jnp.where(no_query, 0.0, 1.0 / total))
            p_ref[b * IMAGES + n, g] = prob
            probs.append(prob)
        for (b, g, n), prob, val in zip(places_of, probs, values):
            put_window(att_tiles, 2 * g, b, n, pick_halves(t_mm(prob, stack_heads(val, masks))))
        return carry

    lax.fori_loop(0, IMAGES // 2, windows, 0)
    att = get_tiles(att_tiles, 0, 4).astype(BF16)
    att_ref[...] = att
    bias = small_ref[layer : layer + 1, 4 * D : 5 * D]
    mid_ref[...] = rows + (mm_t(att, w_proj[...]) + bias)


def attention_backward_kernel(layer, n_packs, n_out, at_ref, gm_ref, x_ref, qkv_ref, p_ref, att_ref, *refs):
    packs, refs = refs[:n_packs], refs[n_packs:]
    small_ref, rest_ref, dx_ref, refs = refs[0], refs[1], refs[2], refs[3:]
    strips, refs = refs[: 3 * layer], refs[3 * layer :]
    dpacks, refs = refs[:n_out], refs[n_out:]
    dtab_ref, dsmall_ref, w_qkv, w_proj, g_tiles, d_tiles, acc_qkv, acc_proj, acc_tab = refs
    step = pl.program_id(0)

    @pl.when(step == 0)
    def _():
        unpack_attention(at_ref, packs, w_qkv, w_proj)
        dsmall_ref[...] = rest_ref[...]
        clear_tail(g_tiles)
        for ref in (acc_tab, acc_qkv, acc_proj):
            ref[...] = jnp.zeros(ref.shape, ref.dtype)

    gain = small_ref[layer : layer + 1, 0:D]
    shift = small_ref[layer : layer + 1, D : 2 * D]
    grad_mid = gm_ref[...]
    mid_low = grad_mid.astype(BF16)
    dsmall_ref[:, 4 * D : 5 * D] += col_sum(mid_low.astype(F32))
    acc_proj[...] += t_mm(mid_low, att_ref[...])
    put_tiles(g_tiles, 0, mm(mid_low, w_proj[...]))
    masks = head_masks()

    def windows(pair, carry):
        places_of = [(b, g, 2 * pair + k) for k in range(2) for b in range(2) for g in range(2)]
        loaded, dprobs = [], []
        for b, g, n in places_of:
            w = b * IMAGES + n
            q, key, val = (
                qkv_ref[w, :, part * D + g * HALF : part * D + (g + 1) * HALF] for part in range(3)
            )
            grad = stack_halves(to_sixty_four(get_window(g_tiles, 2 * g, b, n)))
            dprobs.append(mm_t(stack_heads(val, masks), grad))
            loaded.append((q, key, grad, p_ref[w, g]))
        lows = []
        sums = [None, None]
        for (b, g, _), dprob, (_, _, _, prob) in zip(places_of, dprobs, loaded):
            dprob = dprob.reshape(4, AROWS, LANES)[:, :WROWS]
            p = prob.astype(F32).reshape(4, AROWS, LANES)[:, :WROWS]
            delta = jnp.sum(p * dprob, axis=1, keepdims=True)
            dscore = p * (dprob - delta)
            sums[g] = dscore if sums[g] is None else sums[g] + dscore
            lows.append(pad_keys(dscore))
        for g in range(2):
            acc_tab[g] += sums[g]
        for (b, g, n), low, (q, key, grad, prob) in zip(places_of, lows, loaded):
            put_window(d_tiles, 2 * g, b, n, pick_halves(t_mm(low, stack_heads(key, masks))) * SCALE)
            put_window(d_tiles, 4 + 2 * g, b, n, pick_heads(mm(low, stack_halves(q))) * SCALE)
            put_window(d_tiles, 8 + 2 * g, b, n, pick_heads(mm(prob, grad)))
        return carry

    lax.fori_loop(0, IMAGES // 2, windows, 0)
    xhat, rstd = normalize(x_ref[...].reshape(STEP_ROWS, D))
    normed = (xhat * gain + shift).astype(BF16)
    grad_normed = None
    for part in range(3):
        cols = slice(part * D, (part + 1) * D)
        low = get_tiles(d_tiles, 4 * part, 4).astype(BF16)
        dsmall_ref[:, 6 * D + part * D : 7 * D + part * D] += col_sum(low.astype(F32))
        acc_qkv[cols, :] += t_mm(low, normed)
        term = mm(low, w_qkv[cols, :])
        grad_normed = term if grad_normed is None else grad_normed + term
    dsmall_ref[:, :D] += col_sum(grad_normed * xhat)
    dsmall_ref[:, D : 2 * D] += col_sum(grad_normed)
    grad_x = grad_mid + norm_back(grad_normed, xhat, rstd, gain)
    dx_ref[...] = grad_x.reshape(WIN, SIDE, IMAGES, D)
    if layer:
        last_strips(dx_ref, strips)

    @pl.when(step == STEPS - 1)
    def _():
        pack_attention(at_ref, acc_qkv, acc_proj, dpacks)
        for g in range(2):
            for a in range(4):
                dtab_ref[8 * g + a] = acc_tab[g, a, :, :AROWS]
                dtab_ref[8 * g + 4 + a] = acc_tab[g, a, :, AROWS:]


def mlp_forward_kernel(layer, n_packs, at_ref, mid_ref, *refs):
    packs, refs = refs[:n_packs], refs[n_packs:]
    small_ref, y_ref, *strips, act_ref, slope_ref, w_one, w_two = refs

    @pl.when(pl.program_id(0) == 0)
    def _():
        unpack_mlp(at_ref, packs, w_one, w_two)

    mid = mid_ref[...]
    xhat, _ = normalize(mid)
    gain = small_ref[layer : layer + 1, 2 * D : 3 * D]
    shift = small_ref[layer : layer + 1, 3 * D : 4 * D]
    normed = (xhat * gain + shift).astype(BF16)
    total = mid + small_ref[layer : layer + 1, 5 * D : 6 * D]

    def hidden(c):
        bias = small_ref[layer : layer + 1, 9 * D + c * CHUNK : 9 * D + (c + 1) * CHUNK]
        return mm(normed, w_one[:, c * CHUNK : (c + 1) * CHUNK]) + bias

    pre = hidden(0)
    for c in range(CHUNKS):
        following = hidden(c + 1) if c + 1 < CHUNKS else None
        act, slope = gelu_both(pre)
        act_ref[c] = act
        slope_ref[c] = slope
        total = total + mm_t(act, w_two[c])
        pre = following
    y_ref[...] = total.reshape(WIN, SIDE, IMAGES, D)
    first_strips(y_ref, strips)


def mlp_backward_kernel(layer, forward, n_packs, n_out, at_ref, mid_ref, dy_ref, *refs):
    strips, refs = refs[:3], refs[3:]
    if not forward:
        (act_ref, slope_ref), refs = refs[:2], refs[2:]
    packs, small_ref, refs = refs[:n_packs], refs[n_packs], refs[n_packs + 1 :]
    if forward:
        (y_ref, *out_strips), refs = refs[:4], refs[4:]
    gm_ref, dpacks, refs = refs[0], refs[1 : 1 + n_out], refs[1 + n_out :]
    dsmall_ref, w_one, w_two, acc_one, acc_two, moved = refs
    step = pl.program_id(0)

    @pl.when(step == 0)
    def _():
        unpack_mlp(at_ref, packs, w_one, w_two)
        for ref in (dsmall_ref, acc_one, acc_two):
            ref[...] = jnp.zeros(ref.shape, ref.dtype)

    mid = mid_ref[...]
    xhat, rstd = normalize(mid)
    gain = small_ref[layer : layer + 1, 2 * D : 3 * D]
    shift = small_ref[layer : layer + 1, 3 * D : 4 * D]
    normed = (xhat * gain + shift).astype(BF16)
    dy = (next_rows if forward else prev_rows)(dy_ref, strips, moved)
    dy_low = dy.astype(BF16)
    dsmall_ref[:, 5 * D : 6 * D] += col_sum(dy_low.astype(F32))
    total = None
    if forward:
        total = mid + small_ref[layer : layer + 1, 5 * D : 6 * D]

    def products(c):
        grad_act = mm(dy_low, w_two[c])
        if not forward:
            return None, grad_act
        bias = small_ref[layer : layer + 1, 9 * D + c * CHUNK : 9 * D + (c + 1) * CHUNK]
        return mm(normed, w_one[:, c * CHUNK : (c + 1) * CHUNK]) + bias, grad_act

    grad_normed = None
    normed_turned, dy_turned = normed.T, dy_low.T
    pre, grad_act = products(0)
    for c in range(CHUNKS):
        cols = slice(c * CHUNK, (c + 1) * CHUNK)
        following = products(c + 1) if c + 1 < CHUNKS else (None, None)
        if forward:
            act, slope = gelu_both(pre)
            total = total + mm_t(act, w_two[c])
        else:
            act = act_ref[c]
            slope = slope_ref[c]
        grad_pre = (grad_act * slope.astype(F32)).astype(BF16)
        dsmall_ref[:, 9 * D + c * CHUNK : 9 * D + (c + 1) * CHUNK] += col_sum(grad_pre.astype(F32))
        term = mm_t(grad_pre, w_one[:, cols])
        grad_normed = term if grad_normed is None else grad_normed + term
        acc_one[:, cols] += mm(normed_turned, grad_pre)
        acc_two[c] += mm(dy_turned, act)
        pre, grad_act = following
    dsmall_ref[:, 2 * D : 3 * D] += col_sum(grad_normed * xhat)
    dsmall_ref[:, 3 * D : 4 * D] += col_sum(grad_normed)
    gm_ref[...] = dy + norm_back(grad_normed, xhat, rstd, gain)
    if forward:
        moved[...] = total.reshape(WIN, SIDE, IMAGES, D)
        last_strips(moved, out_strips)

        def place(a):
            if a == 0:
                y_ref[SHIFT : SHIFT + WIN, SHIFT:] = moved[:, :KEPT]
            else:
                y_ref[SHIFT + WIN :, SHIFT:] = moved[: WIN - SHIFT, :KEPT]

        both_steps(place)

    @pl.when(step == STEPS - 1)
    def _():
        pack_mlp(at_ref, acc_one, acc_two, dpacks)


def fixed(shape):
    return pl.BlockSpec(shape, lambda s: (0,) * len(shape), pipeline_mode=pl.Buffered(1))


def stepped(shape, axis=0):
    return pl.BlockSpec(shape, lambda s: tuple(s if d == axis else 0 for d in range(len(shape))))


def call(kernel, ins, in_specs, outs, scratch, flops, moved_bytes):
    return pl.pallas_call(
        kernel,
        grid=(STEPS,),
        in_specs=in_specs,
        out_shape=[jax.ShapeDtypeStruct(shape, kind) for shape, kind, _ in outs],
        out_specs=[spec for _, _, spec in outs],
        scratch_shapes=scratch,
        compiler_params=pltpu.CompilerParams(
            dimension_semantics=("arbitrary",), vmem_limit_bytes=VMEM_LIMIT
        ),
        cost_estimate=pl.CostEstimate(
            flops=int(flops), bytes_accessed=int(moved_bytes), transcendentals=0
        ),
    )(*ins)


GRID = (SIDE, SIDE, IMAGES, D)
GRID_STEP = stepped((WIN, SIDE, IMAGES, D))
ROWS_STEP = stepped((STEP_ROWS, D))
WINDOWS_STEP = stepped((STEP_WINDOWS, AROWS, 3 * D))
PROBS_STEP = stepped((STEP_WINDOWS, 2, 4 * AROWS, LANES))
HIDDEN_STEP = stepped((CHUNKS, STEP_ROWS, CHUNK), 1)
STRIPS = ((SHIFT, KEPT, IMAGES, D), (KEPT, SHIFT, IMAGES, D), (SHIFT, SHIFT, IMAGES, D))
STRIP_SPECS = [fixed(shape) for shape in STRIPS]
STRIP_OUTS = [(shape, BF16, fixed(shape)) for shape in STRIPS]
SCALARS = pl.BlockSpec(memory_space=pltpu.SMEM)
SHARD_A = (N_QKV + N_OUT, HALF)
SHARD_B = (N_FC1 + 4 * N_OUT, HALF)
ROW_SUMS = 9 * D + MLP
MOVED = pltpu.VMEM((WIN, SIDE, IMAGES, D), F32)


def tiles_of(features):
    return pltpu.VMEM((features // LANES, STEP_ROWS + IMAGES, LANES), F32)


def pack_specs(packs, shard):
    at = 0 if shard == SHARD_B else packs[0].shape[-2] // shard[0] - 1
    lead = packs[0].shape[:-2]
    return [
        pl.BlockSpec(
            lead + shard, lambda s: (0,) * len(lead) + (at, 0), pipeline_mode=pl.Buffered(1)
        )
    ] * len(packs)


def pack_outs(shard, single):
    if single:
        return [((32,) + shard, BF16, fixed((32,) + shard))]
    return [((4, 4) + shard, BF16, fixed((4, 4) + shard))] * 2


def attention_forward(layer, at, grid_field, strips, packs, small, base):
    out = call(
        partial(attention_forward_kernel, layer, len(packs)),
        (at, grid_field, *strips, *packs, small, base),
        [SCALARS, fixed(GRID) if layer else GRID_STEP]
        + STRIP_SPECS[: len(strips)]
        + pack_specs(packs, SHARD_A)
        + [fixed(small.shape), fixed(base.shape)],
        [((ROWS, D), F32, ROWS_STEP)] * layer
        + [
            ((STEPS * STEP_WINDOWS, AROWS, 3 * D), BF16, WINDOWS_STEP),
            ((STEPS * STEP_WINDOWS, 2, 4 * AROWS, LANES), BF16, PROBS_STEP),
            ((ROWS, D), BF16, ROWS_STEP),
            ((ROWS, D), F32, ROWS_STEP),
        ],
        [
            pltpu.VMEM((3 * D, D), BF16),
            pltpu.VMEM((D, D), BF16),
            tiles_of(3 * D),
            tiles_of(D),
            pltpu.VMEM((4 if layer else 1, 2, 4, WROWS, 2 * AROWS), F32),
        ]
        + [MOVED] * layer,
        2 * ROWS * 4 * D * D * 2,
        30e6,
    )
    return (list(out[:-1]) if layer else [grid_field] + list(out[:-1])), out[-1]


def attention_backward(layer, at, grad_mid, saved, packs, small, rest, single):
    outs = pack_outs(SHARD_A, single)
    out = call(
        partial(attention_backward_kernel, layer, len(packs), len(outs)),
        (at, grad_mid, *saved, *packs, small, rest),
        [
            SCALARS,
            ROWS_STEP,
            ROWS_STEP if layer else GRID_STEP,
            WINDOWS_STEP,
            PROBS_STEP,
            ROWS_STEP,
        ]
        + pack_specs(packs, SHARD_A)
        + [fixed(small.shape), fixed(rest.shape)],
        [(GRID, F32, GRID_STEP)]
        + STRIP_OUTS[: 3 * layer]
        + outs
        + [
            ((HEADS, WROWS, AROWS), F32, fixed((HEADS, WROWS, AROWS))),
            ((1, ROW_SUMS), F32, fixed((1, ROW_SUMS))),
        ],
        [
            pltpu.VMEM((3 * D, D), BF16),
            pltpu.VMEM((D, D), BF16),
            tiles_of(D),
            tiles_of(3 * D),
            pltpu.VMEM((3 * D, D), F32),
            pltpu.VMEM((D, D), F32),
            pltpu.VMEM((2, 4, WROWS, 2 * AROWS), F32),
        ],
        2 * ROWS * 4 * D * D * 5,
        30e6,
    )
    at_pack = 1 + 3 * layer
    return out[0], out[1:at_pack], out[at_pack:-2], out[-2], out[-1]


MLP_WEIGHTS = [pltpu.VMEM((D, MLP), BF16), pltpu.VMEM((CHUNKS, D, CHUNK), BF16)]


def mlp_forward(layer, at, mid, packs, small):
    out = call(
        partial(mlp_forward_kernel, layer, len(packs)),
        (at, mid, *packs, small),
        [SCALARS, ROWS_STEP] + pack_specs(packs, SHARD_B) + [fixed(small.shape)],
        [(GRID, F32, GRID_STEP)]
        + STRIP_OUTS
        + [((CHUNKS, ROWS, CHUNK), BF16, HIDDEN_STEP)] * 2,
        MLP_WEIGHTS,
        2 * ROWS * 2 * D * MLP,
        26e6,
    )
    return out[0], out[1:4], out[4:]


def mlp_backward(layer, at, mid, dy, strips, saved, packs, small, single):
    outs = pack_outs(SHARD_B, single)
    forward = not saved
    extra = 4 if forward else 0
    out = call(
        partial(mlp_backward_kernel, layer, forward, len(packs), len(outs)),
        (at, mid, dy, *strips, *saved, *packs, small),
        [SCALARS, ROWS_STEP, fixed(GRID)]
        + STRIP_SPECS
        + [HIDDEN_STEP] * len(saved)
        + pack_specs(packs, SHARD_B)
        + [fixed(small.shape)],
        ([(GRID, F32, fixed(GRID))] + STRIP_OUTS)[:extra]
        + [((ROWS, D), F32, ROWS_STEP)]
        + outs
        + [((1, ROW_SUMS), F32, fixed((1, ROW_SUMS)))],
        MLP_WEIGHTS
        + [pltpu.VMEM((D, MLP), F32), pltpu.VMEM((CHUNKS, D, CHUNK), F32), MOVED],
        2 * ROWS * (6 if forward else 4) * D * MLP,
        30e6,
    )
    return out[:extra], out[extra], out[extra + 1 : -1], out[-1]


def moved(x, step_of):
    sizes = [lax.axis_size(axis) for axis in AXES]

    def flat(i, r, c):
        return (i * sizes[1] + r) * sizes[2] + c

    pairs = [
        (flat(i, r, c), flat(*step_of(i, r, c)))
        for i in range(sizes[0])
        for r in range(sizes[1])
        for c in range(sizes[2])
    ]
    return lax.ppermute(x, AXES, pairs)


def swapped(x, img=0, down=0, core=0, across=0):
    return moved(x, lambda i, r, c: (i ^ img, r ^ (2 * down + core), c ^ across))


def send_strips(strips, by):
    rows, cols = lax.axis_size("row"), lax.axis_size("col")
    low, right, corner = strips
    return (
        moved(low, lambda i, r, c: (i, (r + by) % rows, c)),
        moved(right, lambda i, r, c: (i, r, (c + by) % cols)),
        moved(corner, lambda i, r, c: (i, (r + by) % rows, (c + by) % cols)),
    )


def fill_prev(grid_field, strips):
    high, left, corner = (strip.astype(F32) for strip in strips)
    grid_field = lax.dynamic_update_slice(grid_field, high, (0, SHIFT, 0, 0))
    grid_field = lax.dynamic_update_slice(grid_field, left, (SHIFT, 0, 0, 0))
    return lax.dynamic_update_slice(grid_field, corner, (0, 0, 0, 0))


QUADS = ((0, 0), (0, 1), (1, 0), (1, 1))


def after(values, *others):
    return lax.optimization_barrier((values, others))[0]


def together(*values):
    return lax.optimization_barrier(values)


def is_small():
    return lax.axis_size("img") == 2


def gather_line(pack):
    if not is_small():
        return pack
    return jnp.stack([pack] + [swapped(pack, across=m) for m in (1, 2, 3)])


def gather_quad(line):
    return jnp.stack([line] + [swapped(line, img=i, down=y) for i, y in QUADS[1:]])


def gather_whole(pack, canonical):
    whole = lax.all_gather(pack, AXES, axis=0, tiled=False)
    if not is_small():
        whole = canonical(whole.reshape((lax.axis_size("img"), 16) + pack.shape))
        whole = whole.reshape((32,) + whole.shape[2:])
    return (whole,)


def scatter_whole(whole, in_shards):
    if not is_small():
        whole = in_shards(whole.reshape((2, 16) + whole.shape[1:]), lax.axis_size("img"))
    flat = whole.reshape(-1, whole.shape[-1])
    return lax.psum_scatter(flat, AXES, scatter_dimension=0, tiled=True)


def scatter_plane(whole):
    if not is_small():
        return whole
    flat = whole.reshape(-1, whole.shape[-1])
    part = lax.psum_scatter(flat, ("img", "row"), scatter_dimension=0, tiled=True)
    return part.reshape((4,) + whole.shape[1:])


def scatter_col(part, in_shards):
    if not is_small():
        return scatter_whole(part, in_shards)
    flat = part.reshape(-1, part.shape[-1])
    return lax.psum_scatter(flat, "col", scatter_dimension=0, tiled=True)


def pair_swap(packs):
    return swapped(packs[1], core=1) if is_small() else packs


def scatter_pair(packs, got):
    if not is_small():
        return packs
    half = packs[0].astype(F32) + got.astype(F32)
    return [half[0]] + [half[m].astype(BF16) for m in (1, 2, 3)]


def quad_swaps(halves):
    if not is_small():
        return []
    return [swapped(h, img=i, down=y) for h, (i, y) in zip(halves[1:], QUADS[1:])]


def scatter_quad(halves, got):
    if not is_small():
        return halves
    got = [g.astype(F32) for g in got]
    line = (halves[0] + got[0]) + (got[1] + got[2])
    return [line[0]] + [line[m].astype(BF16) for m in (1, 2, 3)]


def near_swap(x):
    return swapped(x, across=1)


def far_swap(x):
    return swapped(x, across=2)


def line_swaps(line):
    return [swapped(line[m], across=m) for m in (1, 2, 3)] if is_small() else []


def padded_index(rel_index):
    cells = rel_index.T.reshape(WIN, WIN, WIN, WIN)
    gap = (0, SLOT - WIN)
    cells = jnp.pad(cells, [(0, 0), gap, (0, AROWS // SLOT - WIN), gap], constant_values=-1)
    return cells.reshape(1, WROWS * AROWS)


def packing_kernel(w_qkv, w_proj, w_fc1, w_fc2, first_a, second_a, first_b, second_b):
    for l, (pack_a, pack_b) in enumerate(((first_a, first_b), (second_a, second_b))):
        pack_a[:N_QKV] = w_qkv[l].astype(BF16)
        pack_a[N_QKV:] = w_proj[l].astype(BF16)
        for h in range(2):
            pack_b[:N_FC1, h * LANES : (h + 1) * LANES] = w_fc1[
                l, h * LANES : (h + 1) * LANES, :
            ].astype(BF16)
        for k in range(4):
            pack_b[N_FC1 + k * N_OUT : N_FC1 + (k + 1) * N_OUT] = w_fc2[
                l, :, k * HALF : (k + 1) * HALF
            ].astype(BF16)


def turned(matrices):
    w_qkv, w_proj, w_fc1, w_fc2 = matrices
    return w_qkv.swapaxes(1, 2), w_proj.swapaxes(1, 2), w_fc1, w_fc2.swapaxes(1, 2)


def make_packs(masters):
    w_qkv, w_proj, w_fc1, w_fc2 = turned(masters)
    if is_small():
        kinds = [jax.ShapeDtypeStruct(shape, BF16) for shape in (SHARD_A, SHARD_A, SHARD_B, SHARD_B)]
        return pl.pallas_call(
            packing_kernel,
            out_shape=kinds,
            compiler_params=pltpu.CompilerParams(vmem_limit_bytes=VMEM_LIMIT),
        )(w_qkv, w_proj, w_fc1, w_fc2)
    cols = w_qkv.shape[2]
    packs = [jnp.concatenate([w_qkv[l], w_proj[l]], axis=0).astype(BF16) for l in range(2)]
    for l in range(2):
        second = w_fc2[l].reshape(N_OUT, 4, cols).transpose(1, 0, 2).reshape(-1, cols)
        packs.append(jnp.concatenate([w_fc1[l].T, second], axis=0).astype(BF16))
    return packs


def update_kernel(kinds, rates, *refs):
    sums, refs = refs[:5], refs[5:]
    count = len(rates)
    ins, outs = refs[: 3 * count], refs[3 * count :]
    for l in range(2):
        if l == 0:
            near, far, both = (s[...].astype(F32) for s in sums[1:4])
            total = (sums[0][...] + near) + (far + both)
        else:
            total = sums[4][...].astype(F32)
        for k, grad in enumerate(kinds(total)):
            rate, decay = rates[k]
            new = adam_step(*(ins[3 * k + m][l] for m in range(3)), grad, rate, decay)
            for m in range(3):
                outs[3 * k + m][l] = new[m]


def attention_kinds(total):
    return total[:N_QKV], total[N_QKV:]


def mlp_kinds(total):
    first = jnp.concatenate([total[:N_FC1, :LANES], total[:N_FC1, LANES:]], axis=0)
    second = [total[N_FC1 + k * N_OUT : N_FC1 + (k + 1) * N_OUT] for k in range(4)]
    return first, jnp.concatenate(second, axis=1)


def update(kinds, sums, arrays):
    rates = ((RATE_MATRIX, DECAY_MATRIX),) * (len(arrays) // 3)
    return pl.pallas_call(
        partial(update_kernel, kinds, rates),
        out_shape=[jax.ShapeDtypeStruct(x.shape, F32) for x in arrays],
        compiler_params=pltpu.CompilerParams(vmem_limit_bytes=VMEM_LIMIT),
    )(*sums, *arrays)


def attention_canonical(whole):
    _, ranks, rows, _ = whole.shape
    whole = whole.transpose(1, 2, 0, 3).reshape(ranks, rows, 2, HALF)
    return whole.transpose(2, 0, 1, 3)


def attention_shards(pack, size):
    _, ranks, rows, _ = pack.shape
    pack = pack.transpose(1, 2, 0, 3).reshape(ranks, rows, size, D // size)
    return pack.transpose(2, 0, 1, 3)


def mlp_canonical(whole):
    size, ranks, _, cols = whole.shape
    first = attention_canonical(whole[:, :, :N_FC1]).swapaxes(2, 3)
    first = first.reshape(2, ranks, 2, LANES, N_FC1).transpose(0, 1, 3, 2, 4).reshape(2, ranks, LANES, HALF)
    second = whole[:, :, N_FC1:].reshape(size, ranks, 4, N_OUT, cols)
    second = second.transpose(1, 3, 0, 2, 4).reshape(ranks, N_OUT, 2, 4, HALF)
    second = second.transpose(2, 0, 3, 1, 4).reshape(2, ranks, 4 * N_OUT, HALF)
    return jnp.concatenate([first, second], axis=2)


def mlp_shards(pack, size):
    _, ranks, _, _ = pack.shape
    cols = D // size
    first = pack[:, :, :N_FC1].reshape(2, ranks, LANES, 2, N_FC1).transpose(0, 1, 3, 2, 4)
    first = attention_shards(first.reshape(2, ranks, HALF, N_FC1).swapaxes(2, 3), size)
    second = pack[:, :, N_FC1:].reshape(2, ranks, 4, N_OUT, HALF)
    second = second.transpose(1, 3, 0, 2, 4).reshape(ranks, N_OUT, size, 4, cols)
    second = second.transpose(2, 0, 3, 1, 4).reshape(size, ranks, 4 * N_OUT, cols)
    return jnp.concatenate([first, second], axis=2)


def adam_step(weight, moment_one, second, gradient, rate_value, decay_rate):
    moment_one = BETA_ONE * moment_one + (1.0 - BETA_ONE) * gradient
    second = BETA_TWO * second + (1.0 - BETA_TWO) * gradient * gradient
    update = (
        moment_one / (1.0 - BETA_ONE**STEP) / (jnp.sqrt(second / (1.0 - BETA_TWO**STEP)) + EPS_ADAM)
    )
    return (weight - rate_value * (update + decay_rate * weight), moment_one, second)


def shards(
    images,
    grad_out,
    w_qkv,
    w_proj,
    w_fc1,
    w_fc2,
    first_qkv,
    first_proj,
    first_fc1,
    first_fc2,
    second_qkv,
    second_proj,
    second_fc1,
    second_fc2,
    small_params,
    small_first,
    small_second,
    rel_index,
):
    assert images.shape == (IMAGES, SIDE, SIDE, D)
    size = lax.axis_size("img")
    small = is_small()
    row, col = lax.axis_index("row"), lax.axis_index("col")
    last = [row == lax.axis_size("row") - 1, col == lax.axis_size("col") - 1]
    place = [lax.axis_index("img"), row // 2, row % 2, col]
    at = jnp.stack([jnp.asarray(value, jnp.int32) for value in place + last])
    images = images.transpose(1, 2, 0, 3)
    grad_out = grad_out.transpose(1, 2, 0, 3)

    masters = (w_qkv, w_proj, w_fc1, w_fc2)
    pack_a_zero, pack_a_one, pack_b_zero, pack_b_one = make_packs(masters)
    if small:
        line_a, near_b, near_a = together(
            gather_line(pack_a_zero), near_swap(pack_b_zero), near_swap(pack_a_one)
        )
        pair_b, pair_a = jnp.stack([pack_b_zero, near_b]), jnp.stack([pack_a_one, near_a])
        packs_b_one = gather_whole(after(pack_b_one, line_a, near_b), mlp_canonical)
        got, far_b = together(quad_swaps([line_a] * 4), far_swap(pair_b))
        quad = jnp.stack([line_a, *got])
        packs_a_zero = quad, swapped(quad, core=1)
        line_b = jnp.concatenate([pair_b, far_b])
    else:
        packs_a_zero = gather_whole(pack_a_zero, attention_canonical)
        packs_b_zero = gather_whole(pack_b_zero, mlp_canonical)
        packs_a_one = gather_whole(pack_a_one, attention_canonical)
        packs_b_one = gather_whole(pack_b_one, mlp_canonical)

    onehot = (
        jnp.arange(RELPOS, dtype=jnp.int32)[:, None] == padded_index(rel_index)
    ).astype(F32)
    tables = small_params[:, 9 * D + MLP :].reshape(2, RELPOS, HEADS)
    base = jnp.einsum("lrh,rp->lhp", tables * LOG2E, onehot, precision=lax.Precision.HIGHEST)
    base = base.reshape(2, HEADS, WROWS, AROWS)
    grad_strips = (
        grad_out[:SHIFT, SHIFT:].astype(BF16),
        grad_out[SHIFT:, :SHIFT].astype(BF16),
        grad_out[:SHIFT, :SHIFT].astype(BF16),
    )

    def table_row(sums, dtab):
        table = jnp.einsum(
            "hp,rp->rh", dtab.reshape(HEADS, -1), onehot, precision=lax.Precision.HIGHEST
        )
        return jnp.concatenate([sums, table.reshape(1, -1)], axis=1)

    packs_a_zero = after(packs_a_zero, base, grad_strips)
    saved_zero, mid_zero = attention_forward(0, at, images, (), packs_a_zero, small_params, base[0])
    if small:
        mid_zero, got, far_a = together(mid_zero, quad_swaps([line_b] * 4), far_swap(pair_a))
        quad = jnp.stack([line_b, *got])
        packs_b_zero = quad, swapped(quad, core=1)
        line_a = jnp.concatenate([pair_a, far_a])
    grad_strips = send_strips(after(grad_strips, mid_zero), -1)
    out_zero, strips, hidden_zero = mlp_forward(0, at, mid_zero, packs_b_zero, small_params)
    strips, grad_strips = together(strips, grad_strips)
    if small:
        strips, got = together(strips, quad_swaps([line_a] * 4))
        quad = jnp.stack([line_a, *got])
        strips, other = together(send_strips(strips, -1), swapped(quad, core=1))
        packs_a_one = quad, other
    else:
        strips = send_strips(strips, -1)
    saved_one, mid_one = attention_forward(
        1, at, out_zero, strips, packs_a_one, small_params, base[1]
    )
    (out_one, *out_strips), gm_one, dpacks, rest = mlp_backward(
        1, at, mid_one, grad_out, grad_strips, (), packs_b_one, small_params, True
    )

    plane_b_one = scatter_plane(dpacks[0])
    dx_one, strips, dpacks, dtab_one, sums = attention_backward(
        1, at, gm_one, saved_one, packs_a_one, small_params, rest, True
    )
    plane_a_one = scatter_plane(dpacks[0])
    strips, plane_b_one, row_one = together(
        send_strips(strips, 1), plane_b_one, table_row(sums, dtab_one)
    )
    out_strips = send_strips(after(out_strips, strips), 1)
    _, gm_zero, dpacks, rest = mlp_backward(
        0, at, mid_zero, dx_one, strips, hidden_zero, packs_b_zero, small_params, not small
    )

    dpacks, out_strips = together(dpacks, out_strips)
    got, out_one = together(pair_swap(dpacks), fill_prev(out_one, out_strips))
    outputs = out_one.transpose(2, 0, 1, 3)
    halves_b_zero = scatter_pair(dpacks, got)
    gm_zero, halves_b_zero = together(gm_zero, halves_b_zero)
    sum_b_one = scatter_col(plane_b_one, mlp_shards)
    grad_input, _, dpacks, dtab_zero, sums = attention_backward(
        0, at, gm_zero, saved_zero, packs_a_zero, small_params, rest, not small
    )
    grad_input = grad_input.transpose(2, 0, 1, 3)

    dpacks, got_b, sum_b_one, plane_a_one = together(
        dpacks, quad_swaps(halves_b_zero), sum_b_one, plane_a_one
    )
    sum_a_one = scatter_col(plane_a_one, attention_shards)
    got, row_zero = together(pair_swap(dpacks), table_row(sums, dtab_zero))
    halves_a = scatter_pair(dpacks, got)
    small_grad = jnp.concatenate([row_zero, row_one], axis=0)

    def small_swaps(*steps):
        return [swapped(small_grad, **step) for step in steps] if small else []

    halves_b_zero, got_b = after((halves_b_zero, got_b), halves_a)
    line_b = scatter_quad(halves_b_zero, got_b)
    got, parts = together(quad_swaps(halves_a), small_swaps({"core": 1}))
    line_a = scatter_quad(halves_a, got)
    small_grad = sum(parts, small_grad)
    steps = [{"img": i, "down": y} for i, y in QUADS[1:]]
    sums_b = line_swaps(line_b)
    sums_a, parts = together(line_swaps(line_a), small_swaps(*steps))
    if small:
        small_grad = (small_grad + parts[0]) + (parts[1] + parts[2])
        parts = small_swaps(*({"across": m} for m in (1, 2, 3)))
        small_grad = (small_grad + parts[0]) + (parts[1] + parts[2])
    else:
        small_grad = lax.psum(small_grad, AXES)

    states = [turned(group) for group in (
        masters,
        (first_qkv, first_proj, first_fc1, first_fc2),
        (second_qkv, second_proj, second_fc1, second_fc2),
    )]
    if small:
        new_a = update(
            attention_kinds, (line_a[0], *sums_a, sum_a_one), [s[k] for k in (0, 1) for s in states]
        )
        new_b = update(
            mlp_kinds, (line_b[0], *sums_b, sum_b_one), [s[k] for k in (2, 3) for s in states]
        )
    else:
        cols = D // size
        total_a = [scatter_whole(line_a[0], attention_shards), sum_a_one]
        total_b = [scatter_whole(line_b[0], mlp_shards), sum_b_one]
        kinds = (
            [t[:N_QKV] for t in total_a],
            [t[N_QKV:] for t in total_a],
            [t[:N_FC1].T for t in total_b],
            [t[N_FC1:].reshape(4, N_OUT, cols).transpose(1, 0, 2).reshape(N_OUT, -1) for t in total_b],
        )
        new = []
        for k in range(4):
            grad = jnp.stack(kinds[k]).astype(F32)
            new += adam_step(*(s[k] for s in states), grad, RATE_MATRIX, DECAY_MATRIX)
        new_a, new_b = new[:6], new[6:]
    small_new = adam_step(small_params, small_first, small_second, small_grad, RATE_SMALL, 0.0)
    new = list(new_a) + list(new_b)
    new = [turned(new[m::3]) for m in range(3)]
    return (outputs, grad_input) + new[0] + new[1] + new[2] + tuple(small_new)


def solution(mesh):
    grid_spec = P("img", "row", "col", None)
    matrix = P(None, "img", ("row", "col"))
    in_specs = (grid_spec,) * 2 + (matrix,) * 12 + (P(),) * 4
    out_specs = (grid_spec,) * 2 + (matrix,) * 12 + (P(),) * 3
    return jax.shard_map(shards, mesh=mesh, in_specs=in_specs, out_specs=out_specs, check_vma=False)
```

```python
from functools import partial

import jax
import jax.numpy as jnp
from jax import lax
from jax.experimental import pallas as pl
from jax.experimental.pallas import tpu as pltpu
from jax.sharding import PartitionSpec as P

D = 512
HEADS = 16
HEAD_DIM = 32
MLP = 2048
WIN = 7
SHIFT = 3
STEP = 10
RELPOS = 169

EPS_NORM = 1e-05
BETA_ONE = 0.9
BETA_TWO = 0.999
EPS_ADAM = 1e-08
RATE_MATRIX = 0.05
RATE_SMALL = 0.3
DECAY_MATRIX = 0.05
MASKED = -1e30

AXES = ("img", "row", "col")
F32 = jnp.float32
BF16 = jnp.bfloat16
LOG2E = 1.4426950408889634
SCALE = HEAD_DIM ** (-0.5)

SIDE = 2 * WIN
IMAGES = 8
SLOT = 8
WROWS = WIN * SLOT
AROWS = 64
STEPS = 2
STEP_ROWS = WIN * SIDE * IMAGES
ROWS = STEPS * STEP_ROWS
STEP_WINDOWS = 2 * IMAGES
KEPT = SIDE - SHIFT
CHUNK = 512
CHUNKS = MLP // CHUNK
HALF = D // 2
LANES = 128
MIB = 1024 * 1024


def mm(left, right):
    return lax.dot_general(left, right, (((1,), (0,)), ((), ())), preferred_element_type=F32)


def mm_t(left, right):
    return lax.dot_general(left, right, (((1,), (1,)), ((), ())), preferred_element_type=F32)


def t_mm(left, right):
    return lax.dot_general(left, right, (((0,), (0,)), ((), ())), preferred_element_type=F32)


def col_sum(value):
    return jnp.sum(value, axis=0, keepdims=True)


def normalize(rows):
    center = rows - jnp.mean(rows, axis=-1, keepdims=True)
    spread = jnp.mean(center * center, axis=-1, keepdims=True)
    rstd = lax.rsqrt(spread + EPS_NORM)
    return center * rstd, rstd


def norm_back(grad, xhat, rstd, gain):
    scaled = grad * gain
    mean_one = jnp.mean(scaled, axis=-1, keepdims=True)
    mean_two = jnp.mean(scaled * xhat, axis=-1, keepdims=True)
    return rstd * (scaled - mean_one - xhat * mean_two)


def gelu_both(pre):
    pre = pre.astype(BF16)
    t = 1.0 / (1.0 + jnp.abs(pre) * (0.3275911 * 0.7071067811865476))
    bell = jnp.exp2(pre * pre * (-0.5 * LOG2E))
    poly = t * (0.5 * 1.061405429) + 0.5 * -1.453152027
    poly = poly * t + 0.5 * 1.421413741
    poly = poly * t + 0.5 * -0.284496736
    poly = poly * t + 0.5 * 0.254829592
    tail = poly * t * bell
    cdf = jnp.where(pre >= 0.0, 1.0 - tail, tail)
    return pre * cdf, cdf + pre * bell * 0.3989422804014327


def both_steps(body):
    for a in range(STEPS):
        pl.when(pl.program_id(0) == a)(partial(body, a))


def next_rows(grid_ref, strip_refs, rows_ref):
    low_ref, right_ref, corner_ref = strip_refs

    def body(a):
        if a == 0:
            rows_ref[:, :KEPT] = grid_ref[SHIFT : SHIFT + WIN, SHIFT:]
            rows_ref[:, KEPT:] = right_ref[:WIN].astype(F32)
        else:
            rows_ref[: WIN - SHIFT, :KEPT] = grid_ref[SHIFT + WIN :, SHIFT:]
            rows_ref[: WIN - SHIFT, KEPT:] = right_ref[WIN:].astype(F32)
            rows_ref[WIN - SHIFT :, :KEPT] = low_ref[...].astype(F32)
            rows_ref[WIN - SHIFT :, KEPT:] = corner_ref[...].astype(F32)

    both_steps(body)
    return rows_ref[...].reshape(STEP_ROWS, D)


def prev_rows(grid_ref, strip_refs, rows_ref):
    high_ref, left_ref, corner_ref = strip_refs

    def body(a):
        if a == 0:
            rows_ref[:SHIFT, SHIFT:] = high_ref[...].astype(F32)
            rows_ref[:SHIFT, :SHIFT] = corner_ref[...].astype(F32)
            rows_ref[SHIFT:, SHIFT:] = grid_ref[: WIN - SHIFT, :KEPT]
            rows_ref[SHIFT:, :SHIFT] = left_ref[: WIN - SHIFT].astype(F32)
        else:
            rows_ref[:, SHIFT:] = grid_ref[WIN - SHIFT : KEPT, :KEPT]
            rows_ref[:, :SHIFT] = left_ref[WIN - SHIFT :].astype(F32)

    both_steps(body)
    return rows_ref[...].reshape(STEP_ROWS, D)


def first_strips(block_ref, strip_refs):
    rows_ref, cols_ref, corner_ref = strip_refs

    def body(a):
        if a == 0:
            rows_ref[...] = block_ref[:SHIFT, SHIFT:].astype(BF16)
            cols_ref[: WIN - SHIFT] = block_ref[SHIFT:, :SHIFT].astype(BF16)
            corner_ref[...] = block_ref[:SHIFT, :SHIFT].astype(BF16)
        else:
            cols_ref[WIN - SHIFT :] = block_ref[:, :SHIFT].astype(BF16)

    both_steps(body)


def last_strips(block_ref, strip_refs):
    rows_ref, cols_ref, corner_ref = strip_refs

    def body(a):
        if a == 0:
            cols_ref[:WIN] = block_ref[:, KEPT:].astype(BF16)
        else:
            cols_ref[WIN:] = block_ref[: WIN - SHIFT, KEPT:].astype(BF16)
            rows_ref[...] = block_ref[WIN - SHIFT :, :KEPT].astype(BF16)
            corner_ref[...] = block_ref[WIN - SHIFT :, KEPT:].astype(BF16)

    both_steps(body)


def put_tiles(tiles, first, value):
    for t in range(value.shape[1] // LANES):
        tiles[first + t, :STEP_ROWS, :] = value[:, t * LANES : (t + 1) * LANES]


def get_tiles(tiles, first, count):
    return jnp.concatenate([tiles[first + t, :STEP_ROWS, :] for t in range(count)], axis=1)


def clear_tail(tiles):
    tiles[:, STEP_ROWS:, :] = jnp.zeros(tiles[:, STEP_ROWS:, :].shape, F32)


def window_at(b, n, r):
    return b * WIN * IMAGES + r * SIDE * IMAGES + n


def get_window(tiles, first, b, n):
    return jnp.concatenate(
        [
            jnp.concatenate(
                [
                    tiles[first + t, pl.ds(window_at(b, n, r), SLOT, stride=IMAGES), :]
                    for r in range(WIN)
                ],
                axis=0,
            )
            for t in range(2)
        ],
        axis=1,
    )


def put_window(tiles, first, b, n, value):
    for t in range(2):
        for r in range(WIN):
            tiles[first + t, pl.ds(window_at(b, n, r), WIN, stride=IMAGES), :] = value[
                r * SLOT : r * SLOT + WIN, t * LANES : (t + 1) * LANES
            ]


def to_sixty_four(window):
    padding = jnp.zeros((AROWS - WROWS, window.shape[1]), F32)
    return jnp.concatenate([window, padding], axis=0).astype(BF16)


def head_masks():
    lane = lax.broadcasted_iota(jnp.int32, (16, HALF), 1)
    head = jnp.bitwise_and(lax.shift_right_logical(lane, 5), 3)
    return [jnp.where(head == a, 1.0, 0.0).astype(BF16) for a in range(4)]


def stack_heads(part, masks):
    split = part.reshape(AROWS // 16, 16, HALF)
    return jnp.concatenate(
        [(split * mask[None]).reshape(AROWS, HALF) for mask in masks], axis=0
    )


def stack_halves(part):
    zero = jnp.zeros((AROWS, HALF // 2), part.dtype)
    return jnp.concatenate(
        [
            jnp.concatenate([part[:, : HALF // 2], zero], axis=1),
            jnp.concatenate([zero, part[:, HALF // 2 :]], axis=1),
        ],
        axis=0,
    )


def pick_halves(result):
    return jnp.concatenate(
        [result[:WROWS, : HALF // 2], result[AROWS : AROWS + WROWS, HALF // 2 :]], axis=1
    )


def pick_heads(result):
    lane = lax.broadcasted_iota(jnp.int32, (WROWS, HALF), 1)
    head = jnp.bitwise_and(lax.shift_right_logical(lane, 5), 3)
    picked = result[3 * AROWS : 3 * AROWS + WROWS]
    for a in (2, 1, 0):
        picked = jnp.where(head == a, result[a * AROWS : a * AROWS + WROWS], picked)
    return picked


def pad_keys(value):
    padding = jnp.zeros((4, AROWS - WROWS, 128), F32)
    return jnp.concatenate([value, padding], axis=1).astype(BF16).reshape(4 * AROWS, 128)


def places(at_ref, packs, turn=True):
    if len(packs) == 1:
        for shard in range(packs[0].shape[0]):
            yield 0, (shard,), shard // 16, shard % 16
        return
    for core in range(2):
        for quad in range(4):
            for across in range(4):
                i = jnp.bitwise_xor(at_ref[0], quad >> 1)
                y = jnp.bitwise_xor(at_ref[1], quad & 1)
                c = jnp.bitwise_xor(at_ref[2], core)
                z = jnp.bitwise_xor(at_ref[3], across) if turn else across
                yield core, (quad, across), i, (2 * y + c) * 4 + z


def piece(start, length):
    if isinstance(start, int):
        return pl.ds(start * length, length)
    return pl.ds(pl.multiple_of(start * length, length), length)


N_QKV = 3 * D // 16
N_OUT = D // 16
N_FC1 = MLP // 16


def unpack_attention(at_ref, packs, w_qkv, w_proj):
    for core, at, i, r in places(at_ref, packs):
        cols = piece(i, HALF)
        w_qkv[piece(r, N_QKV), cols] = packs[core][at + (slice(0, N_QKV),)]
        w_proj[piece(r, N_OUT), cols] = packs[core][at + (slice(N_QKV, None),)]


def pack_attention(at_ref, g_qkv, g_proj, packs):
    for core, at, i, r in places(at_ref, packs):
        cols = piece(i, HALF)
        packs[core][at + (slice(0, N_QKV),)] = g_qkv[piece(r, N_QKV), cols].astype(BF16)
        packs[core][at + (slice(N_QKV, None),)] = g_proj[piece(r, N_OUT), cols].astype(BF16)


def unpack_mlp(at_ref, packs, w_one, w_two):
    for core, at, i, r in places(at_ref, packs):
        for h in range(2):
            w_one[piece(2 * i + h, LANES), piece(r, N_FC1)] = packs[core][
                at + (slice(0, N_FC1), slice(h * LANES, (h + 1) * LANES))
            ]
        for k in range(4):
            w_two[2 * i + k // 2, piece(r, N_OUT), (k % 2) * HALF : (k % 2 + 1) * HALF] = packs[core][
                at + (slice(N_FC1 + k * N_OUT, N_FC1 + (k + 1) * N_OUT),)
            ]


def pack_mlp(at_ref, g_one, g_two, packs):
    for core, at, i, r in places(at_ref, packs, False):
        for h in range(2):
            packs[core][at + (slice(0, N_FC1), slice(h * LANES, (h + 1) * LANES))] = g_one[
                piece(2 * i + h, LANES), piece(r, N_FC1)
            ].astype(BF16)
        for k in range(4):
            packs[core][at + (slice(N_FC1 + k * N_OUT, N_FC1 + (k + 1) * N_OUT),)] = g_two[
                2 * i + k // 2, piece(r, N_OUT), (k % 2) * HALF : (k % 2 + 1) * HALF
            ].astype(BF16)


def spread_bias(layer, at_ref, base_ref, bias):
    row = lax.broadcasted_iota(jnp.int32, (WROWS, 2 * AROWS), 0)
    lane = jnp.bitwise_and(lax.broadcasted_iota(jnp.int32, (WROWS, 2 * AROWS), 1), AROWS - 1)
    key_row, key_col = row // SLOT, jnp.bitwise_and(row, SLOT - 1)
    query_row, query_col = lane // SLOT, jnp.bitwise_and(lane, SLOT - 1)
    kept = WIN - SHIFT
    other_row = ((key_row >= kept) != (query_row >= kept)).astype(jnp.int32)
    other_col = ((key_col >= kept) != (query_col >= kept)).astype(jnp.int32)
    padding = (key_col == WIN).astype(jnp.int32)
    for v in range(bias.shape[0]):
        hidden = padding
        if layer == 1:
            if v >> 1:
                hidden = hidden + other_row * at_ref[4]
            if v & 1:
                hidden = hidden + other_col * at_ref[5]
        for g in range(2):
            for a in range(4):
                both = jnp.concatenate([base_ref[8 * g + a], base_ref[8 * g + 4 + a]], axis=1)
                bias[v, g, a] = jnp.where(hidden > 0, MASKED, both)


def attention_forward_kernel(layer, n_packs, at_ref, x_ref, *refs):
    strips, refs = refs[: 3 * layer], refs[3 * layer :]
    packs, refs = refs[:n_packs], refs[n_packs:]
    small_ref, base_ref, refs = refs[0], refs[1], refs[2:]
    if layer:
        xs_ref, refs = refs[0], refs[1:]
    qkv_ref, p_ref, att_ref, mid_ref, w_qkv, w_proj, tiles, att_tiles, bias_ref, *moved = refs
    step = pl.program_id(0)

    @pl.when(step == 0)
    def _():
        unpack_attention(at_ref, packs, w_qkv, w_proj)
        spread_bias(layer, at_ref, base_ref, bias_ref)
        clear_tail(tiles)

    gain = small_ref[layer : layer + 1, 0:D]
    shift = small_ref[layer : layer + 1, D : 2 * D]
    if layer:
        rows = next_rows(x_ref, strips, moved[0])
        xs_ref[...] = rows
    else:
        rows = x_ref[...].reshape(STEP_ROWS, D)
    xhat, _ = normalize(rows)
    normed = (xhat * gain + shift).astype(BF16)
    for part in range(3):
        cols = slice(part * D, (part + 1) * D)
        bias = small_ref[layer : layer + 1, 6 * D + part * D : 7 * D + part * D]
        put_tiles(tiles, 4 * part, mm_t(normed, w_qkv[cols, :]) + bias)
    masks = head_masks()
    lane = jnp.bitwise_and(lax.broadcasted_iota(jnp.int32, (4, 1, LANES), 2), AROWS - 1)
    no_query = (jnp.bitwise_and(lane, SLOT - 1) == WIN) | (lane >= WROWS)

    def windows(pair, carry):
        places_of = [(b, g, 2 * pair + k) for k in range(2) for b in range(2) for g in range(2)]
        scores, values = [], []
        for b, g, n in places_of:
            q, key, val = (
                to_sixty_four(get_window(tiles, 4 * part + 2 * g, b, n)) for part in range(3)
            )
            for part, value in enumerate((q, key, val)):
                at = part * D + g * HALF
                qkv_ref[b * IMAGES + n, :, at : at + HALF] = value
            scores.append(mm_t(stack_heads(key, masks), stack_halves(q)))
            values.append(val)
        probs = []
        for (b, g, n), score in zip(places_of, scores):
            v = 2 * step + b if layer else 0
            score = score.reshape(4, AROWS, LANES)[:, :WROWS] * (SCALE * LOG2E) + bias_ref[v, g]
            powers = jnp.exp2(score - jnp.max(score, axis=1, keepdims=True))
            total = jnp.sum(powers, axis=1, keepdims=True)
            prob = pad_keys(powers * jnp.where(no_query, 0.0, 1.0 / total))
            p_ref[b * IMAGES + n, g] = prob
            probs.append(prob)
        for (b, g, n), prob, val in zip(places_of, probs, values):
            put_window(att_tiles, 2 * g, b, n, pick_halves(t_mm(prob, stack_heads(val, masks))))
        return carry

    lax.fori_loop(0, IMAGES // 2, windows, 0)
    att = get_tiles(att_tiles, 0, 4).astype(BF16)
    att_ref[...] = att
    bias = small_ref[layer : layer + 1, 4 * D : 5 * D]
    mid_ref[...] = rows + (mm_t(att, w_proj[...]) + bias)


def attention_backward_kernel(layer, n_packs, n_out, at_ref, gm_ref, x_ref, qkv_ref, p_ref, att_ref, *refs):
    packs, refs = refs[:n_packs], refs[n_packs:]
    small_ref, rest_ref, dx_ref, refs = refs[0], refs[1], refs[2], refs[3:]
    strips, refs = refs[: 3 * layer], refs[3 * layer :]
    dpacks, refs = refs[:n_out], refs[n_out:]
    dtab_ref, dsmall_ref, w_qkv, w_proj, g_tiles, d_tiles, acc_qkv, acc_proj, acc_tab = refs
    step = pl.program_id(0)

    @pl.when(step == 0)
    def _():
        unpack_attention(at_ref, packs, w_qkv, w_proj)
        dsmall_ref[...] = rest_ref[...]
        clear_tail(g_tiles)
        for ref in (acc_tab, acc_qkv, acc_proj):
            ref[...] = jnp.zeros(ref.shape, ref.dtype)

    gain = small_ref[layer : layer + 1, 0:D]
    shift = small_ref[layer : layer + 1, D : 2 * D]
    grad_mid = gm_ref[...]
    mid_low = grad_mid.astype(BF16)
    dsmall_ref[:, 4 * D : 5 * D] += col_sum(mid_low.astype(F32))
    acc_proj[...] += t_mm(mid_low, att_ref[...])
    put_tiles(g_tiles, 0, mm(mid_low, w_proj[...]))
    masks = head_masks()

    def windows(pair, carry):
        places_of = [(b, g, 2 * pair + k) for k in range(2) for b in range(2) for g in range(2)]
        loaded, dprobs = [], []
        for b, g, n in places_of:
            w = b * IMAGES + n
            q, key, val = (
                qkv_ref[w, :, part * D + g * HALF : part * D + (g + 1) * HALF] for part in range(3)
            )
            grad = stack_halves(to_sixty_four(get_window(g_tiles, 2 * g, b, n)))
            dprobs.append(mm_t(stack_heads(val, masks), grad))
            loaded.append((q, key, grad, p_ref[w, g]))
        lows = []
        sums = [None, None]
        for (b, g, _), dprob, (_, _, _, prob) in zip(places_of, dprobs, loaded):
            dprob = dprob.reshape(4, AROWS, LANES)[:, :WROWS]
            p = prob.astype(F32).reshape(4, AROWS, LANES)[:, :WROWS]
            delta = jnp.sum(p * dprob, axis=1, keepdims=True)
            dscore = p * (dprob - delta)
            sums[g] = dscore if sums[g] is None else sums[g] + dscore
            lows.append(pad_keys(dscore))
        for g in range(2):
            acc_tab[g] += sums[g]
        for (b, g, n), low, (q, key, grad, prob) in zip(places_of, lows, loaded):
            put_window(d_tiles, 2 * g, b, n, pick_halves(t_mm(low, stack_heads(key, masks))) * SCALE)
            put_window(d_tiles, 4 + 2 * g, b, n, pick_heads(mm(low, stack_halves(q))) * SCALE)
            put_window(d_tiles, 8 + 2 * g, b, n, pick_heads(mm(prob, grad)))
        return carry

    lax.fori_loop(0, IMAGES // 2, windows, 0)
    xhat, rstd = normalize(x_ref[...].reshape(STEP_ROWS, D))
    normed = (xhat * gain + shift).astype(BF16)
    grad_normed = None
    for part in range(3):
        cols = slice(part * D, (part + 1) * D)
        low = get_tiles(d_tiles, 4 * part, 4).astype(BF16)
        dsmall_ref[:, 6 * D + part * D : 7 * D + part * D] += col_sum(low.astype(F32))
        acc_qkv[cols, :] += t_mm(low, normed)
        term = mm(low, w_qkv[cols, :])
        grad_normed = term if grad_normed is None else grad_normed + term
    dsmall_ref[:, :D] += col_sum(grad_normed * xhat)
    dsmall_ref[:, D : 2 * D] += col_sum(grad_normed)
    grad_x = grad_mid + norm_back(grad_normed, xhat, rstd, gain)
    dx_ref[...] = grad_x.reshape(WIN, SIDE, IMAGES, D)
    if layer:
        last_strips(dx_ref, strips)

    @pl.when(step == STEPS - 1)
    def _():
        pack_attention(at_ref, acc_qkv, acc_proj, dpacks)
        for g in range(2):
            for a in range(4):
                dtab_ref[8 * g + a] = acc_tab[g, a, :, :AROWS]
                dtab_ref[8 * g + 4 + a] = acc_tab[g, a, :, AROWS:]


def mlp_forward_kernel(layer, n_packs, at_ref, mid_ref, *refs):
    packs, refs = refs[:n_packs], refs[n_packs:]
    small_ref, y_ref, *strips, act_ref, slope_ref, w_one, w_two = refs

    @pl.when(pl.program_id(0) == 0)
    def _():
        unpack_mlp(at_ref, packs, w_one, w_two)

    mid = mid_ref[...]
    xhat, _ = normalize(mid)
    gain = small_ref[layer : layer + 1, 2 * D : 3 * D]
    shift = small_ref[layer : layer + 1, 3 * D : 4 * D]
    normed = (xhat * gain + shift).astype(BF16)
    total = mid + small_ref[layer : layer + 1, 5 * D : 6 * D]

    def hidden(c):
        bias = small_ref[layer : layer + 1, 9 * D + c * CHUNK : 9 * D + (c + 1) * CHUNK]
        return mm(normed, w_one[:, c * CHUNK : (c + 1) * CHUNK]) + bias

    pre = hidden(0)
    for c in range(CHUNKS):
        following = hidden(c + 1) if c + 1 < CHUNKS else None
        act, slope = gelu_both(pre)
        act_ref[c] = act
        slope_ref[c] = slope
        total = total + mm_t(act, w_two[c])
        pre = following
    y_ref[...] = total.reshape(WIN, SIDE, IMAGES, D)
    first_strips(y_ref, strips)


def mlp_backward_kernel(layer, forward, n_packs, n_out, at_ref, mid_ref, dy_ref, *refs):
    strips, refs = refs[:3], refs[3:]
    if not forward:
        (act_ref, slope_ref), refs = refs[:2], refs[2:]
    packs, small_ref, refs = refs[:n_packs], refs[n_packs], refs[n_packs + 1 :]
    if forward:
        (y_ref, *out_strips), refs = refs[:4], refs[4:]
    gm_ref, dpacks, refs = refs[0], refs[1 : 1 + n_out], refs[1 + n_out :]
    dsmall_ref, w_one, w_two, acc_one, acc_two, moved = refs
    step = pl.program_id(0)

    @pl.when(step == 0)
    def _():
        unpack_mlp(at_ref, packs, w_one, w_two)
        for ref in (dsmall_ref, acc_one, acc_two):
            ref[...] = jnp.zeros(ref.shape, ref.dtype)

    mid = mid_ref[...]
    xhat, rstd = normalize(mid)
    gain = small_ref[layer : layer + 1, 2 * D : 3 * D]
    shift = small_ref[layer : layer + 1, 3 * D : 4 * D]
    normed = (xhat * gain + shift).astype(BF16)
    dy = (next_rows if forward else prev_rows)(dy_ref, strips, moved)
    dy_low = dy.astype(BF16)
    dsmall_ref[:, 5 * D : 6 * D] += col_sum(dy_low.astype(F32))
    total = None
    if forward:
        total = mid + small_ref[layer : layer + 1, 5 * D : 6 * D]

    def products(c):
        grad_act = mm(dy_low, w_two[c])
        if not forward:
            return None, grad_act
        bias = small_ref[layer : layer + 1, 9 * D + c * CHUNK : 9 * D + (c + 1) * CHUNK]
        return mm(normed, w_one[:, c * CHUNK : (c + 1) * CHUNK]) + bias, grad_act

    grad_normed = None
    normed_turned, dy_turned = normed.T, dy_low.T
    pre, grad_act = products(0)
    for c in range(CHUNKS):
        cols = slice(c * CHUNK, (c + 1) * CHUNK)
        following = products(c + 1) if c + 1 < CHUNKS else (None, None)
        if forward:
            act, slope = gelu_both(pre)
            total = total + mm_t(act, w_two[c])
        else:
            act = act_ref[c]
            slope = slope_ref[c]
        grad_pre = (grad_act * slope.astype(F32)).astype(BF16)
        dsmall_ref[:, 9 * D + c * CHUNK : 9 * D + (c + 1) * CHUNK] += col_sum(grad_pre.astype(F32))
        term = mm_t(grad_pre, w_one[:, cols])
        grad_normed = term if grad_normed is None else grad_normed + term
        acc_one[:, cols] += mm(normed_turned, grad_pre)
        acc_two[c] += mm(dy_turned, act)
        pre, grad_act = following
    dsmall_ref[:, 2 * D : 3 * D] += col_sum(grad_normed * xhat)
    dsmall_ref[:, 3 * D : 4 * D] += col_sum(grad_normed)
    gm_ref[...] = dy + norm_back(grad_normed, xhat, rstd, gain)
    if forward:
        moved[...] = total.reshape(WIN, SIDE, IMAGES, D)
        last_strips(moved, out_strips)

        def place(a):
            if a == 0:
                y_ref[SHIFT : SHIFT + WIN, SHIFT:] = moved[:, :KEPT]
            else:
                y_ref[SHIFT + WIN :, SHIFT:] = moved[: WIN - SHIFT, :KEPT]

        both_steps(place)

    @pl.when(step == STEPS - 1)
    def _():
        pack_mlp(at_ref, acc_one, acc_two, dpacks)


def fixed(shape):
    return pl.BlockSpec(shape, lambda s: (0,) * len(shape), pipeline_mode=pl.Buffered(1))


def stepped(shape, axis=0):
    return pl.BlockSpec(shape, lambda s: tuple(s if d == axis else 0 for d in range(len(shape))))


def call(kernel, ins, in_specs, outs, scratch, flops, moved_bytes, vmem):
    return pl.pallas_call(
        kernel,
        grid=(STEPS,),
        in_specs=in_specs,
        out_shape=[jax.ShapeDtypeStruct(shape, kind) for shape, kind, _ in outs],
        out_specs=[spec for _, _, spec in outs],
        scratch_shapes=scratch,
        compiler_params=pltpu.CompilerParams(
            dimension_semantics=("arbitrary",), vmem_limit_bytes=vmem * MIB
        ),
        cost_estimate=pl.CostEstimate(
            flops=int(flops), bytes_accessed=int(moved_bytes), transcendentals=0
        ),
    )(*ins)


GRID = (SIDE, SIDE, IMAGES, D)
GRID_STEP = stepped((WIN, SIDE, IMAGES, D))
ROWS_STEP = stepped((STEP_ROWS, D))
WINDOWS_STEP = stepped((STEP_WINDOWS, AROWS, 3 * D))
PROBS_STEP = stepped((STEP_WINDOWS, 2, 4 * AROWS, LANES))
HIDDEN_STEP = stepped((CHUNKS, STEP_ROWS, CHUNK), 1)
STRIPS = ((SHIFT, KEPT, IMAGES, D), (KEPT, SHIFT, IMAGES, D), (SHIFT, SHIFT, IMAGES, D))
STRIP_SPECS = [fixed(shape) for shape in STRIPS]
STRIP_OUTS = [(shape, BF16, fixed(shape)) for shape in STRIPS]
SCALARS = pl.BlockSpec(memory_space=pltpu.SMEM)
SHARD_A = (N_QKV + N_OUT, HALF)
SHARD_B = (N_FC1 + 4 * N_OUT, HALF)
ROW_SUMS = 9 * D + MLP
MOVED = pltpu.VMEM((WIN, SIDE, IMAGES, D), F32)


def tiles_of(features):
    return pltpu.VMEM((features // LANES, STEP_ROWS + IMAGES, LANES), F32)


def pack_specs(packs, shard):
    at = 0 if shard == SHARD_B else packs[0].shape[-2] // shard[0] - 1
    lead = packs[0].shape[:-2]
    return [
        pl.BlockSpec(
            lead + shard, lambda s: (0,) * len(lead) + (at, 0), pipeline_mode=pl.Buffered(1)
        )
    ] * len(packs)


def pack_outs(shard, single):
    if single:
        return [((32,) + shard, BF16, fixed((32,) + shard))]
    return [((4, 4) + shard, BF16, fixed((4, 4) + shard))] * 2


def attention_forward(layer, at, grid_field, strips, packs, small, base):
    out = call(
        partial(attention_forward_kernel, layer, len(packs)),
        (at, grid_field, *strips, *packs, small, base),
        [SCALARS, fixed(GRID) if layer else GRID_STEP]
        + STRIP_SPECS[: len(strips)]
        + pack_specs(packs, SHARD_A)
        + [fixed(small.shape), fixed(base.shape)],
        [((ROWS, D), F32, ROWS_STEP)] * layer
        + [
            ((STEPS * STEP_WINDOWS, AROWS, 3 * D), BF16, WINDOWS_STEP),
            ((STEPS * STEP_WINDOWS, 2, 4 * AROWS, LANES), BF16, PROBS_STEP),
            ((ROWS, D), BF16, ROWS_STEP),
            ((ROWS, D), F32, ROWS_STEP),
        ],
        [
            pltpu.VMEM((3 * D, D), BF16),
            pltpu.VMEM((D, D), BF16),
            tiles_of(3 * D),
            tiles_of(D),
            pltpu.VMEM((4 if layer else 1, 2, 4, WROWS, 2 * AROWS), F32),
        ]
        + [MOVED] * layer,
        2 * ROWS * 4 * D * D * 2,
        30e6,
        28,
    )
    return (list(out[:-1]) if layer else [grid_field] + list(out[:-1])), out[-1]


def attention_backward(layer, at, grad_mid, saved, packs, small, rest, single):
    outs = pack_outs(SHARD_A, single)
    out = call(
        partial(attention_backward_kernel, layer, len(packs), len(outs)),
        (at, grad_mid, *saved, *packs, small, rest),
        [
            SCALARS,
            ROWS_STEP,
            ROWS_STEP if layer else GRID_STEP,
            WINDOWS_STEP,
            PROBS_STEP,
            ROWS_STEP,
        ]
        + pack_specs(packs, SHARD_A)
        + [fixed(small.shape), fixed(rest.shape)],
        [(GRID, F32, GRID_STEP)]
        + STRIP_OUTS[: 3 * layer]
        + outs
        + [
            ((HEADS, WROWS, AROWS), F32, fixed((HEADS, WROWS, AROWS))),
            ((1, ROW_SUMS), F32, fixed((1, ROW_SUMS))),
        ],
        [
            pltpu.VMEM((3 * D, D), BF16),
            pltpu.VMEM((D, D), BF16),
            tiles_of(D),
            tiles_of(3 * D),
            pltpu.VMEM((3 * D, D), F32),
            pltpu.VMEM((D, D), F32),
            pltpu.VMEM((2, 4, WROWS, 2 * AROWS), F32),
        ],
        2 * ROWS * 4 * D * D * 5,
        30e6,
        32,
    )
    at_pack = 1 + 3 * layer
    return out[0], out[1:at_pack], out[at_pack:-2], out[-2], out[-1]


MLP_WEIGHTS = [pltpu.VMEM((D, MLP), BF16), pltpu.VMEM((CHUNKS, D, CHUNK), BF16)]


def mlp_forward(layer, at, mid, packs, small):
    out = call(
        partial(mlp_forward_kernel, layer, len(packs)),
        (at, mid, *packs, small),
        [SCALARS, ROWS_STEP] + pack_specs(packs, SHARD_B) + [fixed(small.shape)],
        [(GRID, F32, GRID_STEP)]
        + STRIP_OUTS
        + [((CHUNKS, ROWS, CHUNK), BF16, HIDDEN_STEP)] * 2,
        MLP_WEIGHTS,
        2 * ROWS * 2 * D * MLP,
        26e6,
        26,
    )
    return out[0], out[1:4], out[4:]


def mlp_backward(layer, at, mid, dy, strips, saved, packs, small, single):
    outs = pack_outs(SHARD_B, single)
    forward = not saved
    extra = 4 if forward else 0
    out = call(
        partial(mlp_backward_kernel, layer, forward, len(packs), len(outs)),
        (at, mid, dy, *strips, *saved, *packs, small),
        [SCALARS, ROWS_STEP, fixed(GRID)]
        + STRIP_SPECS
        + [HIDDEN_STEP] * len(saved)
        + pack_specs(packs, SHARD_B)
        + [fixed(small.shape)],
        ([(GRID, F32, fixed(GRID))] + STRIP_OUTS)[:extra]
        + [((ROWS, D), F32, ROWS_STEP)]
        + outs
        + [((1, ROW_SUMS), F32, fixed((1, ROW_SUMS)))],
        MLP_WEIGHTS
        + [pltpu.VMEM((D, MLP), F32), pltpu.VMEM((CHUNKS, D, CHUNK), F32), MOVED],
        2 * ROWS * (6 if forward else 4) * D * MLP,
        30e6,
        58 if forward else 38,
    )
    return out[:extra], out[extra], out[extra + 1 : -1], out[-1]


def moved(x, step_of):
    sizes = [lax.axis_size(axis) for axis in AXES]

    def flat(i, r, c):
        return (i * sizes[1] + r) * sizes[2] + c

    pairs = [
        (flat(i, r, c), flat(*step_of(i, r, c)))
        for i in range(sizes[0])
        for r in range(sizes[1])
        for c in range(sizes[2])
    ]
    return lax.ppermute(x, AXES, pairs)


def swapped(x, img=0, down=0, core=0, across=0):
    return moved(x, lambda i, r, c: (i ^ img, r ^ (2 * down + core), c ^ across))


def send_strips(strips, by):
    rows, cols = lax.axis_size("row"), lax.axis_size("col")
    low, right, corner = strips
    return (
        moved(low, lambda i, r, c: (i, (r + by) % rows, c)),
        moved(right, lambda i, r, c: (i, r, (c + by) % cols)),
        moved(corner, lambda i, r, c: (i, (r + by) % rows, (c + by) % cols)),
    )


def fill_prev(grid_field, strips):
    high, left, corner = (strip.astype(F32) for strip in strips)
    grid_field = lax.dynamic_update_slice(grid_field, high, (0, SHIFT, 0, 0))
    grid_field = lax.dynamic_update_slice(grid_field, left, (SHIFT, 0, 0, 0))
    return lax.dynamic_update_slice(grid_field, corner, (0, 0, 0, 0))


QUADS = ((0, 0), (0, 1), (1, 0), (1, 1))


def after(values, *others):
    return lax.optimization_barrier((values, others))[0]


def together(*values):
    return lax.optimization_barrier(values)


def is_small():
    return lax.axis_size("img") == 2


def gather_line(pack):
    if not is_small():
        return pack
    return jnp.stack([pack] + [swapped(pack, across=m) for m in (1, 2, 3)])


def gather_quad(line):
    return jnp.stack([line] + [swapped(line, img=i, down=y) for i, y in QUADS[1:]])


def gather_whole(pack, canonical):
    whole = lax.all_gather(pack, AXES, axis=0, tiled=False)
    if not is_small():
        whole = canonical(whole.reshape((lax.axis_size("img"), 16) + pack.shape))
        whole = whole.reshape((32,) + whole.shape[2:])
    return (whole,)


def scatter_whole(whole, in_shards):
    if not is_small():
        whole = in_shards(whole.reshape((2, 16) + whole.shape[1:]), lax.axis_size("img"))
    flat = whole.reshape(-1, whole.shape[-1])
    return lax.psum_scatter(flat, AXES, scatter_dimension=0, tiled=True)


def scatter_plane(whole):
    if not is_small():
        return whole
    flat = whole.reshape(-1, whole.shape[-1])
    part = lax.psum_scatter(flat, ("img", "row"), scatter_dimension=0, tiled=True)
    return part.reshape((4,) + whole.shape[1:])


def scatter_col(part, in_shards):
    if not is_small():
        return scatter_whole(part, in_shards)
    flat = part.reshape(-1, part.shape[-1])
    return lax.psum_scatter(flat, "col", scatter_dimension=0, tiled=True)


def pair_swap(packs):
    return swapped(packs[1], core=1) if is_small() else packs


def scatter_pair(packs, got):
    if not is_small():
        return packs
    half = packs[0].astype(F32) + got.astype(F32)
    return [half[0]] + [half[m].astype(BF16) for m in (1, 2, 3)]


def quad_swaps(halves):
    if not is_small():
        return []
    return [swapped(h, img=i, down=y) for h, (i, y) in zip(halves[1:], QUADS[1:])]


def scatter_quad(halves, got):
    if not is_small():
        return halves
    got = [g.astype(F32) for g in got]
    line = (halves[0] + got[0]) + (got[1] + got[2])
    return [line[0]] + [line[m].astype(BF16) for m in (1, 2, 3)]


def near_swap(x):
    return swapped(x, across=1)


def far_swap(x):
    return swapped(x, across=2)


def line_swaps(line):
    return [swapped(line[m], across=m) for m in (1, 2, 3)] if is_small() else []


def padded_index(rel_index):
    cells = rel_index.T.reshape(WIN, WIN, WIN, WIN)
    gap = (0, SLOT - WIN)
    cells = jnp.pad(cells, [(0, 0), gap, (0, AROWS // SLOT - WIN), gap], constant_values=-1)
    return cells.reshape(1, WROWS * AROWS)


def packing_kernel(w_qkv, w_proj, w_fc1, w_fc2, first_a, second_a, first_b, second_b):
    for l, (pack_a, pack_b) in enumerate(((first_a, first_b), (second_a, second_b))):
        pack_a[:N_QKV] = w_qkv[l].astype(BF16)
        pack_a[N_QKV:] = w_proj[l].astype(BF16)
        for h in range(2):
            pack_b[:N_FC1, h * LANES : (h + 1) * LANES] = w_fc1[
                l, h * LANES : (h + 1) * LANES, :
            ].astype(BF16)
        for k in range(4):
            pack_b[N_FC1 + k * N_OUT : N_FC1 + (k + 1) * N_OUT] = w_fc2[
                l, :, k * HALF : (k + 1) * HALF
            ].astype(BF16)


def turned(matrices):
    w_qkv, w_proj, w_fc1, w_fc2 = matrices
    return w_qkv.swapaxes(1, 2), w_proj.swapaxes(1, 2), w_fc1, w_fc2.swapaxes(1, 2)


def make_packs(masters):
    w_qkv, w_proj, w_fc1, w_fc2 = turned(masters)
    if is_small():
        kinds = [jax.ShapeDtypeStruct(shape, BF16) for shape in (SHARD_A, SHARD_A, SHARD_B, SHARD_B)]
        return pl.pallas_call(
            packing_kernel,
            out_shape=kinds,
            compiler_params=pltpu.CompilerParams(vmem_limit_bytes=16 * MIB),
        )(w_qkv, w_proj, w_fc1, w_fc2)
    cols = w_qkv.shape[2]
    packs = [jnp.concatenate([w_qkv[l], w_proj[l]], axis=0).astype(BF16) for l in range(2)]
    for l in range(2):
        second = w_fc2[l].reshape(N_OUT, 4, cols).transpose(1, 0, 2).reshape(-1, cols)
        packs.append(jnp.concatenate([w_fc1[l].T, second], axis=0).astype(BF16))
    return packs


def update_kernel(kinds, total_of, n_sums, rates, *refs):
    sums, refs = refs[:n_sums], refs[n_sums:]
    count = len(rates)
    ins, outs = refs[: 3 * count], refs[3 * count :]
    for l in range(2):
        total = total_of(l, sums)
        for k, grad in enumerate(kinds(total)):
            rate, decay = rates[k]
            new = adam_step(*(ins[3 * k + m][l] for m in range(3)), grad, rate, decay)
            for m in range(3):
                outs[3 * k + m][l] = new[m]


def attention_total(layer, sums):
    if layer:
        return sums[4][: SHARD_A[0]].astype(F32)
    near, far, both = (s[...].astype(F32) for s in sums[1:4])
    return (sums[0][...] + near) + (far + both)


def mlp_total(layer, sums):
    return (sums[1][...] if layer else sums[0][SHARD_A[0] :]).astype(F32)


def attention_kinds(total):
    return total[:N_QKV], total[N_QKV:]


def mlp_kinds(total):
    first = jnp.concatenate([total[:N_FC1, :LANES], total[:N_FC1, LANES:]], axis=0)
    second = [total[N_FC1 + k * N_OUT : N_FC1 + (k + 1) * N_OUT] for k in range(4)]
    return first, jnp.concatenate(second, axis=1)


def update(kinds, total_of, sums, arrays):
    rates = ((RATE_MATRIX, DECAY_MATRIX),) * (len(arrays) // 3)
    return pl.pallas_call(
        partial(update_kernel, kinds, total_of, len(sums), rates),
        out_shape=[jax.ShapeDtypeStruct(x.shape, F32) for x in arrays],
        compiler_params=pltpu.CompilerParams(vmem_limit_bytes=16 * MIB),
    )(*sums, *arrays)


def attention_canonical(whole):
    _, ranks, rows, _ = whole.shape
    whole = whole.transpose(1, 2, 0, 3).reshape(ranks, rows, 2, HALF)
    return whole.transpose(2, 0, 1, 3)


def attention_shards(pack, size):
    _, ranks, rows, _ = pack.shape
    pack = pack.transpose(1, 2, 0, 3).reshape(ranks, rows, size, D // size)
    return pack.transpose(2, 0, 1, 3)


def mlp_canonical(whole):
    size, ranks, _, cols = whole.shape
    first = attention_canonical(whole[:, :, :N_FC1]).swapaxes(2, 3)
    first = first.reshape(2, ranks, 2, LANES, N_FC1).transpose(0, 1, 3, 2, 4).reshape(2, ranks, LANES, HALF)
    second = whole[:, :, N_FC1:].reshape(size, ranks, 4, N_OUT, cols)
    second = second.transpose(1, 3, 0, 2, 4).reshape(ranks, N_OUT, 2, 4, HALF)
    second = second.transpose(2, 0, 3, 1, 4).reshape(2, ranks, 4 * N_OUT, HALF)
    return jnp.concatenate([first, second], axis=2)


def mlp_shards(pack, size):
    _, ranks, _, _ = pack.shape
    cols = D // size
    first = pack[:, :, :N_FC1].reshape(2, ranks, LANES, 2, N_FC1).transpose(0, 1, 3, 2, 4)
    first = attention_shards(first.reshape(2, ranks, HALF, N_FC1).swapaxes(2, 3), size)
    second = pack[:, :, N_FC1:].reshape(2, ranks, 4, N_OUT, HALF)
    second = second.transpose(1, 3, 0, 2, 4).reshape(ranks, N_OUT, size, 4, cols)
    second = second.transpose(2, 0, 3, 1, 4).reshape(size, ranks, 4 * N_OUT, cols)
    return jnp.concatenate([first, second], axis=2)


def adam_step(weight, moment_one, second, gradient, rate_value, decay_rate):
    moment_one = BETA_ONE * moment_one + (1.0 - BETA_ONE) * gradient
    second = BETA_TWO * second + (1.0 - BETA_TWO) * gradient * gradient
    update = (
        moment_one / (1.0 - BETA_ONE**STEP) / (jnp.sqrt(second / (1.0 - BETA_TWO**STEP)) + EPS_ADAM)
    )
    return (weight - rate_value * (update + decay_rate * weight), moment_one, second)


def shards(
    images,
    grad_out,
    w_qkv,
    w_proj,
    w_fc1,
    w_fc2,
    first_qkv,
    first_proj,
    first_fc1,
    first_fc2,
    second_qkv,
    second_proj,
    second_fc1,
    second_fc2,
    small_params,
    small_first,
    small_second,
    rel_index,
):
    assert images.shape == (IMAGES, SIDE, SIDE, D)
    size = lax.axis_size("img")
    small = is_small()
    row, col = lax.axis_index("row"), lax.axis_index("col")
    last = [row == lax.axis_size("row") - 1, col == lax.axis_size("col") - 1]
    place = [lax.axis_index("img"), row // 2, row % 2, col]
    at = jnp.stack([jnp.asarray(value, jnp.int32) for value in place + last])
    images = images.transpose(1, 2, 0, 3)
    grad_out = grad_out.transpose(1, 2, 0, 3)

    onehot = (
        jnp.arange(RELPOS, dtype=jnp.int32)[:, None] == padded_index(rel_index)
    ).astype(F32)
    tables = small_params[:, 9 * D + MLP :].reshape(2, RELPOS, HEADS)
    base = jnp.einsum("lrh,rp->lhp", tables * LOG2E, onehot, precision=lax.Precision.HIGHEST)
    base = base.reshape(2, HEADS, WROWS, AROWS)
    masters = (w_qkv, w_proj, w_fc1, w_fc2)
    pack_a_zero, pack_a_one, pack_b_zero, pack_b_one = make_packs(masters)
    if small:
        line_a = gather_line(pack_a_zero)
        pair_b = jnp.stack([pack_b_zero, near_swap(pack_b_zero)])
        pair_a = jnp.stack([pack_a_one, near_swap(pack_a_one)])
        got, far_b, at, base = together(quad_swaps([line_a] * 4), far_swap(pair_b), at, base)
        quad = jnp.stack([line_a, *got])
        packs_a_zero = quad, swapped(quad, core=1)
        line_b = jnp.concatenate([pair_b, far_b])
    else:
        packs_a_zero = gather_whole(pack_a_zero, attention_canonical)
        packs_b_zero = gather_whole(pack_b_zero, mlp_canonical)
        packs_a_one = gather_whole(pack_a_one, attention_canonical)
        packs_b_one = gather_whole(pack_b_one, mlp_canonical)

    grad_strips = (
        grad_out[:SHIFT, SHIFT:].astype(BF16),
        grad_out[SHIFT:, :SHIFT].astype(BF16),
        grad_out[:SHIFT, :SHIFT].astype(BF16),
    )

    def table_row(sums, dtab):
        table = jnp.einsum(
            "hp,rp->rh", dtab.reshape(HEADS, -1), onehot, precision=lax.Precision.HIGHEST
        )
        return jnp.concatenate([sums, table.reshape(1, -1)], axis=1)

    packs_a_zero = after(packs_a_zero, grad_strips)
    saved_zero, mid_zero = attention_forward(0, at, images, (), packs_a_zero, small_params, base[0])
    if small:
        mid_zero, got, far_a = together(mid_zero, quad_swaps([line_b] * 4), far_swap(pair_a))
        quad = jnp.stack([line_b, *got])
        packs_b_zero = quad, swapped(quad, core=1)
        line_a = jnp.concatenate([pair_a, far_a])
        packs_b_one = gather_whole(after(pack_b_one, mid_zero), mlp_canonical)
    grad_strips = send_strips(after(grad_strips, mid_zero), -1)
    out_zero, strips, hidden_zero = mlp_forward(0, at, mid_zero, packs_b_zero, small_params)
    strips, grad_strips = together(strips, grad_strips)
    if small:
        strips, got = together(strips, quad_swaps([line_a] * 4))
        quad = jnp.stack([line_a, *got])
        strips, other = together(send_strips(strips, -1), swapped(quad, core=1))
        packs_a_one = quad, other
    else:
        strips = send_strips(strips, -1)
    saved_one, mid_one = attention_forward(
        1, at, out_zero, strips, packs_a_one, small_params, base[1]
    )
    (out_one, *out_strips), gm_one, dpacks, rest = mlp_backward(
        1, at, mid_one, grad_out, grad_strips, (), packs_b_one, small_params, True
    )

    plane_b_one = scatter_plane(dpacks[0])
    dx_one, strips, dpacks, dtab_one, sums = attention_backward(
        1, at, gm_one, saved_one, packs_a_one, small_params, rest, True
    )
    plane_a_one = scatter_plane(dpacks[0])
    strips, row_one = together(send_strips(strips, 1), table_row(sums, dtab_one))
    out_strips = send_strips(after(out_strips, strips), 1)
    _, gm_zero, dpacks, rest = mlp_backward(
        0, at, mid_zero, dx_one, strips, hidden_zero, packs_b_zero, small_params, not small
    )

    dpacks, out_strips, plane_b_one = together(dpacks, out_strips, plane_b_one)
    got, out_one = together(pair_swap(dpacks), fill_prev(out_one, out_strips))
    outputs = out_one.transpose(2, 0, 1, 3)
    halves_b_zero = scatter_pair(dpacks, got)
    gm_zero, halves_b_zero = together(gm_zero, halves_b_zero)
    sum_b_one = scatter_col(plane_b_one, mlp_shards)
    grad_input, _, dpacks, dtab_zero, sums = attention_backward(
        0, at, gm_zero, saved_zero, packs_a_zero, small_params, rest, not small
    )
    grad_input = grad_input.transpose(2, 0, 1, 3)

    dpacks, got_b, sum_b_one, plane_a_one = together(
        dpacks, quad_swaps(halves_b_zero), sum_b_one, plane_a_one
    )
    if small:
        line_b = scatter_quad(halves_b_zero, got_b)
        line_b = jnp.stack([line_b[0].astype(BF16), *line_b[1:]])
        sum_mixed = scatter_col(jnp.concatenate([plane_a_one, line_b], axis=1), None)
    else:
        sum_mixed = jnp.concatenate(
            [scatter_whole(plane_a_one, attention_shards), scatter_whole(halves_b_zero[0], mlp_shards)]
        )
    got, row_zero = together(pair_swap(dpacks), table_row(sums, dtab_zero))
    halves_a = scatter_pair(dpacks, got)
    small_grad = jnp.concatenate([row_zero, row_one], axis=0)

    def small_swaps(*steps):
        return [swapped(small_grad, **step) for step in steps] if small else []

    got, parts = together(quad_swaps(halves_a), small_swaps({"core": 1}))
    line_a = scatter_quad(halves_a, got)
    small_grad = sum(parts, small_grad)
    steps = [{"img": i, "down": y} for i, y in QUADS[1:]]
    sums_a, parts = together(line_swaps(line_a), small_swaps(*steps))
    if small:
        small_grad = (small_grad + parts[0]) + (parts[1] + parts[2])
        parts = small_swaps(*({"across": m} for m in (1, 2, 3)))
        small_grad = (small_grad + parts[0]) + (parts[1] + parts[2])
    else:
        small_grad = lax.psum(small_grad, AXES)

    states = [turned(group) for group in (
        masters,
        (first_qkv, first_proj, first_fc1, first_fc2),
        (second_qkv, second_proj, second_fc1, second_fc2),
    )]
    if small:
        new_a = update(
            attention_kinds,
            attention_total,
            (line_a[0], *sums_a, sum_mixed),
            [s[k] for k in (0, 1) for s in states],
        )
        new_b = update(
            mlp_kinds, mlp_total, (sum_mixed, sum_b_one), [s[k] for k in (2, 3) for s in states]
        )
    else:
        cols = D // size
        total_a = [scatter_whole(line_a[0], attention_shards), sum_mixed[: SHARD_A[0]]]
        total_b = [sum_mixed[SHARD_A[0] :], sum_b_one]
        kinds = (
            [t[:N_QKV] for t in total_a],
            [t[N_QKV:] for t in total_a],
            [t[:N_FC1].T for t in total_b],
            [t[N_FC1:].reshape(4, N_OUT, cols).transpose(1, 0, 2).reshape(N_OUT, -1) for t in total_b],
        )
        new = []
        for k in range(4):
            grad = jnp.stack(kinds[k]).astype(F32)
            new += adam_step(*(s[k] for s in states), grad, RATE_MATRIX, DECAY_MATRIX)
        new_a, new_b = new[:6], new[6:]
    small_new = adam_step(small_params, small_first, small_second, small_grad, RATE_SMALL, 0.0)
    new = list(new_a) + list(new_b)
    new = [turned(new[m::3]) for m in range(3)]
    return (outputs, grad_input) + new[0] + new[1] + new[2] + tuple(small_new)


def solution(mesh):
    grid_spec = P("img", "row", "col", None)
    matrix = P(None, "img", ("row", "col"))
    in_specs = (grid_spec,) * 2 + (matrix,) * 12 + (P(),) * 4
    out_specs = (grid_spec,) * 2 + (matrix,) * 12 + (P(),) * 3
    return jax.shard_map(shards, mesh=mesh, in_specs=in_specs, out_specs=out_specs, check_vma=False)
```

```python
from functools import partial

import jax
import jax.numpy as jnp
from jax import lax
from jax.experimental import pallas as pl
from jax.experimental.pallas import tpu as pltpu
from jax.sharding import PartitionSpec as P

D = 512
HEADS = 16
HEAD_DIM = 32
MLP = 2048
WIN = 7
SHIFT = 3
STEP = 10
RELPOS = 169

EPS_NORM = 1e-05
BETA_ONE = 0.9
BETA_TWO = 0.999
EPS_ADAM = 1e-08
RATE_MATRIX = 0.05
RATE_SMALL = 0.3
DECAY_MATRIX = 0.05
MASKED = -1e30

AXES = ("img", "row", "col")
F32 = jnp.float32
BF16 = jnp.bfloat16
LOG2E = 1.4426950408889634
SCALE = HEAD_DIM ** (-0.5)

SIDE = 2 * WIN
IMAGES = 8
SLOT = 8
WROWS = WIN * SLOT
AROWS = 64
STEPS = 2
STEP_ROWS = WIN * SIDE * IMAGES
ROWS = STEPS * STEP_ROWS
STEP_WINDOWS = 2 * IMAGES
KEPT = SIDE - SHIFT
CHUNK = 512
CHUNKS = MLP // CHUNK
HALF = D // 2
LANES = 128
MIB = 1024 * 1024


def mm(left, right):
    return lax.dot_general(left, right, (((1,), (0,)), ((), ())), preferred_element_type=F32)


def mm_t(left, right):
    return lax.dot_general(left, right, (((1,), (1,)), ((), ())), preferred_element_type=F32)


def t_mm(left, right):
    return lax.dot_general(left, right, (((0,), (0,)), ((), ())), preferred_element_type=F32)


def col_sum(value):
    return jnp.sum(value, axis=0, keepdims=True)


def normalize(rows):
    center = rows - jnp.mean(rows, axis=-1, keepdims=True)
    spread = jnp.mean(center * center, axis=-1, keepdims=True)
    rstd = lax.rsqrt(spread + EPS_NORM)
    return center * rstd, rstd


def norm_back(grad, xhat, rstd, gain):
    scaled = grad * gain
    mean_one = jnp.mean(scaled, axis=-1, keepdims=True)
    mean_two = jnp.mean(scaled * xhat, axis=-1, keepdims=True)
    return rstd * (scaled - mean_one - xhat * mean_two)


def gelu_both(pre):
    pre = pre.astype(BF16)
    t = 1.0 / (1.0 + jnp.abs(pre) * (0.3275911 * 0.7071067811865476))
    bell = jnp.exp2(pre * pre * (-0.5 * LOG2E))
    poly = t * (0.5 * 1.061405429) + 0.5 * -1.453152027
    poly = poly * t + 0.5 * 1.421413741
    poly = poly * t + 0.5 * -0.284496736
    poly = poly * t + 0.5 * 0.254829592
    tail = poly * t * bell
    cdf = jnp.where(pre >= 0.0, 1.0 - tail, tail)
    return pre * cdf, cdf + pre * bell * 0.3989422804014327


def both_steps(body):
    for a in range(STEPS):
        pl.when(pl.program_id(0) == a)(partial(body, a))


def next_rows(grid_ref, strip_refs, rows_ref):
    low_ref, right_ref, corner_ref = strip_refs

    def body(a):
        if a == 0:
            rows_ref[:, :KEPT] = grid_ref[SHIFT : SHIFT + WIN, SHIFT:]
            rows_ref[:, KEPT:] = right_ref[:WIN].astype(F32)
        else:
            rows_ref[: WIN - SHIFT, :KEPT] = grid_ref[SHIFT + WIN :, SHIFT:]
            rows_ref[: WIN - SHIFT, KEPT:] = right_ref[WIN:].astype(F32)
            rows_ref[WIN - SHIFT :, :KEPT] = low_ref[...].astype(F32)
            rows_ref[WIN - SHIFT :, KEPT:] = corner_ref[...].astype(F32)

    both_steps(body)
    return rows_ref[...].reshape(STEP_ROWS, D)


def prev_rows(grid_ref, strip_refs, rows_ref):
    high_ref, left_ref, corner_ref = strip_refs

    def body(a):
        if a == 0:
            rows_ref[:SHIFT, SHIFT:] = high_ref[...].astype(F32)
            rows_ref[:SHIFT, :SHIFT] = corner_ref[...].astype(F32)
            rows_ref[SHIFT:, SHIFT:] = grid_ref[: WIN - SHIFT, :KEPT]
            rows_ref[SHIFT:, :SHIFT] = left_ref[: WIN - SHIFT].astype(F32)
        else:
            rows_ref[:, SHIFT:] = grid_ref[WIN - SHIFT : KEPT, :KEPT]
            rows_ref[:, :SHIFT] = left_ref[WIN - SHIFT :].astype(F32)

    both_steps(body)
    return rows_ref[...].reshape(STEP_ROWS, D)


def first_strips(block_ref, strip_refs):
    rows_ref, cols_ref, corner_ref = strip_refs

    def body(a):
        if a == 0:
            rows_ref[...] = block_ref[:SHIFT, SHIFT:].astype(BF16)
            cols_ref[: WIN - SHIFT] = block_ref[SHIFT:, :SHIFT].astype(BF16)
            corner_ref[...] = block_ref[:SHIFT, :SHIFT].astype(BF16)
        else:
            cols_ref[WIN - SHIFT :] = block_ref[:, :SHIFT].astype(BF16)

    both_steps(body)


def last_strips(block_ref, strip_refs):
    rows_ref, cols_ref, corner_ref = strip_refs

    def body(a):
        if a == 0:
            cols_ref[:WIN] = block_ref[:, KEPT:].astype(BF16)
        else:
            cols_ref[WIN:] = block_ref[: WIN - SHIFT, KEPT:].astype(BF16)
            rows_ref[...] = block_ref[WIN - SHIFT :, :KEPT].astype(BF16)
            corner_ref[...] = block_ref[WIN - SHIFT :, KEPT:].astype(BF16)

    both_steps(body)


def put_tiles(tiles, first, value):
    for t in range(value.shape[1] // LANES):
        tiles[first + t, :STEP_ROWS, :] = value[:, t * LANES : (t + 1) * LANES]


def get_tiles(tiles, first, count):
    return jnp.concatenate([tiles[first + t, :STEP_ROWS, :] for t in range(count)], axis=1)


def clear_tail(tiles):
    tiles[:, STEP_ROWS:, :] = jnp.zeros(tiles[:, STEP_ROWS:, :].shape, F32)


def window_at(b, n, r):
    return b * WIN * IMAGES + r * SIDE * IMAGES + n


def get_window(tiles, first, b, n):
    return jnp.concatenate(
        [
            jnp.concatenate(
                [
                    tiles[first + t, pl.ds(window_at(b, n, r), SLOT, stride=IMAGES), :]
                    for r in range(WIN)
                ],
                axis=0,
            )
            for t in range(2)
        ],
        axis=1,
    )


def put_window(tiles, first, b, n, value):
    for t in range(2):
        for r in range(WIN):
            tiles[first + t, pl.ds(window_at(b, n, r), WIN, stride=IMAGES), :] = value[
                r * SLOT : r * SLOT + WIN, t * LANES : (t + 1) * LANES
            ]


def to_sixty_four(window):
    padding = jnp.zeros((AROWS - WROWS, window.shape[1]), F32)
    return jnp.concatenate([window, padding], axis=0).astype(BF16)


def head_masks():
    lane = lax.broadcasted_iota(jnp.int32, (16, HALF), 1)
    head = jnp.bitwise_and(lax.shift_right_logical(lane, 5), 3)
    return [jnp.where(head == a, 1.0, 0.0).astype(BF16) for a in range(4)]


def stack_heads(part, masks):
    split = part.reshape(AROWS // 16, 16, HALF)
    return jnp.concatenate(
        [(split * mask[None]).reshape(AROWS, HALF) for mask in masks], axis=0
    )


def stack_halves(part):
    zero = jnp.zeros((AROWS, HALF // 2), part.dtype)
    return jnp.concatenate(
        [
            jnp.concatenate([part[:, : HALF // 2], zero], axis=1),
            jnp.concatenate([zero, part[:, HALF // 2 :]], axis=1),
        ],
        axis=0,
    )


def pick_halves(result):
    return jnp.concatenate(
        [result[:WROWS, : HALF // 2], result[AROWS : AROWS + WROWS, HALF // 2 :]], axis=1
    )


def pick_heads(result):
    lane = lax.broadcasted_iota(jnp.int32, (WROWS, HALF), 1)
    head = jnp.bitwise_and(lax.shift_right_logical(lane, 5), 3)
    picked = result[3 * AROWS : 3 * AROWS + WROWS]
    for a in (2, 1, 0):
        picked = jnp.where(head == a, result[a * AROWS : a * AROWS + WROWS], picked)
    return picked


def pad_keys(value):
    padding = jnp.zeros((4, AROWS - WROWS, 128), F32)
    return jnp.concatenate([value, padding], axis=1).astype(BF16).reshape(4 * AROWS, 128)


def places(at_ref, packs, turn=True):
    if len(packs) == 1:
        for shard in range(packs[0].shape[0]):
            yield 0, (shard,), shard // 16, shard % 16
        return
    for core in range(2):
        for quad in range(4):
            for across in range(4):
                i = jnp.bitwise_xor(at_ref[0], quad >> 1)
                y = jnp.bitwise_xor(at_ref[1], quad & 1)
                c = jnp.bitwise_xor(at_ref[2], core)
                z = jnp.bitwise_xor(at_ref[3], across) if turn else across
                yield core, (quad, across), i, (2 * y + c) * 4 + z


def piece(start, length):
    if isinstance(start, int):
        return pl.ds(start * length, length)
    return pl.ds(pl.multiple_of(start * length, length), length)


N_QKV = 3 * D // 16
N_OUT = D // 16
N_FC1 = MLP // 16


def unpack_attention(at_ref, packs, w_qkv, w_proj):
    for core, at, i, r in places(at_ref, packs):
        cols = piece(i, HALF)
        w_qkv[piece(r, N_QKV), cols] = packs[core][at + (slice(0, N_QKV),)]
        w_proj[piece(r, N_OUT), cols] = packs[core][at + (slice(N_QKV, None),)]


def pack_attention(at_ref, g_qkv, g_proj, packs):
    for core, at, i, r in places(at_ref, packs):
        cols = piece(i, HALF)
        packs[core][at + (slice(0, N_QKV),)] = g_qkv[piece(r, N_QKV), cols].astype(BF16)
        packs[core][at + (slice(N_QKV, None),)] = g_proj[piece(r, N_OUT), cols].astype(BF16)


def unpack_mlp(at_ref, packs, w_one, w_two):
    for core, at, i, r in places(at_ref, packs):
        for h in range(2):
            w_one[piece(2 * i + h, LANES), piece(r, N_FC1)] = packs[core][
                at + (slice(0, N_FC1), slice(h * LANES, (h + 1) * LANES))
            ]
        for k in range(4):
            w_two[2 * i + k // 2, piece(r, N_OUT), (k % 2) * HALF : (k % 2 + 1) * HALF] = packs[core][
                at + (slice(N_FC1 + k * N_OUT, N_FC1 + (k + 1) * N_OUT),)
            ]


def pack_mlp(at_ref, g_one, g_two, packs):
    for core, at, i, r in places(at_ref, packs, False):
        for h in range(2):
            packs[core][at + (slice(0, N_FC1), slice(h * LANES, (h + 1) * LANES))] = g_one[
                piece(2 * i + h, LANES), piece(r, N_FC1)
            ].astype(BF16)
        for k in range(4):
            packs[core][at + (slice(N_FC1 + k * N_OUT, N_FC1 + (k + 1) * N_OUT),)] = g_two[
                2 * i + k // 2, piece(r, N_OUT), (k % 2) * HALF : (k % 2 + 1) * HALF
            ].astype(BF16)


def spread_bias(layer, at_ref, base_ref, bias):
    row = lax.broadcasted_iota(jnp.int32, (WROWS, 2 * AROWS), 0)
    lane = jnp.bitwise_and(lax.broadcasted_iota(jnp.int32, (WROWS, 2 * AROWS), 1), AROWS - 1)
    key_row, key_col = row // SLOT, jnp.bitwise_and(row, SLOT - 1)
    query_row, query_col = lane // SLOT, jnp.bitwise_and(lane, SLOT - 1)
    kept = WIN - SHIFT
    other_row = ((key_row >= kept) != (query_row >= kept)).astype(jnp.int32)
    other_col = ((key_col >= kept) != (query_col >= kept)).astype(jnp.int32)
    padding = (key_col == WIN).astype(jnp.int32)
    for v in range(bias.shape[0]):
        hidden = padding
        if layer == 1:
            if v >> 1:
                hidden = hidden + other_row * at_ref[4]
            if v & 1:
                hidden = hidden + other_col * at_ref[5]
        for g in range(2):
            for a in range(4):
                both = jnp.concatenate([base_ref[8 * g + a], base_ref[8 * g + 4 + a]], axis=1)
                bias[v, g, a] = jnp.where(hidden > 0, MASKED, both)


def attention_forward_kernel(layer, n_packs, at_ref, x_ref, *refs):
    strips, refs = refs[: 3 * layer], refs[3 * layer :]
    packs, refs = refs[:n_packs], refs[n_packs:]
    small_ref, base_ref, refs = refs[0], refs[1], refs[2:]
    if layer:
        xs_ref, refs = refs[0], refs[1:]
    qkv_ref, p_ref, att_ref, mid_ref, w_qkv, w_proj, tiles, att_tiles, bias_ref, *moved = refs
    step = pl.program_id(0)

    @pl.when(step == 0)
    def _():
        unpack_attention(at_ref, packs, w_qkv, w_proj)
        spread_bias(layer, at_ref, base_ref, bias_ref)
        clear_tail(tiles)

    gain = small_ref[layer : layer + 1, 0:D]
    shift = small_ref[layer : layer + 1, D : 2 * D]
    if layer:
        rows = next_rows(x_ref, strips, moved[0])
        xs_ref[...] = rows
    else:
        rows = x_ref[...].reshape(STEP_ROWS, D)
    xhat, _ = normalize(rows)
    normed = (xhat * gain + shift).astype(BF16)
    for part in range(3):
        cols = slice(part * D, (part + 1) * D)
        bias = small_ref[layer : layer + 1, 6 * D + part * D : 7 * D + part * D]
        put_tiles(tiles, 4 * part, mm_t(normed, w_qkv[cols, :]) + bias)
    masks = head_masks()
    lane = jnp.bitwise_and(lax.broadcasted_iota(jnp.int32, (4, 1, LANES), 2), AROWS - 1)
    no_query = (jnp.bitwise_and(lane, SLOT - 1) == WIN) | (lane >= WROWS)

    def windows(pair, carry):
        places_of = [(b, g, 2 * pair + k) for k in range(2) for b in range(2) for g in range(2)]
        scores, values = [], []
        for b, g, n in places_of:
            q, key, val = (
                to_sixty_four(get_window(tiles, 4 * part + 2 * g, b, n)) for part in range(3)
            )
            for part, value in enumerate((q, key, val)):
                at = part * D + g * HALF
                qkv_ref[b * IMAGES + n, :, at : at + HALF] = value
            scores.append(mm_t(stack_heads(key, masks), stack_halves(q)))
            values.append(val)
        probs = []
        for (b, g, n), score in zip(places_of, scores):
            v = 2 * step + b if layer else 0
            score = score.reshape(4, AROWS, LANES)[:, :WROWS] * (SCALE * LOG2E) + bias_ref[v, g]
            powers = jnp.exp2(score - jnp.max(score, axis=1, keepdims=True))
            total = jnp.sum(powers, axis=1, keepdims=True)
            prob = pad_keys(powers * jnp.where(no_query, 0.0, 1.0 / total))
            p_ref[b * IMAGES + n, g] = prob
            probs.append(prob)
        for (b, g, n), prob, val in zip(places_of, probs, values):
            put_window(att_tiles, 2 * g, b, n, pick_halves(t_mm(prob, stack_heads(val, masks))))
        return carry

    lax.fori_loop(0, IMAGES // 2, windows, 0)
    att = get_tiles(att_tiles, 0, 4).astype(BF16)
    att_ref[...] = att
    bias = small_ref[layer : layer + 1, 4 * D : 5 * D]
    mid_ref[...] = rows + (mm_t(att, w_proj[...]) + bias)


def attention_backward_kernel(layer, n_packs, n_out, at_ref, gm_ref, x_ref, qkv_ref, p_ref, att_ref, *refs):
    packs, refs = refs[:n_packs], refs[n_packs:]
    small_ref, rest_ref, dx_ref, refs = refs[0], refs[1], refs[2], refs[3:]
    strips, refs = refs[: 3 * layer], refs[3 * layer :]
    dpacks, refs = refs[:n_out], refs[n_out:]
    dtab_ref, dsmall_ref, w_qkv, w_proj, g_tiles, d_tiles, acc_qkv, acc_proj, acc_tab = refs
    step = pl.program_id(0)

    @pl.when(step == 0)
    def _():
        unpack_attention(at_ref, packs, w_qkv, w_proj)
        dsmall_ref[...] = rest_ref[...]
        clear_tail(g_tiles)
        for ref in (acc_tab, acc_qkv, acc_proj):
            ref[...] = jnp.zeros(ref.shape, ref.dtype)

    gain = small_ref[layer : layer + 1, 0:D]
    shift = small_ref[layer : layer + 1, D : 2 * D]
    grad_mid = gm_ref[...]
    mid_low = grad_mid.astype(BF16)
    dsmall_ref[:, 4 * D : 5 * D] += col_sum(mid_low.astype(F32))
    acc_proj[...] += t_mm(mid_low, att_ref[...])
    put_tiles(g_tiles, 0, mm(mid_low, w_proj[...]))
    masks = head_masks()

    def windows(pair, carry):
        places_of = [(b, g, 2 * pair + k) for k in range(2) for b in range(2) for g in range(2)]
        loaded, dprobs = [], []
        for b, g, n in places_of:
            w = b * IMAGES + n
            q, key, val = (
                qkv_ref[w, :, part * D + g * HALF : part * D + (g + 1) * HALF] for part in range(3)
            )
            grad = stack_halves(to_sixty_four(get_window(g_tiles, 2 * g, b, n)))
            dprobs.append(mm_t(stack_heads(val, masks), grad))
            loaded.append((q, key, grad, p_ref[w, g]))
        lows = []
        sums = [None, None]
        for (b, g, _), dprob, (_, _, _, prob) in zip(places_of, dprobs, loaded):
            dprob = dprob.reshape(4, AROWS, LANES)[:, :WROWS]
            p = prob.astype(F32).reshape(4, AROWS, LANES)[:, :WROWS]
            delta = jnp.sum(p * dprob, axis=1, keepdims=True)
            dscore = p * (dprob - delta)
            sums[g] = dscore if sums[g] is None else sums[g] + dscore
            lows.append(pad_keys(dscore))
        for g in range(2):
            acc_tab[g] += sums[g]
        for (b, g, n), low, (q, key, grad, prob) in zip(places_of, lows, loaded):
            put_window(d_tiles, 2 * g, b, n, pick_halves(t_mm(low, stack_heads(key, masks))) * SCALE)
            put_window(d_tiles, 4 + 2 * g, b, n, pick_heads(mm(low, stack_halves(q))) * SCALE)
            put_window(d_tiles, 8 + 2 * g, b, n, pick_heads(mm(prob, grad)))
        return carry

    lax.fori_loop(0, IMAGES // 2, windows, 0)
    xhat, rstd = normalize(x_ref[...].reshape(STEP_ROWS, D))
    normed = (xhat * gain + shift).astype(BF16)
    grad_normed = None
    for part in range(3):
        cols = slice(part * D, (part + 1) * D)
        low = get_tiles(d_tiles, 4 * part, 4).astype(BF16)
        dsmall_ref[:, 6 * D + part * D : 7 * D + part * D] += col_sum(low.astype(F32))
        acc_qkv[cols, :] += t_mm(low, normed)
        term = mm(low, w_qkv[cols, :])
        grad_normed = term if grad_normed is None else grad_normed + term
    dsmall_ref[:, :D] += col_sum(grad_normed * xhat)
    dsmall_ref[:, D : 2 * D] += col_sum(grad_normed)
    grad_x = grad_mid + norm_back(grad_normed, xhat, rstd, gain)
    dx_ref[...] = grad_x.reshape(WIN, SIDE, IMAGES, D)
    if layer:
        last_strips(dx_ref, strips)

    @pl.when(step == STEPS - 1)
    def _():
        pack_attention(at_ref, acc_qkv, acc_proj, dpacks)
        for g in range(2):
            for a in range(4):
                dtab_ref[8 * g + a] = acc_tab[g, a, :, :AROWS]
                dtab_ref[8 * g + 4 + a] = acc_tab[g, a, :, AROWS:]


def mlp_forward_kernel(layer, n_packs, at_ref, mid_ref, *refs):
    packs, refs = refs[:n_packs], refs[n_packs:]
    small_ref, y_ref, *strips, act_ref, slope_ref, w_one, w_two = refs

    @pl.when(pl.program_id(0) == 0)
    def _():
        unpack_mlp(at_ref, packs, w_one, w_two)

    mid = mid_ref[...]
    xhat, _ = normalize(mid)
    gain = small_ref[layer : layer + 1, 2 * D : 3 * D]
    shift = small_ref[layer : layer + 1, 3 * D : 4 * D]
    normed = (xhat * gain + shift).astype(BF16)
    total = mid + small_ref[layer : layer + 1, 5 * D : 6 * D]

    def hidden(c):
        bias = small_ref[layer : layer + 1, 9 * D + c * CHUNK : 9 * D + (c + 1) * CHUNK]
        return mm(normed, w_one[:, c * CHUNK : (c + 1) * CHUNK]) + bias

    pre = hidden(0)
    for c in range(CHUNKS):
        following = hidden(c + 1) if c + 1 < CHUNKS else None
        act, slope = gelu_both(pre)
        act_ref[c] = act
        slope_ref[c] = slope
        total = total + mm_t(act, w_two[c])
        pre = following
    y_ref[...] = total.reshape(WIN, SIDE, IMAGES, D)
    first_strips(y_ref, strips)


def mlp_backward_kernel(layer, forward, n_packs, n_out, at_ref, mid_ref, dy_ref, *refs):
    strips, refs = refs[:3], refs[3:]
    if not forward:
        (act_ref, slope_ref), refs = refs[:2], refs[2:]
    packs, small_ref, refs = refs[:n_packs], refs[n_packs], refs[n_packs + 1 :]
    if forward:
        (y_ref, *out_strips), refs = refs[:4], refs[4:]
    gm_ref, dpacks, refs = refs[0], refs[1 : 1 + n_out], refs[1 + n_out :]
    dsmall_ref, w_one, w_two, acc_one, acc_two, moved = refs
    step = pl.program_id(0)

    @pl.when(step == 0)
    def _():
        unpack_mlp(at_ref, packs, w_one, w_two)
        for ref in (dsmall_ref, acc_one, acc_two):
            ref[...] = jnp.zeros(ref.shape, ref.dtype)

    mid = mid_ref[...]
    xhat, rstd = normalize(mid)
    gain = small_ref[layer : layer + 1, 2 * D : 3 * D]
    shift = small_ref[layer : layer + 1, 3 * D : 4 * D]
    normed = (xhat * gain + shift).astype(BF16)
    dy = (next_rows if forward else prev_rows)(dy_ref, strips, moved)
    dy_low = dy.astype(BF16)
    dsmall_ref[:, 5 * D : 6 * D] += col_sum(dy_low.astype(F32))
    total = None
    if forward:
        total = mid + small_ref[layer : layer + 1, 5 * D : 6 * D]

    def products(c):
        grad_act = mm(dy_low, w_two[c])
        if not forward:
            return None, grad_act
        bias = small_ref[layer : layer + 1, 9 * D + c * CHUNK : 9 * D + (c + 1) * CHUNK]
        return mm(normed, w_one[:, c * CHUNK : (c + 1) * CHUNK]) + bias, grad_act

    grad_normed = None
    normed_turned, dy_turned = normed.T, dy_low.T
    pre, grad_act = products(0)
    for c in range(CHUNKS):
        cols = slice(c * CHUNK, (c + 1) * CHUNK)
        following = products(c + 1) if c + 1 < CHUNKS else (None, None)
        if forward:
            act, slope = gelu_both(pre)
            total = total + mm_t(act, w_two[c])
        else:
            act = act_ref[c]
            slope = slope_ref[c]
        grad_pre = (grad_act * slope.astype(F32)).astype(BF16)
        dsmall_ref[:, 9 * D + c * CHUNK : 9 * D + (c + 1) * CHUNK] += col_sum(grad_pre.astype(F32))
        term = mm_t(grad_pre, w_one[:, cols])
        grad_normed = term if grad_normed is None else grad_normed + term
        acc_one[:, cols] += mm(normed_turned, grad_pre)
        acc_two[c] += mm(dy_turned, act)
        pre, grad_act = following
    dsmall_ref[:, 2 * D : 3 * D] += col_sum(grad_normed * xhat)
    dsmall_ref[:, 3 * D : 4 * D] += col_sum(grad_normed)
    gm_ref[...] = dy + norm_back(grad_normed, xhat, rstd, gain)
    if forward:
        moved[...] = total.reshape(WIN, SIDE, IMAGES, D)
        last_strips(moved, out_strips)

        def place(a):
            if a == 0:
                y_ref[SHIFT : SHIFT + WIN, SHIFT:] = moved[:, :KEPT]
            else:
                y_ref[SHIFT + WIN :, SHIFT:] = moved[: WIN - SHIFT, :KEPT]

        both_steps(place)

    @pl.when(step == STEPS - 1)
    def _():
        pack_mlp(at_ref, acc_one, acc_two, dpacks)


def fixed(shape):
    return pl.BlockSpec(shape, lambda s: (0,) * len(shape), pipeline_mode=pl.Buffered(1))


def stepped(shape, axis=0):
    return pl.BlockSpec(shape, lambda s: tuple(s if d == axis else 0 for d in range(len(shape))))


def call(kernel, ins, in_specs, outs, scratch, flops, moved_bytes, vmem):
    places_of = [out[0] if len(out) == 4 else jax.ShapeDtypeStruct for out in outs]
    outs = [out[-3:] for out in outs]
    return pl.pallas_call(
        kernel,
        grid=(STEPS,),
        in_specs=in_specs,
        out_shape=[place(shape, kind) for place, (shape, kind, _) in zip(places_of, outs)],
        out_specs=[spec for _, _, spec in outs],
        scratch_shapes=scratch,
        compiler_params=pltpu.CompilerParams(
            dimension_semantics=("arbitrary",), vmem_limit_bytes=vmem * MIB
        ),
        cost_estimate=pl.CostEstimate(
            flops=int(flops), bytes_accessed=int(moved_bytes), transcendentals=0
        ),
    )(*ins)


GRID = (SIDE, SIDE, IMAGES, D)
GRID_STEP = stepped((WIN, SIDE, IMAGES, D))
ROWS_STEP = stepped((STEP_ROWS, D))
WINDOWS_STEP = stepped((STEP_WINDOWS, AROWS, 3 * D))
PROBS_STEP = stepped((STEP_WINDOWS, 2, 4 * AROWS, LANES))
HIDDEN_STEP = stepped((CHUNKS, STEP_ROWS, CHUNK), 1)
STRIPS = ((SHIFT, KEPT, IMAGES, D), (KEPT, SHIFT, IMAGES, D), (SHIFT, SHIFT, IMAGES, D))
STRIP_SPECS = [fixed(shape) for shape in STRIPS]
STRIP_OUTS = [(shape, BF16, fixed(shape)) for shape in STRIPS]
SCALARS = pl.BlockSpec(memory_space=pltpu.SMEM)
SHARD_A = (N_QKV + N_OUT, HALF)
SHARD_B = (N_FC1 + 4 * N_OUT, HALF)
ROW_SUMS = 9 * D + MLP
MOVED = pltpu.VMEM((WIN, SIDE, IMAGES, D), F32)


def tiles_of(features):
    return pltpu.VMEM((features // LANES, STEP_ROWS + IMAGES, LANES), F32)


def pack_specs(packs, shard):
    at = 0 if shard == SHARD_B else packs[0].shape[-2] // shard[0] - 1
    lead = packs[0].shape[:-2]
    return [
        pl.BlockSpec(
            lead + shard, lambda s: (0,) * len(lead) + (at, 0), pipeline_mode=pl.Buffered(1)
        )
    ] * len(packs)


def pack_outs(shard, single):
    if single:
        return [(pltpu.HBM, (32,) + shard, BF16, fixed((32,) + shard))]
    return [((4, 4) + shard, BF16, fixed((4, 4) + shard))] * 2


def attention_forward(layer, at, grid_field, strips, packs, small, base):
    out = call(
        partial(attention_forward_kernel, layer, len(packs)),
        (at, grid_field, *strips, *packs, small, base),
        [SCALARS, fixed(GRID) if layer else GRID_STEP]
        + STRIP_SPECS[: len(strips)]
        + pack_specs(packs, SHARD_A)
        + [fixed(small.shape), fixed(base.shape)],
        [(pltpu.HBM, (ROWS, D), F32, ROWS_STEP)] * layer
        + [
            (pltpu.HBM, (STEPS * STEP_WINDOWS, AROWS, 3 * D), BF16, WINDOWS_STEP),
            (pltpu.HBM, (STEPS * STEP_WINDOWS, 2, 4 * AROWS, LANES), BF16, PROBS_STEP),
            (pltpu.HBM, (ROWS, D), BF16, ROWS_STEP),
            ((ROWS, D), F32, ROWS_STEP) if layer else (pltpu.HBM, (ROWS, D), F32, ROWS_STEP),
        ],
        [
            pltpu.VMEM((3 * D, D), BF16),
            pltpu.VMEM((D, D), BF16),
            tiles_of(3 * D),
            tiles_of(D),
            pltpu.VMEM((4 if layer else 1, 2, 4, WROWS, 2 * AROWS), F32),
        ]
        + [MOVED] * layer,
        2 * ROWS * 4 * D * D * 2,
        30e6,
        38,
    )
    return (list(out[:-1]) if layer else [grid_field] + list(out[:-1])), out[-1]


def attention_backward(layer, at, grad_mid, saved, packs, small, rest, single):
    outs = pack_outs(SHARD_A, single)
    out = call(
        partial(attention_backward_kernel, layer, len(packs), len(outs)),
        (at, grad_mid, *saved, *packs, small, rest),
        [
            SCALARS,
            ROWS_STEP,
            ROWS_STEP if layer else GRID_STEP,
            WINDOWS_STEP,
            PROBS_STEP,
            ROWS_STEP,
        ]
        + pack_specs(packs, SHARD_A)
        + [fixed(small.shape), fixed(rest.shape)],
        [(GRID, F32, GRID_STEP) if layer else (pltpu.HBM, GRID, F32, GRID_STEP)]
        + STRIP_OUTS[: 3 * layer]
        + outs
        + [
            ((HEADS, WROWS, AROWS), F32, fixed((HEADS, WROWS, AROWS))),
            ((1, ROW_SUMS), F32, fixed((1, ROW_SUMS))),
        ],
        [
            pltpu.VMEM((3 * D, D), BF16),
            pltpu.VMEM((D, D), BF16),
            tiles_of(D),
            tiles_of(3 * D),
            pltpu.VMEM((3 * D, D), F32),
            pltpu.VMEM((D, D), F32),
            pltpu.VMEM((2, 4, WROWS, 2 * AROWS), F32),
        ],
        2 * ROWS * 4 * D * D * 5,
        30e6,
        41,
    )
    at_pack = 1 + 3 * layer
    return out[0], out[1:at_pack], out[at_pack:-2], out[-2], out[-1]


MLP_WEIGHTS = [pltpu.VMEM((D, MLP), BF16), pltpu.VMEM((CHUNKS, D, CHUNK), BF16)]


def mlp_forward(layer, at, mid, packs, small):
    out = call(
        partial(mlp_forward_kernel, layer, len(packs)),
        (at, mid, *packs, small),
        [SCALARS, ROWS_STEP] + pack_specs(packs, SHARD_B) + [fixed(small.shape)],
        [(GRID, F32, GRID_STEP)]
        + STRIP_OUTS
        + [(pltpu.HBM, (CHUNKS, ROWS, CHUNK), BF16, HIDDEN_STEP)] * 2,
        MLP_WEIGHTS,
        2 * ROWS * 2 * D * MLP,
        26e6,
        34,
    )
    return out[0], out[1:4], out[4:]


def mlp_backward(layer, at, mid, dy, strips, saved, packs, small, single):
    outs = pack_outs(SHARD_B, single)
    forward = not saved
    extra = 4 if forward else 0
    out = call(
        partial(mlp_backward_kernel, layer, forward, len(packs), len(outs)),
        (at, mid, dy, *strips, *saved, *packs, small),
        [SCALARS, ROWS_STEP, fixed(GRID)]
        + STRIP_SPECS
        + [HIDDEN_STEP] * len(saved)
        + pack_specs(packs, SHARD_B)
        + [fixed(small.shape)],
        ([(pltpu.HBM, GRID, F32, fixed(GRID))] + STRIP_OUTS)[:extra]
        + [((ROWS, D), F32, ROWS_STEP)]
        + outs
        + [((1, ROW_SUMS), F32, fixed((1, ROW_SUMS)))],
        MLP_WEIGHTS
        + [pltpu.VMEM((D, MLP), F32), pltpu.VMEM((CHUNKS, D, CHUNK), F32), MOVED],
        2 * ROWS * (6 if forward else 4) * D * MLP,
        30e6,
        58 if forward else 43,
    )
    return out[:extra], out[extra], out[extra + 1 : -1], out[-1]


def moved(x, step_of):
    sizes = [lax.axis_size(axis) for axis in AXES]

    def flat(i, r, c):
        return (i * sizes[1] + r) * sizes[2] + c

    pairs = [
        (flat(i, r, c), flat(*step_of(i, r, c)))
        for i in range(sizes[0])
        for r in range(sizes[1])
        for c in range(sizes[2])
    ]
    return lax.ppermute(x, AXES, pairs)


def swapped(x, img=0, down=0, core=0, across=0):
    return moved(x, lambda i, r, c: (i ^ img, r ^ (2 * down + core), c ^ across))


def send_strips(strips, by):
    rows, cols = lax.axis_size("row"), lax.axis_size("col")
    low, right, corner = strips
    return (
        moved(low, lambda i, r, c: (i, (r + by) % rows, c)),
        moved(right, lambda i, r, c: (i, r, (c + by) % cols)),
        moved(corner, lambda i, r, c: (i, (r + by) % rows, (c + by) % cols)),
    )


def fill_prev(grid_field, strips):
    high, left, corner = (strip.astype(F32) for strip in strips)
    grid_field = lax.dynamic_update_slice(grid_field, high, (0, SHIFT, 0, 0))
    grid_field = lax.dynamic_update_slice(grid_field, left, (SHIFT, 0, 0, 0))
    return lax.dynamic_update_slice(grid_field, corner, (0, 0, 0, 0))


QUADS = ((0, 0), (0, 1), (1, 0), (1, 1))


def after(values, *others):
    return lax.optimization_barrier((values, others))[0]


def together(*values):
    return lax.optimization_barrier(values)


def is_small():
    return lax.axis_size("img") == 2


def gather_line(pack):
    if not is_small():
        return pack
    return jnp.stack([pack] + [swapped(pack, across=m) for m in (1, 2, 3)])


def gather_quad(line):
    return jnp.stack([line] + [swapped(line, img=i, down=y) for i, y in QUADS[1:]])


def gather_whole(pack, canonical):
    whole = lax.all_gather(pack, AXES, axis=0, tiled=False)
    if not is_small():
        whole = canonical(whole.reshape((lax.axis_size("img"), 16) + pack.shape))
        whole = whole.reshape((32,) + whole.shape[2:])
    return (whole,)


def scatter_whole(whole, in_shards):
    if not is_small():
        whole = in_shards(whole.reshape((2, 16) + whole.shape[1:]), lax.axis_size("img"))
    flat = whole.reshape(-1, whole.shape[-1])
    return lax.psum_scatter(flat, AXES, scatter_dimension=0, tiled=True)


def scatter_plane(whole):
    if not is_small():
        return whole
    flat = whole.reshape(-1, whole.shape[-1])
    part = lax.psum_scatter(flat, ("img", "row"), scatter_dimension=0, tiled=True)
    return part.reshape((4,) + whole.shape[1:])


def scatter_col(part, in_shards):
    if not is_small():
        return scatter_whole(part, in_shards)
    flat = part.reshape(-1, part.shape[-1])
    return lax.psum_scatter(flat, "col", scatter_dimension=0, tiled=True)


def pair_swap(packs):
    return swapped(packs[1], core=1) if is_small() else packs


def scatter_pair(packs, got):
    if not is_small():
        return packs
    half = packs[0].astype(F32) + got.astype(F32)
    return [half[0]] + [half[m].astype(BF16) for m in (1, 2, 3)]


def quad_swaps(halves):
    if not is_small():
        return []
    return [swapped(h, img=i, down=y) for h, (i, y) in zip(halves[1:], QUADS[1:])]


def scatter_quad(halves, got):
    if not is_small():
        return halves
    got = [g.astype(F32) for g in got]
    line = (halves[0] + got[0]) + (got[1] + got[2])
    return [line[0]] + [line[m].astype(BF16) for m in (1, 2, 3)]


def near_swap(x):
    return swapped(x, across=1)


def far_swap(x):
    return swapped(x, across=2)


def line_swaps(line):
    return [swapped(line[m], across=m) for m in (1, 2, 3)] if is_small() else []


def padded_index(rel_index):
    cells = rel_index.T.reshape(WIN, WIN, WIN, WIN)
    gap = (0, SLOT - WIN)
    cells = jnp.pad(cells, [(0, 0), gap, (0, AROWS // SLOT - WIN), gap], constant_values=-1)
    return cells.reshape(1, WROWS * AROWS)


def packing_kernel(w_qkv, w_proj, w_fc1, w_fc2, first_a, second_a, first_b, second_b):
    for l, (pack_a, pack_b) in enumerate(((first_a, first_b), (second_a, second_b))):
        pack_a[:N_QKV] = w_qkv[l].astype(BF16)
        pack_a[N_QKV:] = w_proj[l].astype(BF16)
        for h in range(2):
            pack_b[:N_FC1, h * LANES : (h + 1) * LANES] = w_fc1[
                l, h * LANES : (h + 1) * LANES, :
            ].astype(BF16)
        for k in range(4):
            pack_b[N_FC1 + k * N_OUT : N_FC1 + (k + 1) * N_OUT] = w_fc2[
                l, :, k * HALF : (k + 1) * HALF
            ].astype(BF16)


def turned(matrices):
    w_qkv, w_proj, w_fc1, w_fc2 = matrices
    return w_qkv.swapaxes(1, 2), w_proj.swapaxes(1, 2), w_fc1, w_fc2.swapaxes(1, 2)


def make_packs(masters):
    w_qkv, w_proj, w_fc1, w_fc2 = turned(masters)
    if is_small():
        kinds = [jax.ShapeDtypeStruct(shape, BF16) for shape in (SHARD_A, SHARD_A, SHARD_B, SHARD_B)]
        return pl.pallas_call(
            packing_kernel,
            out_shape=kinds,
            compiler_params=pltpu.CompilerParams(vmem_limit_bytes=16 * MIB),
        )(w_qkv, w_proj, w_fc1, w_fc2)
    cols = w_qkv.shape[2]
    packs = [jnp.concatenate([w_qkv[l], w_proj[l]], axis=0).astype(BF16) for l in range(2)]
    for l in range(2):
        second = w_fc2[l].reshape(N_OUT, 4, cols).transpose(1, 0, 2).reshape(-1, cols)
        packs.append(jnp.concatenate([w_fc1[l].T, second], axis=0).astype(BF16))
    return packs


def update_kernel(kinds, total_of, n_sums, rates, *refs):
    sums, refs = refs[:n_sums], refs[n_sums:]
    count = len(rates)
    ins, outs = refs[: 3 * count], refs[3 * count :]
    for l in range(2):
        total = total_of(l, sums)
        for k, grad in enumerate(kinds(total)):
            rate, decay = rates[k]
            new = adam_step(*(ins[3 * k + m][l] for m in range(3)), grad, rate, decay)
            for m in range(3):
                outs[3 * k + m][l] = new[m]


def attention_total(layer, sums):
    if layer:
        return sums[4][: SHARD_A[0]].astype(F32)
    near, far, both = (s[...].astype(F32) for s in sums[1:4])
    return (sums[0][...] + near) + (far + both)


def mlp_total(layer, sums):
    return (sums[1][...] if layer else sums[0][SHARD_A[0] :]).astype(F32)


def attention_kinds(total):
    return total[:N_QKV], total[N_QKV:]


def mlp_kinds(total):
    first = jnp.concatenate([total[:N_FC1, :LANES], total[:N_FC1, LANES:]], axis=0)
    second = [total[N_FC1 + k * N_OUT : N_FC1 + (k + 1) * N_OUT] for k in range(4)]
    return first, jnp.concatenate(second, axis=1)


def update(kinds, total_of, sums, arrays):
    rates = ((RATE_MATRIX, DECAY_MATRIX),) * (len(arrays) // 3)
    return pl.pallas_call(
        partial(update_kernel, kinds, total_of, len(sums), rates),
        out_shape=[jax.ShapeDtypeStruct(x.shape, F32) for x in arrays],
        compiler_params=pltpu.CompilerParams(vmem_limit_bytes=16 * MIB),
    )(*sums, *arrays)


def attention_canonical(whole):
    _, ranks, rows, _ = whole.shape
    whole = whole.transpose(1, 2, 0, 3).reshape(ranks, rows, 2, HALF)
    return whole.transpose(2, 0, 1, 3)


def attention_shards(pack, size):
    _, ranks, rows, _ = pack.shape
    pack = pack.transpose(1, 2, 0, 3).reshape(ranks, rows, size, D // size)
    return pack.transpose(2, 0, 1, 3)


def mlp_canonical(whole):
    size, ranks, _, cols = whole.shape
    first = attention_canonical(whole[:, :, :N_FC1]).swapaxes(2, 3)
    first = first.reshape(2, ranks, 2, LANES, N_FC1).transpose(0, 1, 3, 2, 4).reshape(2, ranks, LANES, HALF)
    second = whole[:, :, N_FC1:].reshape(size, ranks, 4, N_OUT, cols)
    second = second.transpose(1, 3, 0, 2, 4).reshape(ranks, N_OUT, 2, 4, HALF)
    second = second.transpose(2, 0, 3, 1, 4).reshape(2, ranks, 4 * N_OUT, HALF)
    return jnp.concatenate([first, second], axis=2)


def mlp_shards(pack, size):
    _, ranks, _, _ = pack.shape
    cols = D // size
    first = pack[:, :, :N_FC1].reshape(2, ranks, LANES, 2, N_FC1).transpose(0, 1, 3, 2, 4)
    first = attention_shards(first.reshape(2, ranks, HALF, N_FC1).swapaxes(2, 3), size)
    second = pack[:, :, N_FC1:].reshape(2, ranks, 4, N_OUT, HALF)
    second = second.transpose(1, 3, 0, 2, 4).reshape(ranks, N_OUT, size, 4, cols)
    second = second.transpose(2, 0, 3, 1, 4).reshape(size, ranks, 4 * N_OUT, cols)
    return jnp.concatenate([first, second], axis=2)


def adam_step(weight, moment_one, second, gradient, rate_value, decay_rate):
    moment_one = BETA_ONE * moment_one + (1.0 - BETA_ONE) * gradient
    second = BETA_TWO * second + (1.0 - BETA_TWO) * gradient * gradient
    update = (
        moment_one / (1.0 - BETA_ONE**STEP) / (jnp.sqrt(second / (1.0 - BETA_TWO**STEP)) + EPS_ADAM)
    )
    return (weight - rate_value * (update + decay_rate * weight), moment_one, second)


def shards(
    images,
    grad_out,
    w_qkv,
    w_proj,
    w_fc1,
    w_fc2,
    first_qkv,
    first_proj,
    first_fc1,
    first_fc2,
    second_qkv,
    second_proj,
    second_fc1,
    second_fc2,
    small_params,
    small_first,
    small_second,
    rel_index,
):
    assert images.shape == (IMAGES, SIDE, SIDE, D)
    size = lax.axis_size("img")
    small = is_small()
    row, col = lax.axis_index("row"), lax.axis_index("col")
    last = [row == lax.axis_size("row") - 1, col == lax.axis_size("col") - 1]
    place = [lax.axis_index("img"), row // 2, row % 2, col]
    at = jnp.stack([jnp.asarray(value, jnp.int32) for value in place + last])
    images = images.transpose(1, 2, 0, 3)
    grad_out = grad_out.transpose(1, 2, 0, 3)

    onehot = (
        jnp.arange(RELPOS, dtype=jnp.int32)[:, None] == padded_index(rel_index)
    ).astype(F32)
    tables = small_params[:, 9 * D + MLP :].reshape(2, RELPOS, HEADS)
    base = jnp.einsum("lrh,rp->lhp", tables * LOG2E, onehot, precision=lax.Precision.HIGHEST)
    base = base.reshape(2, HEADS, WROWS, AROWS)
    masters = (w_qkv, w_proj, w_fc1, w_fc2)
    pack_a_zero, pack_a_one, pack_b_zero, pack_b_one = make_packs(masters)
    if small:
        line_a = gather_line(pack_a_zero)
        pair_b = jnp.stack([pack_b_zero, near_swap(pack_b_zero)])
        pair_a = jnp.stack([pack_a_one, near_swap(pack_a_one)])
        got, far_b, at, base = together(quad_swaps([line_a] * 4), far_swap(pair_b), at, base)
        quad = jnp.stack([line_a, *got])
        packs_a_zero = quad, swapped(quad, core=1)
        line_b = jnp.concatenate([pair_b, far_b])
    else:
        packs_a_zero = gather_whole(pack_a_zero, attention_canonical)
        packs_b_zero = gather_whole(pack_b_zero, mlp_canonical)
        packs_a_one = gather_whole(pack_a_one, attention_canonical)
        packs_b_one = gather_whole(pack_b_one, mlp_canonical)

    grad_strips = (
        grad_out[:SHIFT, SHIFT:].astype(BF16),
        grad_out[SHIFT:, :SHIFT].astype(BF16),
        grad_out[:SHIFT, :SHIFT].astype(BF16),
    )

    def table_row(sums, dtab):
        table = jnp.einsum(
            "hp,rp->rh", dtab.reshape(HEADS, -1), onehot, precision=lax.Precision.HIGHEST
        )
        return jnp.concatenate([sums, table.reshape(1, -1)], axis=1)

    packs_a_zero = after(packs_a_zero, grad_strips)
    saved_zero, mid_zero = attention_forward(0, at, images, (), packs_a_zero, small_params, base[0])
    if small:
        mid_zero, got, far_a = together(mid_zero, quad_swaps([line_b] * 4), far_swap(pair_a))
        quad = jnp.stack([line_b, *got])
        packs_b_zero = quad, swapped(quad, core=1)
        line_a = jnp.concatenate([pair_a, far_a])
        packs_b_one = gather_whole(after(pack_b_one, mid_zero), mlp_canonical)
    grad_strips = send_strips(after(grad_strips, mid_zero), -1)
    out_zero, strips, hidden_zero = mlp_forward(0, at, mid_zero, packs_b_zero, small_params)
    strips, grad_strips = together(strips, grad_strips)
    if small:
        strips, got = together(strips, quad_swaps([line_a] * 4))
        quad = jnp.stack([line_a, *got])
        strips, other = together(send_strips(strips, -1), swapped(quad, core=1))
        packs_a_one = quad, other
    else:
        strips = send_strips(strips, -1)
    saved_one, mid_one = attention_forward(
        1, at, out_zero, strips, packs_a_one, small_params, base[1]
    )
    (out_one, *out_strips), gm_one, dpacks, rest = mlp_backward(
        1, at, mid_one, grad_out, grad_strips, (), packs_b_one, small_params, True
    )

    plane_b_one = scatter_plane(dpacks[0])
    dx_one, strips, dpacks, dtab_one, sums = attention_backward(
        1, at, gm_one, saved_one, packs_a_one, small_params, rest, True
    )
    plane_a_one = scatter_plane(dpacks[0])
    strips, row_one = together(send_strips(strips, 1), table_row(sums, dtab_one))
    out_strips = send_strips(after(out_strips, strips), 1)
    _, gm_zero, dpacks, rest = mlp_backward(
        0, at, mid_zero, dx_one, strips, hidden_zero, packs_b_zero, small_params, not small
    )

    dpacks, out_strips, plane_b_one = together(dpacks, out_strips, plane_b_one)
    got, out_one = together(pair_swap(dpacks), fill_prev(out_one, out_strips))
    outputs = out_one.transpose(2, 0, 1, 3)
    halves_b_zero = scatter_pair(dpacks, got)
    gm_zero, halves_b_zero = together(gm_zero, halves_b_zero)
    sum_b_one = scatter_col(plane_b_one, mlp_shards)
    grad_input, _, dpacks, dtab_zero, sums = attention_backward(
        0, at, gm_zero, saved_zero, packs_a_zero, small_params, rest, not small
    )
    grad_input = grad_input.transpose(2, 0, 1, 3)

    dpacks, got_b, sum_b_one, plane_a_one = together(
        dpacks, quad_swaps(halves_b_zero), sum_b_one, plane_a_one
    )
    if small:
        line_b = scatter_quad(halves_b_zero, got_b)
        line_b = jnp.stack([line_b[0].astype(BF16), *line_b[1:]])
        sum_mixed = scatter_col(jnp.concatenate([plane_a_one, line_b], axis=1), None)
    else:
        sum_mixed = jnp.concatenate(
            [scatter_whole(plane_a_one, attention_shards), scatter_whole(halves_b_zero[0], mlp_shards)]
        )
    got, row_zero = together(pair_swap(dpacks), table_row(sums, dtab_zero))
    halves_a = scatter_pair(dpacks, got)
    small_grad = jnp.concatenate([row_zero, row_one], axis=0)

    def small_swaps(*steps):
        return [swapped(small_grad, **step) for step in steps] if small else []

    got, parts = together(quad_swaps(halves_a), small_swaps({"core": 1}))
    line_a = scatter_quad(halves_a, got)
    small_grad = sum(parts, small_grad)
    steps = [{"img": i, "down": y} for i, y in QUADS[1:]]
    sums_a, parts, sum_mixed = together(line_swaps(line_a), small_swaps(*steps), sum_mixed)
    if small:
        small_grad = (small_grad + parts[0]) + (parts[1] + parts[2])
        parts = small_swaps(*({"across": m} for m in (1, 2, 3)))
        small_grad = (small_grad + parts[0]) + (parts[1] + parts[2])
    else:
        small_grad = lax.psum(small_grad, AXES)

    states = [turned(group) for group in (
        masters,
        (first_qkv, first_proj, first_fc1, first_fc2),
        (second_qkv, second_proj, second_fc1, second_fc2),
    )]
    if small:
        new_a = update(
            attention_kinds,
            attention_total,
            (line_a[0], *sums_a, sum_mixed),
            [s[k] for k in (0, 1) for s in states],
        )
        new_b = update(
            mlp_kinds, mlp_total, (sum_mixed, sum_b_one), [s[k] for k in (2, 3) for s in states]
        )
    else:
        cols = D // size
        total_a = [scatter_whole(line_a[0], attention_shards), sum_mixed[: SHARD_A[0]]]
        total_b = [sum_mixed[SHARD_A[0] :], sum_b_one]
        kinds = (
            [t[:N_QKV] for t in total_a],
            [t[N_QKV:] for t in total_a],
            [t[:N_FC1].T for t in total_b],
            [t[N_FC1:].reshape(4, N_OUT, cols).transpose(1, 0, 2).reshape(N_OUT, -1) for t in total_b],
        )
        new = []
        for k in range(4):
            grad = jnp.stack(kinds[k]).astype(F32)
            new += adam_step(*(s[k] for s in states), grad, RATE_MATRIX, DECAY_MATRIX)
        new_a, new_b = new[:6], new[6:]
    small_new = adam_step(small_params, small_first, small_second, small_grad, RATE_SMALL, 0.0)
    new = list(new_a) + list(new_b)
    new = [turned(new[m::3]) for m in range(3)]
    return (outputs, grad_input) + new[0] + new[1] + new[2] + tuple(small_new)


def solution(mesh):
    grid_spec = P("img", "row", "col", None)
    matrix = P(None, "img", ("row", "col"))
    in_specs = (grid_spec,) * 2 + (matrix,) * 12 + (P(),) * 4
    out_specs = (grid_spec,) * 2 + (matrix,) * 12 + (P(),) * 3
    return jax.shard_map(shards, mesh=mesh, in_specs=in_specs, out_specs=out_specs, check_vma=False)
```

```python
from functools import partial

import jax
import jax.numpy as jnp
from jax import lax
from jax.experimental import pallas as pl
from jax.experimental.pallas import tpu as pltpu
from jax.sharding import PartitionSpec as P

D = 512
HEADS = 16
HEAD_DIM = 32
MLP = 2048
WIN = 7
SHIFT = 3
STEP = 10
RELPOS = 169

EPS_NORM = 1e-05
BETA_ONE = 0.9
BETA_TWO = 0.999
EPS_ADAM = 1e-08
RATE_MATRIX = 0.05
RATE_SMALL = 0.3
DECAY_MATRIX = 0.05
MASKED = -1e30

AXES = ("img", "row", "col")
F32 = jnp.float32
BF16 = jnp.bfloat16
LOG2E = 1.4426950408889634
SCALE = HEAD_DIM ** (-0.5)

SIDE = 2 * WIN
IMAGES = 8
SLOT = 8
WROWS = WIN * SLOT
AROWS = 64
STEPS = 2
STEP_ROWS = WIN * SIDE * IMAGES
ROWS = STEPS * STEP_ROWS
STEP_WINDOWS = 2 * IMAGES
KEPT = SIDE - SHIFT
CHUNK = 512
CHUNKS = MLP // CHUNK
HALF = D // 2
LANES = 128
VMEM_LIMIT = 60 * 1024 * 1024


def mm(left, right):
    return lax.dot_general(left, right, (((1,), (0,)), ((), ())), preferred_element_type=F32)


def mm_t(left, right):
    return lax.dot_general(left, right, (((1,), (1,)), ((), ())), preferred_element_type=F32)


def t_mm(left, right):
    return lax.dot_general(left, right, (((0,), (0,)), ((), ())), preferred_element_type=F32)


def col_sum(value):
    return jnp.sum(value, axis=0, keepdims=True)


def normalize(rows):
    center = rows - jnp.mean(rows, axis=-1, keepdims=True)
    spread = jnp.mean(center * center, axis=-1, keepdims=True)
    rstd = lax.rsqrt(spread + EPS_NORM)
    return center * rstd, rstd


def norm_back(grad, xhat, rstd, gain):
    scaled = grad * gain
    mean_one = jnp.mean(scaled, axis=-1, keepdims=True)
    mean_two = jnp.mean(scaled * xhat, axis=-1, keepdims=True)
    return rstd * (scaled - mean_one - xhat * mean_two)


def gelu_both(pre):
    pre = pre.astype(BF16)
    t = 1.0 / (1.0 + jnp.abs(pre) * (0.3275911 * 0.7071067811865476))
    bell = jnp.exp2(pre * pre * (-0.5 * LOG2E))
    poly = t * (0.5 * 1.061405429) + 0.5 * -1.453152027
    poly = poly * t + 0.5 * 1.421413741
    poly = poly * t + 0.5 * -0.284496736
    poly = poly * t + 0.5 * 0.254829592
    tail = poly * t * bell
    cdf = jnp.where(pre >= 0.0, 1.0 - tail, tail)
    return pre * cdf, cdf + pre * bell * 0.3989422804014327


def both_steps(body):
    for a in range(STEPS):
        pl.when(pl.program_id(0) == a)(partial(body, a))


def next_rows(grid_ref, strip_refs, rows_ref):
    low_ref, right_ref, corner_ref = strip_refs

    def body(a):
        if a == 0:
            rows_ref[:, :KEPT] = grid_ref[SHIFT : SHIFT + WIN, SHIFT:]
            rows_ref[:, KEPT:] = right_ref[:WIN].astype(F32)
        else:
            rows_ref[: WIN - SHIFT, :KEPT] = grid_ref[SHIFT + WIN :, SHIFT:]
            rows_ref[: WIN - SHIFT, KEPT:] = right_ref[WIN:].astype(F32)
            rows_ref[WIN - SHIFT :, :KEPT] = low_ref[...].astype(F32)
            rows_ref[WIN - SHIFT :, KEPT:] = corner_ref[...].astype(F32)

    both_steps(body)
    return rows_ref[...].reshape(STEP_ROWS, D)


def prev_rows(grid_ref, strip_refs, rows_ref):
    high_ref, left_ref, corner_ref = strip_refs

    def body(a):
        if a == 0:
            rows_ref[:SHIFT, SHIFT:] = high_ref[...].astype(F32)
            rows_ref[:SHIFT, :SHIFT] = corner_ref[...].astype(F32)
            rows_ref[SHIFT:, SHIFT:] = grid_ref[: WIN - SHIFT, :KEPT]
            rows_ref[SHIFT:, :SHIFT] = left_ref[: WIN - SHIFT].astype(F32)
        else:
            rows_ref[:, SHIFT:] = grid_ref[WIN - SHIFT : KEPT, :KEPT]
            rows_ref[:, :SHIFT] = left_ref[WIN - SHIFT :].astype(F32)

    both_steps(body)
    return rows_ref[...].reshape(STEP_ROWS, D)


def first_strips(block_ref, strip_refs):
    rows_ref, cols_ref, corner_ref = strip_refs

    def body(a):
        if a == 0:
            rows_ref[...] = block_ref[:SHIFT, SHIFT:].astype(BF16)
            cols_ref[: WIN - SHIFT] = block_ref[SHIFT:, :SHIFT].astype(BF16)
            corner_ref[...] = block_ref[:SHIFT, :SHIFT].astype(BF16)
        else:
            cols_ref[WIN - SHIFT :] = block_ref[:, :SHIFT].astype(BF16)

    both_steps(body)


def last_strips(block_ref, strip_refs):
    rows_ref, cols_ref, corner_ref = strip_refs

    def body(a):
        if a == 0:
            cols_ref[:WIN] = block_ref[:, KEPT:].astype(BF16)
        else:
            cols_ref[WIN:] = block_ref[: WIN - SHIFT, KEPT:].astype(BF16)
            rows_ref[...] = block_ref[WIN - SHIFT :, :KEPT].astype(BF16)
            corner_ref[...] = block_ref[WIN - SHIFT :, KEPT:].astype(BF16)

    both_steps(body)


def put_tiles(tiles, first, value):
    for t in range(value.shape[1] // LANES):
        tiles[first + t, :STEP_ROWS, :] = value[:, t * LANES : (t + 1) * LANES]


def get_tiles(tiles, first, count):
    return jnp.concatenate([tiles[first + t, :STEP_ROWS, :] for t in range(count)], axis=1)


def clear_tail(tiles):
    tiles[:, STEP_ROWS:, :] = jnp.zeros(tiles[:, STEP_ROWS:, :].shape, F32)


def window_at(b, n, r):
    return b * WIN * IMAGES + r * SIDE * IMAGES + n


def get_window(tiles, first, b, n):
    return jnp.concatenate(
        [
            jnp.concatenate(
                [
                    tiles[first + t, pl.ds(window_at(b, n, r), SLOT, stride=IMAGES), :]
                    for r in range(WIN)
                ],
                axis=0,
            )
            for t in range(2)
        ],
        axis=1,
    )


def put_window(tiles, first, b, n, value):
    for t in range(2):
        for r in range(WIN):
            tiles[first + t, pl.ds(window_at(b, n, r), WIN, stride=IMAGES), :] = value[
                r * SLOT : r * SLOT + WIN, t * LANES : (t + 1) * LANES
            ]


def to_sixty_four(window):
    padding = jnp.zeros((AROWS - WROWS, window.shape[1]), F32)
    return jnp.concatenate([window, padding], axis=0).astype(BF16)


def head_masks():
    lane = lax.broadcasted_iota(jnp.int32, (16, HALF), 1)
    head = jnp.bitwise_and(lax.shift_right_logical(lane, 5), 3)
    return [jnp.where(head == a, 1.0, 0.0).astype(BF16) for a in range(4)]


def stack_heads(part, masks):
    split = part.reshape(AROWS // 16, 16, HALF)
    return jnp.concatenate(
        [(split * mask[None]).reshape(AROWS, HALF) for mask in masks], axis=0
    )


def stack_halves(part):
    zero = jnp.zeros((AROWS, HALF // 2), part.dtype)
    return jnp.concatenate(
        [
            jnp.concatenate([part[:, : HALF // 2], zero], axis=1),
            jnp.concatenate([zero, part[:, HALF // 2 :]], axis=1),
        ],
        axis=0,
    )


def pick_halves(result):
    return jnp.concatenate(
        [result[:WROWS, : HALF // 2], result[AROWS : AROWS + WROWS, HALF // 2 :]], axis=1
    )


def pick_heads(result):
    lane = lax.broadcasted_iota(jnp.int32, (WROWS, HALF), 1)
    head = jnp.bitwise_and(lax.shift_right_logical(lane, 5), 3)
    picked = result[3 * AROWS : 3 * AROWS + WROWS]
    for a in (2, 1, 0):
        picked = jnp.where(head == a, result[a * AROWS : a * AROWS + WROWS], picked)
    return picked


def pad_keys(value):
    padding = jnp.zeros((4, AROWS - WROWS, 128), F32)
    return jnp.concatenate([value, padding], axis=1).astype(BF16).reshape(4 * AROWS, 128)


def places(at_ref, packs):
    if len(packs) == 1:
        for shard in range(packs[0].shape[0]):
            yield 0, (shard,), shard // 16, shard % 16
        return
    for core in range(2):
        for quad in range(4):
            for across in range(4):
                i = jnp.bitwise_xor(at_ref[0], quad >> 1)
                y = jnp.bitwise_xor(at_ref[1], quad & 1)
                c = jnp.bitwise_xor(at_ref[2], core)
                z = jnp.bitwise_xor(at_ref[3], across)
                yield core, (quad, across), i, (2 * y + c) * 4 + z


def piece(start, length):
    if isinstance(start, int):
        return pl.ds(start * length, length)
    return pl.ds(pl.multiple_of(start * length, length), length)


N_QKV = 3 * D // 16
N_OUT = D // 16
N_FC1 = MLP // 16


def unpack_attention(at_ref, packs, w_qkv, w_proj):
    for core, at, i, r in places(at_ref, packs):
        cols = piece(i, HALF)
        w_qkv[piece(r, N_QKV), cols] = packs[core][at + (slice(0, N_QKV),)]
        w_proj[piece(r, N_OUT), cols] = packs[core][at + (slice(N_QKV, None),)]


def pack_attention(at_ref, g_qkv, g_proj, packs):
    for core, at, i, r in places(at_ref, packs):
        cols = piece(i, HALF)
        packs[core][at + (slice(0, N_QKV),)] = g_qkv[piece(r, N_QKV), cols].astype(BF16)
        packs[core][at + (slice(N_QKV, None),)] = g_proj[piece(r, N_OUT), cols].astype(BF16)


def unpack_mlp(at_ref, packs, w_one, w_two):
    for core, at, i, r in places(at_ref, packs):
        for h in range(2):
            w_one[piece(2 * i + h, LANES), piece(r, N_FC1)] = packs[core][
                at + (slice(0, N_FC1), slice(h * LANES, (h + 1) * LANES))
            ]
        for k in range(4):
            w_two[2 * i + k // 2, piece(r, N_OUT), (k % 2) * HALF : (k % 2 + 1) * HALF] = packs[core][
                at + (slice(N_FC1 + k * N_OUT, N_FC1 + (k + 1) * N_OUT),)
            ]


def pack_mlp(at_ref, g_one, g_two, packs):
    for core, at, i, r in places(at_ref, packs):
        for h in range(2):
            packs[core][at + (slice(0, N_FC1), slice(h * LANES, (h + 1) * LANES))] = g_one[
                piece(2 * i + h, LANES), piece(r, N_FC1)
            ].astype(BF16)
        for k in range(4):
            packs[core][at + (slice(N_FC1 + k * N_OUT, N_FC1 + (k + 1) * N_OUT),)] = g_two[
                2 * i + k // 2, piece(r, N_OUT), (k % 2) * HALF : (k % 2 + 1) * HALF
            ].astype(BF16)


def spread_bias(layer, at_ref, base_ref, bias):
    row = lax.broadcasted_iota(jnp.int32, (WROWS, 2 * AROWS), 0)
    lane = jnp.bitwise_and(lax.broadcasted_iota(jnp.int32, (WROWS, 2 * AROWS), 1), AROWS - 1)
    key_row, key_col = row // SLOT, jnp.bitwise_and(row, SLOT - 1)
    query_row, query_col = lane // SLOT, jnp.bitwise_and(lane, SLOT - 1)
    kept = WIN - SHIFT
    other_row = ((key_row >= kept) != (query_row >= kept)).astype(jnp.int32)
    other_col = ((key_col >= kept) != (query_col >= kept)).astype(jnp.int32)
    padding = (key_col == WIN).astype(jnp.int32)
    for v in range(bias.shape[0]):
        hidden = padding
        if layer == 1:
            if v >> 1:
                hidden = hidden + other_row * at_ref[4]
            if v & 1:
                hidden = hidden + other_col * at_ref[5]
        for g in range(2):
            for a in range(4):
                both = jnp.concatenate([base_ref[8 * g + a], base_ref[8 * g + 4 + a]], axis=1)
                bias[v, g, a] = jnp.where(hidden > 0, MASKED, both)


def attention_forward_kernel(layer, n_packs, at_ref, x_ref, *refs):
    strips, refs = refs[: 3 * layer], refs[3 * layer :]
    packs, refs = refs[:n_packs], refs[n_packs:]
    small_ref, base_ref, refs = refs[0], refs[1], refs[2:]
    if layer:
        xs_ref, refs = refs[0], refs[1:]
    qkv_ref, p_ref, att_ref, mid_ref, w_qkv, w_proj, tiles, att_tiles, bias_ref, *moved = refs
    step = pl.program_id(0)

    @pl.when(step == 0)
    def _():
        unpack_attention(at_ref, packs, w_qkv, w_proj)
        spread_bias(layer, at_ref, base_ref, bias_ref)
        clear_tail(tiles)

    gain = small_ref[layer : layer + 1, 0:D]
    shift = small_ref[layer : layer + 1, D : 2 * D]
    if layer:
        rows = next_rows(x_ref, strips, moved[0])
        xs_ref[...] = rows
    else:
        rows = x_ref[...].reshape(STEP_ROWS, D)
    xhat, _ = normalize(rows)
    normed = (xhat * gain + shift).astype(BF16)
    for part in range(3):
        cols = slice(part * D, (part + 1) * D)
        bias = small_ref[layer : layer + 1, 6 * D + part * D : 7 * D + part * D]
        put_tiles(tiles, 4 * part, mm_t(normed, w_qkv[cols, :]) + bias)
    masks = head_masks()
    lane = jnp.bitwise_and(lax.broadcasted_iota(jnp.int32, (4, 1, LANES), 2), AROWS - 1)
    no_query = (jnp.bitwise_and(lane, SLOT - 1) == WIN) | (lane >= WROWS)

    def windows(pair, carry):
        places_of = [(b, g, 2 * pair + k) for k in range(2) for b in range(2) for g in range(2)]
        scores, values = [], []
        for b, g, n in places_of:
            q, key, val = (
                to_sixty_four(get_window(tiles, 4 * part + 2 * g, b, n)) for part in range(3)
            )
            for part, value in enumerate((q, key, val)):
                at = part * D + g * HALF
                qkv_ref[b * IMAGES + n, :, at : at + HALF] = value
            scores.append(mm_t(stack_heads(key, masks), stack_halves(q)))
            values.append(val)
        probs = []
        for (b, g, n), score in zip(places_of, scores):
            v = 2 * step + b if layer else 0
            score = score.reshape(4, AROWS, LANES)[:, :WROWS] * (SCALE * LOG2E) + bias_ref[v, g]
            powers = jnp.exp2(score - jnp.max(score, axis=1, keepdims=True))
            total = jnp.sum(powers, axis=1, keepdims=True)
            prob = pad_keys(powers * jnp.where(no_query, 0.0, 1.0 / total))
            p_ref[b * IMAGES + n, g] = prob
            probs.append(prob)
        for (b, g, n), prob, val in zip(places_of, probs, values):
            put_window(att_tiles, 2 * g, b, n, pick_halves(t_mm(prob, stack_heads(val, masks))))
        return carry

    lax.fori_loop(0, IMAGES // 2, windows, 0)
    att = get_tiles(att_tiles, 0, 4).astype(BF16)
    att_ref[...] = att
    bias = small_ref[layer : layer + 1, 4 * D : 5 * D]
    mid_ref[...] = rows + (mm_t(att, w_proj[...]) + bias)


def attention_backward_kernel(layer, n_packs, n_out, at_ref, gm_ref, x_ref, qkv_ref, p_ref, att_ref, *refs):
    packs, refs = refs[:n_packs], refs[n_packs:]
    small_ref, rest_ref, dx_ref, refs = refs[0], refs[1], refs[2], refs[3:]
    strips, refs = refs[: 3 * layer], refs[3 * layer :]
    dpacks, refs = refs[:n_out], refs[n_out:]
    dtab_ref, dsmall_ref, w_qkv, w_proj, g_tiles, d_tiles, acc_qkv, acc_proj, acc_tab = refs
    step = pl.program_id(0)

    @pl.when(step == 0)
    def _():
        unpack_attention(at_ref, packs, w_qkv, w_proj)
        dsmall_ref[...] = rest_ref[...]
        clear_tail(g_tiles)
        for ref in (acc_tab, acc_qkv, acc_proj):
            ref[...] = jnp.zeros(ref.shape, ref.dtype)

    gain = small_ref[layer : layer + 1, 0:D]
    shift = small_ref[layer : layer + 1, D : 2 * D]
    grad_mid = gm_ref[...]
    mid_low = grad_mid.astype(BF16)
    dsmall_ref[:, 4 * D : 5 * D] += col_sum(mid_low.astype(F32))
    acc_proj[...] += t_mm(mid_low, att_ref[...])
    put_tiles(g_tiles, 0, mm(mid_low, w_proj[...]))
    masks = head_masks()

    def windows(pair, carry):
        places_of = [(b, g, 2 * pair + k) for k in range(2) for b in range(2) for g in range(2)]
        loaded, dprobs = [], []
        for b, g, n in places_of:
            w = b * IMAGES + n
            q, key, val = (
                qkv_ref[w, :, part * D + g * HALF : part * D + (g + 1) * HALF] for part in range(3)
            )
            grad = stack_halves(to_sixty_four(get_window(g_tiles, 2 * g, b, n)))
            dprobs.append(mm_t(stack_heads(val, masks), grad))
            loaded.append((q, key, grad, p_ref[w, g]))
        lows = []
        sums = [None, None]
        for (b, g, _), dprob, (_, _, _, prob) in zip(places_of, dprobs, loaded):
            dprob = dprob.reshape(4, AROWS, LANES)[:, :WROWS]
            p = prob.astype(F32).reshape(4, AROWS, LANES)[:, :WROWS]
            delta = jnp.sum(p * dprob, axis=1, keepdims=True)
            dscore = p * (dprob - delta)
            sums[g] = dscore if sums[g] is None else sums[g] + dscore
            lows.append(pad_keys(dscore))
        for g in range(2):
            acc_tab[g] += sums[g]
        for (b, g, n), low, (q, key, grad, prob) in zip(places_of, lows, loaded):
            put_window(d_tiles, 2 * g, b, n, pick_halves(t_mm(low, stack_heads(key, masks))) * SCALE)
            put_window(d_tiles, 4 + 2 * g, b, n, pick_heads(mm(low, stack_halves(q))) * SCALE)
            put_window(d_tiles, 8 + 2 * g, b, n, pick_heads(mm(prob, grad)))
        return carry

    lax.fori_loop(0, IMAGES // 2, windows, 0)
    xhat, rstd = normalize(x_ref[...].reshape(STEP_ROWS, D))
    normed = (xhat * gain + shift).astype(BF16)
    grad_normed = None
    for part in range(3):
        cols = slice(part * D, (part + 1) * D)
        low = get_tiles(d_tiles, 4 * part, 4).astype(BF16)
        dsmall_ref[:, 6 * D + part * D : 7 * D + part * D] += col_sum(low.astype(F32))
        acc_qkv[cols, :] += t_mm(low, normed)
        term = mm(low, w_qkv[cols, :])
        grad_normed = term if grad_normed is None else grad_normed + term
    dsmall_ref[:, :D] += col_sum(grad_normed * xhat)
    dsmall_ref[:, D : 2 * D] += col_sum(grad_normed)
    grad_x = grad_mid + norm_back(grad_normed, xhat, rstd, gain)
    dx_ref[...] = grad_x.reshape(WIN, SIDE, IMAGES, D)
    if layer:
        last_strips(dx_ref, strips)

    @pl.when(step == STEPS - 1)
    def _():
        pack_attention(at_ref, acc_qkv, acc_proj, dpacks)
        for g in range(2):
            for a in range(4):
                dtab_ref[8 * g + a] = acc_tab[g, a, :, :AROWS]
                dtab_ref[8 * g + 4 + a] = acc_tab[g, a, :, AROWS:]


def mlp_forward_kernel(layer, n_packs, at_ref, mid_ref, *refs):
    packs, refs = refs[:n_packs], refs[n_packs:]
    small_ref, y_ref, *strips, act_ref, slope_ref, w_one, w_two = refs

    @pl.when(pl.program_id(0) == 0)
    def _():
        unpack_mlp(at_ref, packs, w_one, w_two)

    mid = mid_ref[...]
    xhat, _ = normalize(mid)
    gain = small_ref[layer : layer + 1, 2 * D : 3 * D]
    shift = small_ref[layer : layer + 1, 3 * D : 4 * D]
    normed = (xhat * gain + shift).astype(BF16)
    total = mid + small_ref[layer : layer + 1, 5 * D : 6 * D]

    def hidden(c):
        bias = small_ref[layer : layer + 1, 9 * D + c * CHUNK : 9 * D + (c + 1) * CHUNK]
        return mm(normed, w_one[:, c * CHUNK : (c + 1) * CHUNK]) + bias

    pre = hidden(0)
    for c in range(CHUNKS):
        following = hidden(c + 1) if c + 1 < CHUNKS else None
        act, slope = gelu_both(pre)
        act_ref[c] = act
        slope_ref[c] = slope
        total = total + mm_t(act, w_two[c])
        pre = following
    y_ref[...] = total.reshape(WIN, SIDE, IMAGES, D)
    first_strips(y_ref, strips)


def mlp_backward_kernel(layer, forward, n_packs, n_out, at_ref, mid_ref, dy_ref, *refs):
    strips, refs = refs[:3], refs[3:]
    if not forward:
        (act_ref, slope_ref), refs = refs[:2], refs[2:]
    packs, small_ref, refs = refs[:n_packs], refs[n_packs], refs[n_packs + 1 :]
    if forward:
        (y_ref, *out_strips), refs = refs[:4], refs[4:]
    gm_ref, dpacks, refs = refs[0], refs[1 : 1 + n_out], refs[1 + n_out :]
    dsmall_ref, w_one, w_two, acc_one, acc_two, moved = refs
    step = pl.program_id(0)

    @pl.when(step == 0)
    def _():
        unpack_mlp(at_ref, packs, w_one, w_two)
        for ref in (dsmall_ref, acc_one, acc_two):
            ref[...] = jnp.zeros(ref.shape, ref.dtype)

    mid = mid_ref[...]
    xhat, rstd = normalize(mid)
    gain = small_ref[layer : layer + 1, 2 * D : 3 * D]
    shift = small_ref[layer : layer + 1, 3 * D : 4 * D]
    normed = (xhat * gain + shift).astype(BF16)
    dy = (next_rows if forward else prev_rows)(dy_ref, strips, moved)
    dy_low = dy.astype(BF16)
    dsmall_ref[:, 5 * D : 6 * D] += col_sum(dy_low.astype(F32))
    total = None
    if forward:
        total = mid + small_ref[layer : layer + 1, 5 * D : 6 * D]

    def products(c):
        grad_act = mm(dy_low, w_two[c])
        if not forward:
            return None, grad_act
        bias = small_ref[layer : layer + 1, 9 * D + c * CHUNK : 9 * D + (c + 1) * CHUNK]
        return mm(normed, w_one[:, c * CHUNK : (c + 1) * CHUNK]) + bias, grad_act

    grad_normed = None
    normed_turned, dy_turned = normed.T, dy_low.T
    pre, grad_act = products(0)
    for c in range(CHUNKS):
        cols = slice(c * CHUNK, (c + 1) * CHUNK)
        following = products(c + 1) if c + 1 < CHUNKS else (None, None)
        if forward:
            act, slope = gelu_both(pre)
            total = total + mm_t(act, w_two[c])
        else:
            act = act_ref[c]
            slope = slope_ref[c]
        grad_pre = (grad_act * slope.astype(F32)).astype(BF16)
        dsmall_ref[:, 9 * D + c * CHUNK : 9 * D + (c + 1) * CHUNK] += col_sum(grad_pre.astype(F32))
        term = mm_t(grad_pre, w_one[:, cols])
        grad_normed = term if grad_normed is None else grad_normed + term
        acc_one[:, cols] += mm(normed_turned, grad_pre)
        acc_two[c] += mm(dy_turned, act)
        pre, grad_act = following
    dsmall_ref[:, 2 * D : 3 * D] += col_sum(grad_normed * xhat)
    dsmall_ref[:, 3 * D : 4 * D] += col_sum(grad_normed)
    gm_ref[...] = dy + norm_back(grad_normed, xhat, rstd, gain)
    if forward:
        moved[...] = total.reshape(WIN, SIDE, IMAGES, D)
        last_strips(moved, out_strips)

        def place(a):
            if a == 0:
                y_ref[SHIFT : SHIFT + WIN, SHIFT:] = moved[:, :KEPT]
            else:
                y_ref[SHIFT + WIN :, SHIFT:] = moved[: WIN - SHIFT, :KEPT]

        both_steps(place)

    @pl.when(step == STEPS - 1)
    def _():
        pack_mlp(at_ref, acc_one, acc_two, dpacks)


def fixed(shape):
    return pl.BlockSpec(shape, lambda s: (0,) * len(shape), pipeline_mode=pl.Buffered(1))


def stepped(shape, axis=0):
    return pl.BlockSpec(shape, lambda s: tuple(s if d == axis else 0 for d in range(len(shape))))


def call(kernel, ins, in_specs, outs, scratch, flops, moved_bytes, vmem=VMEM_LIMIT):
    places_of = [out[0] if len(out) == 4 else jax.ShapeDtypeStruct for out in outs]
    outs = [out[-3:] for out in outs]
    return pl.pallas_call(
        kernel,
        grid=(STEPS,),
        in_specs=in_specs,
        out_shape=[place(shape, kind) for place, (shape, kind, _) in zip(places_of, outs)],
        out_specs=[spec for _, _, spec in outs],
        scratch_shapes=scratch,
        compiler_params=pltpu.CompilerParams(
            dimension_semantics=("arbitrary",), vmem_limit_bytes=vmem
        ),
        cost_estimate=pl.CostEstimate(
            flops=int(flops), bytes_accessed=int(moved_bytes), transcendentals=0
        ),
    )(*ins)


GRID = (SIDE, SIDE, IMAGES, D)
GRID_STEP = stepped((WIN, SIDE, IMAGES, D))
ROWS_STEP = stepped((STEP_ROWS, D))
WINDOWS_STEP = stepped((STEP_WINDOWS, AROWS, 3 * D))
PROBS_STEP = stepped((STEP_WINDOWS, 2, 4 * AROWS, LANES))
HIDDEN_STEP = stepped((CHUNKS, STEP_ROWS, CHUNK), 1)
STRIPS = ((SHIFT, KEPT, IMAGES, D), (KEPT, SHIFT, IMAGES, D), (SHIFT, SHIFT, IMAGES, D))
STRIP_SPECS = [fixed(shape) for shape in STRIPS]
STRIP_OUTS = [(shape, BF16, fixed(shape)) for shape in STRIPS]
SCALARS = pl.BlockSpec(memory_space=pltpu.SMEM)
SHARD_A = (N_QKV + N_OUT, HALF)
SHARD_B = (N_FC1 + 4 * N_OUT, HALF)
ROW_SUMS = 9 * D + MLP
MOVED = pltpu.VMEM((WIN, SIDE, IMAGES, D), F32)


def tiles_of(features):
    return pltpu.VMEM((features // LANES, STEP_ROWS + IMAGES, LANES), F32)


def pack_specs(packs, shard):
    at = 0 if shard == SHARD_B else packs[0].shape[-2] // shard[0] - 1
    lead = packs[0].shape[:-2]
    return [
        pl.BlockSpec(
            lead + shard, lambda s: (0,) * len(lead) + (at, 0), pipeline_mode=pl.Buffered(1)
        )
    ] * len(packs)


def pack_outs(shard, single):
    if single:
        return [((32,) + shard, BF16, fixed((32,) + shard))]
    return [((4, 4) + shard, BF16, fixed((4, 4) + shard))] * 2


def attention_forward(layer, at, grid_field, strips, packs, small, base):
    out = call(
        partial(attention_forward_kernel, layer, len(packs)),
        (at, grid_field, *strips, *packs, small, base),
        [SCALARS, fixed(GRID) if layer else GRID_STEP]
        + STRIP_SPECS[: len(strips)]
        + pack_specs(packs, SHARD_A)
        + [fixed(small.shape), fixed(base.shape)],
        [(pltpu.HBM, (ROWS, D), F32, ROWS_STEP)] * layer
        + [
            (pltpu.HBM, (STEPS * STEP_WINDOWS, AROWS, 3 * D), BF16, WINDOWS_STEP),
            (pltpu.HBM, (STEPS * STEP_WINDOWS, 2, 4 * AROWS, LANES), BF16, PROBS_STEP),
            (pltpu.HBM, (ROWS, D), BF16, ROWS_STEP),
            (pltpu.HBM, (ROWS, D), F32, ROWS_STEP),
        ],
        [
            pltpu.VMEM((3 * D, D), BF16),
            pltpu.VMEM((D, D), BF16),
            tiles_of(3 * D),
            tiles_of(D),
            pltpu.VMEM((4 if layer else 1, 2, 4, WROWS, 2 * AROWS), F32),
        ]
        + [MOVED] * layer,
        2 * ROWS * 4 * D * D * 2,
        30e6,
        38 * 1024 * 1024,
    )
    return (list(out[:-1]) if layer else [grid_field] + list(out[:-1])), out[-1]


def attention_backward(layer, at, grad_mid, saved, packs, small, rest, single):
    outs = pack_outs(SHARD_A, single)
    out = call(
        partial(attention_backward_kernel, layer, len(packs), len(outs)),
        (at, grad_mid, *saved, *packs, small, rest),
        [
            SCALARS,
            ROWS_STEP,
            ROWS_STEP if layer else GRID_STEP,
            WINDOWS_STEP,
            PROBS_STEP,
            ROWS_STEP,
        ]
        + pack_specs(packs, SHARD_A)
        + [fixed(small.shape), fixed(rest.shape)],
        [(GRID, F32, GRID_STEP)]
        + STRIP_OUTS[: 3 * layer]
        + outs
        + [
            ((HEADS, WROWS, AROWS), F32, fixed((HEADS, WROWS, AROWS))),
            ((1, ROW_SUMS), F32, fixed((1, ROW_SUMS))),
        ],
        [
            pltpu.VMEM((3 * D, D), BF16),
            pltpu.VMEM((D, D), BF16),
            tiles_of(D),
            tiles_of(3 * D),
            pltpu.VMEM((3 * D, D), F32),
            pltpu.VMEM((D, D), F32),
            pltpu.VMEM((2, 4, WROWS, 2 * AROWS), F32),
        ],
        2 * ROWS * 4 * D * D * 5,
        30e6,
    )
    at_pack = 1 + 3 * layer
    return out[0], out[1:at_pack], out[at_pack:-2], out[-2], out[-1]


MLP_WEIGHTS = [pltpu.VMEM((D, MLP), BF16), pltpu.VMEM((CHUNKS, D, CHUNK), BF16)]


def mlp_forward(layer, at, mid, packs, small):
    out = call(
        partial(mlp_forward_kernel, layer, len(packs)),
        (at, mid, *packs, small),
        [SCALARS, ROWS_STEP] + pack_specs(packs, SHARD_B) + [fixed(small.shape)],
        [(GRID, F32, GRID_STEP)]
        + STRIP_OUTS
        + [(pltpu.HBM, (CHUNKS, ROWS, CHUNK), BF16, HIDDEN_STEP)] * 2,
        MLP_WEIGHTS,
        2 * ROWS * 2 * D * MLP,
        26e6,
        34 * 1024 * 1024,
    )
    return out[0], out[1:4], out[4:]


def mlp_backward(layer, at, mid, dy, strips, saved, packs, small, single):
    outs = pack_outs(SHARD_B, single)
    forward = not saved
    extra = 4 if forward else 0
    out = call(
        partial(mlp_backward_kernel, layer, forward, len(packs), len(outs)),
        (at, mid, dy, *strips, *saved, *packs, small),
        [SCALARS, ROWS_STEP, fixed(GRID)]
        + STRIP_SPECS
        + [HIDDEN_STEP] * len(saved)
        + pack_specs(packs, SHARD_B)
        + [fixed(small.shape)],
        ([(GRID, F32, fixed(GRID))] + STRIP_OUTS)[:extra]
        + [((ROWS, D), F32, ROWS_STEP)]
        + outs
        + [((1, ROW_SUMS), F32, fixed((1, ROW_SUMS)))],
        MLP_WEIGHTS
        + [pltpu.VMEM((D, MLP), F32), pltpu.VMEM((CHUNKS, D, CHUNK), F32), MOVED],
        2 * ROWS * (6 if forward else 4) * D * MLP,
        30e6,
    )
    return out[:extra], out[extra], out[extra + 1 : -1], out[-1]


def moved(x, step_of):
    sizes = [lax.axis_size(axis) for axis in AXES]

    def flat(i, r, c):
        return (i * sizes[1] + r) * sizes[2] + c

    pairs = [
        (flat(i, r, c), flat(*step_of(i, r, c)))
        for i in range(sizes[0])
        for r in range(sizes[1])
        for c in range(sizes[2])
    ]
    return lax.ppermute(x, AXES, pairs)


def swapped(x, img=0, down=0, core=0, across=0):
    return moved(x, lambda i, r, c: (i ^ img, r ^ (2 * down + core), c ^ across))


def send_strips(strips, by):
    rows, cols = lax.axis_size("row"), lax.axis_size("col")
    low, right, corner = strips
    return (
        moved(low, lambda i, r, c: (i, (r + by) % rows, c)),
        moved(right, lambda i, r, c: (i, r, (c + by) % cols)),
        moved(corner, lambda i, r, c: (i, (r + by) % rows, (c + by) % cols)),
    )


def fill_prev(grid_field, strips):
    high, left, corner = (strip.astype(F32) for strip in strips)
    grid_field = lax.dynamic_update_slice(grid_field, high, (0, SHIFT, 0, 0))
    grid_field = lax.dynamic_update_slice(grid_field, left, (SHIFT, 0, 0, 0))
    return lax.dynamic_update_slice(grid_field, corner, (0, 0, 0, 0))


QUADS = ((0, 0), (0, 1), (1, 0), (1, 1))


def after(values, *others):
    return lax.optimization_barrier((values, others))[0]


def together(*values):
    return lax.optimization_barrier(values)


def is_small():
    return lax.axis_size("img") == 2


def gather_line(pack):
    if not is_small():
        return pack
    return jnp.stack([pack] + [swapped(pack, across=m) for m in (1, 2, 3)])


def gather_quad(line):
    return jnp.stack([line] + [swapped(line, img=i, down=y) for i, y in QUADS[1:]])


def gather_whole(pack, canonical):
    whole = lax.all_gather(pack, AXES, axis=0, tiled=False)
    if not is_small():
        whole = canonical(whole.reshape((lax.axis_size("img"), 16) + pack.shape))
        whole = whole.reshape((32,) + whole.shape[2:])
    return (whole,)


def scatter_whole(whole, in_shards):
    if not is_small():
        whole = in_shards(whole.reshape((2, 16) + whole.shape[1:]), lax.axis_size("img"))
    flat = whole.reshape(-1, whole.shape[-1])
    return lax.psum_scatter(flat, AXES, scatter_dimension=0, tiled=True)


def scatter_plane(whole):
    if not is_small():
        return whole
    flat = whole.reshape(-1, whole.shape[-1])
    part = lax.psum_scatter(flat, ("img", "row"), scatter_dimension=0, tiled=True)
    return part.reshape((4,) + whole.shape[1:])


def scatter_col(part, in_shards):
    if not is_small():
        return scatter_whole(part, in_shards)
    flat = part.reshape(-1, part.shape[-1])
    return lax.psum_scatter(flat, "col", scatter_dimension=0, tiled=True)


def pair_swap(packs):
    return swapped(packs[1], core=1) if is_small() else packs


def scatter_pair(packs, got):
    if not is_small():
        return packs
    half = packs[0].astype(F32) + got.astype(F32)
    return [half[0]] + [half[m].astype(BF16) for m in (1, 2, 3)]


def quad_swaps(halves):
    if not is_small():
        return []
    return [swapped(h, img=i, down=y) for h, (i, y) in zip(halves[1:], QUADS[1:])]


def scatter_quad(halves, got):
    if not is_small():
        return halves
    got = [g.astype(F32) for g in got]
    line = (halves[0] + got[0]) + (got[1] + got[2])
    return [line[0]] + [line[m].astype(BF16) for m in (1, 2, 3)]


def near_swap(x):
    return swapped(x, across=1)


def far_swap(x):
    return swapped(x, across=2)


def line_swaps(line):
    return [swapped(line[m], across=m) for m in (1, 2, 3)] if is_small() else []


def padded_index(rel_index):
    cells = rel_index.T.reshape(WIN, WIN, WIN, WIN)
    gap = (0, SLOT - WIN)
    cells = jnp.pad(cells, [(0, 0), gap, (0, AROWS // SLOT - WIN), gap], constant_values=-1)
    return cells.reshape(1, WROWS * AROWS)


def packing_kernel(w_qkv, w_proj, w_fc1, w_fc2, first_a, second_a, first_b, second_b):
    for l, (pack_a, pack_b) in enumerate(((first_a, first_b), (second_a, second_b))):
        pack_a[:N_QKV] = w_qkv[l].astype(BF16)
        pack_a[N_QKV:] = w_proj[l].astype(BF16)
        for h in range(2):
            pack_b[:N_FC1, h * LANES : (h + 1) * LANES] = w_fc1[
                l, h * LANES : (h + 1) * LANES, :
            ].astype(BF16)
        for k in range(4):
            pack_b[N_FC1 + k * N_OUT : N_FC1 + (k + 1) * N_OUT] = w_fc2[
                l, :, k * HALF : (k + 1) * HALF
            ].astype(BF16)


def turned(matrices):
    w_qkv, w_proj, w_fc1, w_fc2 = matrices
    return w_qkv.swapaxes(1, 2), w_proj.swapaxes(1, 2), w_fc1, w_fc2.swapaxes(1, 2)


def make_packs(masters):
    w_qkv, w_proj, w_fc1, w_fc2 = turned(masters)
    if is_small():
        kinds = [jax.ShapeDtypeStruct(shape, BF16) for shape in (SHARD_A, SHARD_A, SHARD_B, SHARD_B)]
        return pl.pallas_call(
            packing_kernel,
            out_shape=kinds,
            compiler_params=pltpu.CompilerParams(vmem_limit_bytes=VMEM_LIMIT),
        )(w_qkv, w_proj, w_fc1, w_fc2)
    cols = w_qkv.shape[2]
    packs = [jnp.concatenate([w_qkv[l], w_proj[l]], axis=0).astype(BF16) for l in range(2)]
    for l in range(2):
        second = w_fc2[l].reshape(N_OUT, 4, cols).transpose(1, 0, 2).reshape(-1, cols)
        packs.append(jnp.concatenate([w_fc1[l].T, second], axis=0).astype(BF16))
    return packs


def update_kernel(kinds, rates, *refs):
    sums, refs = refs[:5], refs[5:]
    count = len(rates)
    ins, outs = refs[: 3 * count], refs[3 * count :]
    for l in range(2):
        if l == 0:
            near, far, both = (s[...].astype(F32) for s in sums[1:4])
            total = (sums[0][...] + near) + (far + both)
        else:
            total = sums[4][...].astype(F32)
        for k, grad in enumerate(kinds(total)):
            rate, decay = rates[k]
            new = adam_step(*(ins[3 * k + m][l] for m in range(3)), grad, rate, decay)
            for m in range(3):
                outs[3 * k + m][l] = new[m]


def attention_kinds(total):
    return total[:N_QKV], total[N_QKV:]


def mlp_kinds(total):
    first = jnp.concatenate([total[:N_FC1, :LANES], total[:N_FC1, LANES:]], axis=0)
    second = [total[N_FC1 + k * N_OUT : N_FC1 + (k + 1) * N_OUT] for k in range(4)]
    return first, jnp.concatenate(second, axis=1)


def update(kinds, sums, arrays):
    rates = ((RATE_MATRIX, DECAY_MATRIX),) * (len(arrays) // 3)
    return pl.pallas_call(
        partial(update_kernel, kinds, rates),
        out_shape=[jax.ShapeDtypeStruct(x.shape, F32) for x in arrays],
        compiler_params=pltpu.CompilerParams(vmem_limit_bytes=VMEM_LIMIT),
    )(*sums, *arrays)


def attention_canonical(whole):
    _, ranks, rows, _ = whole.shape
    whole = whole.transpose(1, 2, 0, 3).reshape(ranks, rows, 2, HALF)
    return whole.transpose(2, 0, 1, 3)


def attention_shards(pack, size):
    _, ranks, rows, _ = pack.shape
    pack = pack.transpose(1, 2, 0, 3).reshape(ranks, rows, size, D // size)
    return pack.transpose(2, 0, 1, 3)


def mlp_canonical(whole):
    size, ranks, _, cols = whole.shape
    first = attention_canonical(whole[:, :, :N_FC1]).swapaxes(2, 3)
    first = first.reshape(2, ranks, 2, LANES, N_FC1).transpose(0, 1, 3, 2, 4).reshape(2, ranks, LANES, HALF)
    second = whole[:, :, N_FC1:].reshape(size, ranks, 4, N_OUT, cols)
    second = second.transpose(1, 3, 0, 2, 4).reshape(ranks, N_OUT, 2, 4, HALF)
    second = second.transpose(2, 0, 3, 1, 4).reshape(2, ranks, 4 * N_OUT, HALF)
    return jnp.concatenate([first, second], axis=2)


def mlp_shards(pack, size):
    _, ranks, _, _ = pack.shape
    cols = D // size
    first = pack[:, :, :N_FC1].reshape(2, ranks, LANES, 2, N_FC1).transpose(0, 1, 3, 2, 4)
    first = attention_shards(first.reshape(2, ranks, HALF, N_FC1).swapaxes(2, 3), size)
    second = pack[:, :, N_FC1:].reshape(2, ranks, 4, N_OUT, HALF)
    second = second.transpose(1, 3, 0, 2, 4).reshape(ranks, N_OUT, size, 4, cols)
    second = second.transpose(2, 0, 3, 1, 4).reshape(size, ranks, 4 * N_OUT, cols)
    return jnp.concatenate([first, second], axis=2)


def adam_step(weight, moment_one, second, gradient, rate_value, decay_rate):
    moment_one = BETA_ONE * moment_one + (1.0 - BETA_ONE) * gradient
    second = BETA_TWO * second + (1.0 - BETA_TWO) * gradient * gradient
    update = (
        moment_one / (1.0 - BETA_ONE**STEP) / (jnp.sqrt(second / (1.0 - BETA_TWO**STEP)) + EPS_ADAM)
    )
    return (weight - rate_value * (update + decay_rate * weight), moment_one, second)


def shards(
    images,
    grad_out,
    w_qkv,
    w_proj,
    w_fc1,
    w_fc2,
    first_qkv,
    first_proj,
    first_fc1,
    first_fc2,
    second_qkv,
    second_proj,
    second_fc1,
    second_fc2,
    small_params,
    small_first,
    small_second,
    rel_index,
):
    assert images.shape == (IMAGES, SIDE, SIDE, D)
    size = lax.axis_size("img")
    small = is_small()
    row, col = lax.axis_index("row"), lax.axis_index("col")
    last = [row == lax.axis_size("row") - 1, col == lax.axis_size("col") - 1]
    place = [lax.axis_index("img"), row // 2, row % 2, col]
    at = jnp.stack([jnp.asarray(value, jnp.int32) for value in place + last])
    images = images.transpose(1, 2, 0, 3)
    grad_out = grad_out.transpose(1, 2, 0, 3)

    onehot = (
        jnp.arange(RELPOS, dtype=jnp.int32)[:, None] == padded_index(rel_index)
    ).astype(F32)
    tables = small_params[:, 9 * D + MLP :].reshape(2, RELPOS, HEADS)
    base = jnp.einsum("lrh,rp->lhp", tables * LOG2E, onehot, precision=lax.Precision.HIGHEST)
    base = base.reshape(2, HEADS, WROWS, AROWS)
    grad_strips = (
        grad_out[:SHIFT, SHIFT:].astype(BF16),
        grad_out[SHIFT:, :SHIFT].astype(BF16),
        grad_out[:SHIFT, :SHIFT].astype(BF16),
    )

    masters = (w_qkv, w_proj, w_fc1, w_fc2)
    pack_a_zero, pack_a_one, pack_b_zero, pack_b_one = make_packs(masters)
    if small:
        line_a = gather_line(pack_a_zero)
        pair_b = jnp.stack([pack_b_zero, near_swap(pack_b_zero)])
        got, far_b, near_a, at, base, grad_strips = together(
            quad_swaps([line_a] * 4),
            far_swap(pair_b),
            near_swap(pack_a_one),
            at,
            base,
            grad_strips,
        )
        pair_a = jnp.stack([pack_a_one, near_a])
        quad = jnp.stack([line_a, *got])
        packs_a_zero = quad, swapped(quad, core=1)
        packs_b_one = gather_whole(after(pack_b_one, got), mlp_canonical)
        line_b = jnp.concatenate([pair_b, far_b])
    else:
        packs_a_zero = gather_whole(pack_a_zero, attention_canonical)
        packs_b_zero = gather_whole(pack_b_zero, mlp_canonical)
        packs_a_one = gather_whole(pack_a_one, attention_canonical)
        packs_b_one = gather_whole(pack_b_one, mlp_canonical)

    def table_row(sums, dtab):
        table = jnp.einsum(
            "hp,rp->rh", dtab.reshape(HEADS, -1), onehot, precision=lax.Precision.HIGHEST
        )
        return jnp.concatenate([sums, table.reshape(1, -1)], axis=1)

    saved_zero, mid_zero = attention_forward(0, at, images, (), packs_a_zero, small_params, base[0])
    if small:
        mid_zero, got, far_a = together(mid_zero, quad_swaps([line_b] * 4), far_swap(pair_a))
        quad = jnp.stack([line_b, *got])
        packs_b_zero = quad, swapped(quad, core=1)
        line_a = jnp.concatenate([pair_a, far_a])
    grad_strips = send_strips(after(grad_strips, mid_zero), -1)
    out_zero, strips, hidden_zero = mlp_forward(0, at, mid_zero, packs_b_zero, small_params)
    strips, grad_strips = together(strips, grad_strips)
    if small:
        strips, got = together(strips, quad_swaps([line_a] * 4))
        quad = jnp.stack([line_a, *got])
        strips, other = together(send_strips(strips, -1), swapped(quad, core=1))
        packs_a_one = quad, other
    else:
        strips = send_strips(strips, -1)
    saved_one, mid_one = attention_forward(
        1, at, out_zero, strips, packs_a_one, small_params, base[1]
    )
    (out_one, *out_strips), gm_one, dpacks, rest = mlp_backward(
        1, at, mid_one, grad_out, grad_strips, (), packs_b_one, small_params, True
    )

    plane_b_one = scatter_plane(dpacks[0])
    dx_one, strips, dpacks, dtab_one, sums = attention_backward(
        1, at, gm_one, saved_one, packs_a_one, small_params, rest, True
    )
    plane_a_one = scatter_plane(dpacks[0])
    strips, row_one = together(send_strips(strips, 1), table_row(sums, dtab_one))
    out_strips = send_strips(after(out_strips, strips), 1)
    _, gm_zero, dpacks, rest = mlp_backward(
        0, at, mid_zero, dx_one, strips, hidden_zero, packs_b_zero, small_params, not small
    )

    dpacks, out_strips, plane_b_one = together(dpacks, out_strips, plane_b_one)
    got, out_one = together(pair_swap(dpacks), fill_prev(out_one, out_strips))
    outputs = out_one.transpose(2, 0, 1, 3)
    halves_b_zero = scatter_pair(dpacks, got)
    gm_zero, halves_b_zero = together(gm_zero, halves_b_zero)
    sum_b_one = scatter_col(plane_b_one, mlp_shards)
    grad_input, _, dpacks, dtab_zero, sums = attention_backward(
        0, at, gm_zero, saved_zero, packs_a_zero, small_params, rest, not small
    )
    grad_input = grad_input.transpose(2, 0, 1, 3)

    dpacks, got_b, sum_b_one, plane_a_one = together(
        dpacks, quad_swaps(halves_b_zero), sum_b_one, plane_a_one
    )
    sum_a_one = scatter_col(plane_a_one, attention_shards)
    got, row_zero = together(pair_swap(dpacks), table_row(sums, dtab_zero))
    halves_a = scatter_pair(dpacks, got)
    small_grad = jnp.concatenate([row_zero, row_one], axis=0)

    def small_swaps(*steps):
        return [swapped(small_grad, **step) for step in steps] if small else []

    halves_b_zero, got_b = after((halves_b_zero, got_b), halves_a)
    line_b = scatter_quad(halves_b_zero, got_b)
    got, parts = together(quad_swaps(halves_a), small_swaps({"core": 1}))
    line_a = scatter_quad(halves_a, got)
    small_grad = sum(parts, small_grad)
    steps = [{"img": i, "down": y} for i, y in QUADS[1:]]
    sums_b = line_swaps(line_b)
    sums_a, parts = together(line_swaps(line_a), small_swaps(*steps))
    if small:
        small_grad = (small_grad + parts[0]) + (parts[1] + parts[2])
        parts = small_swaps(*({"across": m} for m in (1, 2, 3)))
        small_grad = (small_grad + parts[0]) + (parts[1] + parts[2])
    else:
        small_grad = lax.psum(small_grad, AXES)

    states = [turned(group) for group in (
        masters,
        (first_qkv, first_proj, first_fc1, first_fc2),
        (second_qkv, second_proj, second_fc1, second_fc2),
    )]
    if small:
        new_a = update(
            attention_kinds, (line_a[0], *sums_a, sum_a_one), [s[k] for k in (0, 1) for s in states]
        )
        new_b = update(
            mlp_kinds, (line_b[0], *sums_b, sum_b_one), [s[k] for k in (2, 3) for s in states]
        )
    else:
        cols = D // size
        total_a = [scatter_whole(line_a[0], attention_shards), sum_a_one]
        total_b = [scatter_whole(line_b[0], mlp_shards), sum_b_one]
        kinds = (
            [t[:N_QKV] for t in total_a],
            [t[N_QKV:] for t in total_a],
            [t[:N_FC1].T for t in total_b],
            [t[N_FC1:].reshape(4, N_OUT, cols).transpose(1, 0, 2).reshape(N_OUT, -1) for t in total_b],
        )
        new = []
        for k in range(4):
            grad = jnp.stack(kinds[k]).astype(F32)
            new += adam_step(*(s[k] for s in states), grad, RATE_MATRIX, DECAY_MATRIX)
        new_a, new_b = new[:6], new[6:]
    small_new = adam_step(small_params, small_first, small_second, small_grad, RATE_SMALL, 0.0)
    new = list(new_a) + list(new_b)
    new = [turned(new[m::3]) for m in range(3)]
    return (outputs, grad_input) + new[0] + new[1] + new[2] + tuple(small_new)


def solution(mesh):
    grid_spec = P("img", "row", "col", None)
    matrix = P(None, "img", ("row", "col"))
    in_specs = (grid_spec,) * 2 + (matrix,) * 12 + (P(),) * 4
    out_specs = (grid_spec,) * 2 + (matrix,) * 12 + (P(),) * 3
    return jax.shard_map(shards, mesh=mesh, in_specs=in_specs, out_specs=out_specs, check_vma=False)
```
